32 devices in a mesh: dp: 16 (over z, y, x), seq: 2 (over core).
Axes of the slice: x: 2, y: 2, z: 4, core: 2. Of those that a mesh axis runs over, the one named last changes fastest.
Arguments:
- latents: float32 [16, 512, 1024], P('dp', 'seq'), may hold values from -6 to 6
- pixels: float32 [16, 8192, 261], P('dp', 'seq'), may hold values from -6 to 6
- keep_mask: int32 [16, 8192], P('dp', 'seq'), may hold values from 0 to 1, as said below
- cotangent: float32 [16, 512, 1024], P('dp', 'seq'), may hold values from -6 to 6
- square_weights: float32 [4, 1024, 1024], P(None, None, 'dp')
- square_first: float32 [4, 1024, 1024], P(None, None, 'dp')
- square_second: float32 [4, 1024, 1024], P(None, None, 'dp')
- pixel_weights: float32 [2, 261, 1024], P(None, None, 'dp')
- pixel_first: float32 [2, 261, 1024], P(None, None, 'dp')
- pixel_second: float32 [2, 261, 1024], P(None, None, 'dp')
- latent_vectors: float32 [6, 1024], replicated
- latent_first: float32 [6, 1024], replicated
- latent_second: float32 [6, 1024], replicated
- pixel_norm: float32 [2, 261], replicated
- pixel_norm_first: float32 [2, 261], replicated
- pixel_norm_second: float32 [2, 261], replicated
Outputs:
- latents_out: float32 [16, 512, 1024], P('dp', 'seq')
- latents_grad: float32 [16, 512, 1024], P('dp', 'seq')
- pixels_grad: float32 [16, 8192, 261], P('dp', 'seq')
- square_grad: float32 [4, 1024, 1024], P(None, None, 'dp')
- square_first_new: float32 [4, 1024, 1024], P(None, None, 'dp')
- square_second_new: float32 [4, 1024, 1024], P(None, None, 'dp')
- square_new: float32 [4, 1024, 1024], P(None, None, 'dp')
- square_half: bfloat16 [4, 1024, 1024], P(None, None, 'dp')
- pixel_weight_grad: float32 [2, 261, 1024], P(None, None, 'dp')
- pixel_first_new: float32 [2, 261, 1024], P(None, None, 'dp')
- pixel_second_new: float32 [2, 261, 1024], P(None, None, 'dp')
- pixel_new: float32 [2, 261, 1024], P(None, None, 'dp')
- pixel_half: bfloat16 [2, 261, 1024], P(None, None, 'dp')
- latent_first_new: float32 [6, 1024], replicated
- latent_second_new: float32 [6, 1024], replicated
- latent_vectors_new: float32 [6, 1024], replicated
- pixel_norm_first_new: float32 [2, 261], replicated
- pixel_norm_second_new: float32 [2, 261], replicated
- pixel_norm_new: float32 [2, 261], replicated
- matrix_norms: float32 [3, 6], replicated
The draws below stay inside these ranges and needn't reach their ends.
Inputs may be any that keep to these rules, and one draw needn't show every extreme that they name: keep_mask[i, 0] = 1 for every image i; each image drops its other pixels with a share drawn for it between 10 and 60 percent.
All inputs are finite; a program needn't handle non-finite values.
Results may differ from the reference program's by a relative error of at most 0.015.
The reference program's roundings to bfloat16 on the way count: a program that leaves them out, or rounds other values in their place, can miss the bound.
Values may be sent and summed in bfloat16 or wider, within the bound.
No kernel may reach another device: no remote copies, remote signals or barrier semaphores. Data moves between devices by JAX's collectives and lax.ppermute only.
A program may use at most 320 MiB of HBM per device.

```python
import jax
import jax.numpy as jnp
from jax import lax

D = 1024
C = 261
LAT = 512
IMG_DEV = 1
STEP = 10
IMAGES = 16
PIXELS = 8192


query_factor = 0.39


key_factor = 0.77


value_factor = 2.0


def column_rise(width):
    return 1.0 + 2.0 * jnp.arange(width, dtype=jnp.float32) / max(width - 1, 1)


def block_level(key, count, width):
    shards = IMAGES // IMG_DEV
    levels = jnp.exp(jax.random.uniform(key, (count, shards), dtype=jnp.float32, minval=-0.5, maxval=0.5))
    return jnp.repeat(levels, width // shards, axis=1)[:, None, :]


def latent_root():
    return (IMAGES * LAT) ** 0.5


def pixel_root():
    return (IMAGES * PIXELS) ** 0.5


def attention_reach():
    return min(1.0, (32.0 / PIXELS) ** 0.5)


def output_spread():
    return (PIXELS / (8.0 * D)) ** 0.5


def query_grad_size():
    return value_factor * key_factor


def key_grad_size():
    return LAT ** 0.5 * attention_reach() * 16.0 * value_factor * query_factor / (0.65 * PIXELS) ** 0.5


def value_grad_size():
    return LAT ** 0.5 * attention_reach() * 3.3 / (0.65 * PIXELS) ** 0.5


def first_moment(key, extent, scales):
    return scales * jax.random.normal(key, extent, dtype=jnp.float32) / 9.0


def second_moment(key, extent, scales, levels):
    factor = jnp.exp(jax.random.uniform(key, extent, dtype=jnp.float32, minval=-0.6931, maxval=0.6931))
    return 0.001 * levels * scales * scales * factor


def square_grad_scale():
    sizes = [query_grad_size(), 3.3 * value_factor * attention_reach(), 1.3, 1.3]
    return latent_root() * jnp.array(sizes, dtype=jnp.float32)[:, None, None]


def pixel_grad_scale():
    sizes = [key_grad_size(), value_grad_size()]
    return pixel_root() * jnp.array(sizes, dtype=jnp.float32)[:, None, None]


def latent_grad_scale():
    first_norm = query_grad_size() * query_factor * 2.3
    sizes = [first_norm, first_norm, 3.0, 3.0, 1.3, 1.0]
    return latent_root() * jnp.array(sizes, dtype=jnp.float32)[:, None]


def norm_grad_scale():
    size = (D / C) ** 0.5 * 2.3 * (key_grad_size() * key_factor + value_grad_size() * value_factor)
    return pixel_root() * size * jnp.ones((2, 1), dtype=jnp.float32)


def draw_keep_mask(key, part):
    key = jax.random.fold_in(key, 11)
    drop_key, cell_key = jax.random.split(key)
    drop = jax.random.randint(drop_key, (IMAGES, 1), 100, 601)
    cells = jax.random.randint(cell_key, (IMAGES, PIXELS), 0, 1000)
    kept = (cells >= drop).astype(jnp.int32)
    first = (jnp.arange(PIXELS) == 0)[None, :]
    return jnp.where(first, 1, kept).astype(jnp.int32)


def draw_square_weights(key, part):
    key = jax.random.fold_in(key, 1)
    noise_key, level_key = jax.random.split(key)
    extent = (4, D, D)
    noise = jax.random.normal(noise_key, extent, dtype=jnp.float32)
    spread = jnp.array([query_factor, output_spread(), 1.0, 1.0], dtype=jnp.float32) * D ** (-0.5)
    return noise * spread[:, None, None] * column_rise(D)[None, None, :] * block_level(level_key, 4, D)


def draw_square_first(key, part):
    key = jax.random.fold_in(key, 2)
    noise_key, level_key = jax.random.split(key)
    return first_moment(noise_key, (4, D, D), square_grad_scale() * block_level(level_key, 4, D))


def draw_square_second(key, part):
    key = jax.random.fold_in(key, 3)
    levels = jnp.array([1.0, 4.0, 1.0, 1.0], dtype=jnp.float32)[:, None, None]
    return second_moment(key, (4, D, D), square_grad_scale(), levels)


def draw_pixel_weights(key, part):
    key = jax.random.fold_in(key, 4)
    noise_key, level_key = jax.random.split(key)
    extent = (2, C, D)
    noise = jax.random.normal(noise_key, extent, dtype=jnp.float32)
    spread = jnp.array([key_factor, value_factor], dtype=jnp.float32) * C ** (-0.5)
    return noise * spread[:, None, None] * column_rise(D)[None, None, :] * block_level(level_key, 2, D)


def draw_pixel_first(key, part):
    key = jax.random.fold_in(key, 5)
    noise_key, level_key = jax.random.split(key)
    return first_moment(noise_key, (2, C, D), pixel_grad_scale() * block_level(level_key, 2, D))


def draw_pixel_second(key, part):
    key = jax.random.fold_in(key, 6)
    levels = jnp.array([1.0, 4.0], dtype=jnp.float32)[:, None, None]
    return second_moment(key, (2, C, D), pixel_grad_scale(), levels)


def draw_latent_vectors(key, part):
    key = jax.random.fold_in(key, 7)
    gain_key, shift_key = jax.random.split(key)
    gains = 1.0 + 0.3 * jax.random.uniform(gain_key, (6, D), dtype=jnp.float32, minval=-1.0, maxval=1.0)
    shifts = 0.3 * jax.random.normal(shift_key, (6, D), dtype=jnp.float32)
    order = jnp.arange(6)[:, None]
    gain_rows = jnp.logical_and(order % 2 == 0, order < 4)
    return jnp.where(gain_rows, gains, shifts)


def draw_latent_first(key, part):
    key = jax.random.fold_in(key, 8)
    return first_moment(key, (6, D), latent_grad_scale())


def draw_latent_second(key, part):
    key = jax.random.fold_in(key, 9)
    levels = jnp.array([1.0, 1.0, 1.0, 1.0, 2.0, 4.0], dtype=jnp.float32)[:, None]
    return second_moment(key, (6, D), latent_grad_scale(), levels)


def draw_pixel_norm(key, part):
    key = jax.random.fold_in(key, 10)
    gain_key, shift_key = jax.random.split(key)
    gains = 1.0 + 0.3 * jax.random.uniform(gain_key, (1, C), dtype=jnp.float32, minval=-1.0, maxval=1.0)
    shifts = 0.3 * jax.random.normal(shift_key, (1, C), dtype=jnp.float32)
    return jnp.concatenate([gains, shifts], axis=0)


def draw_pixel_norm_first(key, part):
    key = jax.random.fold_in(key, 12)
    return first_moment(key, (2, C), norm_grad_scale())


def draw_pixel_norm_second(key, part):
    key = jax.random.fold_in(key, 13)
    levels = jnp.ones((2, 1), dtype=jnp.float32)
    return second_moment(key, (2, C), norm_grad_scale(), levels)


def block_scale(stream_key, dims, cuts, low, top_value):
    def one(axis_at, shards_of):
        steps = jax.random.uniform(jax.random.fold_in(jax.random.fold_in(stream_key, 6), axis_at), (shards_of,), jnp.float32, low / len(cuts), top_value / len(cuts))
        return jnp.repeat(jnp.exp(steps), dims[axis_at] // shards_of).reshape((-1,) + (1,) * (len(dims) - axis_at - 1))

    factor_of = one(*cuts[0])
    for cut in cuts[1:]:
        factor_of = factor_of * one(*cut)
    return factor_of


def scatter_about(key, shape, deviation, limit, pieces=(), held_as=jnp.bfloat16):
    values = jax.random.normal(key, shape, jnp.float32) * deviation
    if len(pieces) > 0:
        values = block_scale(key, shape, pieces, -0.22, 0.18) * values
    return jnp.clip(values, min=-limit, max=limit).astype(held_as)


def setup_inputs(seed: int = 0) -> dict:
    arg_keys = jax.random.split(jax.random.key(seed), 17)
    latents = scatter_about(arg_keys[0], (IMAGES, LAT, D), 1.0, 6.0, ((0, 16), (1, 2)), jnp.float32)
    pixels = scatter_about(arg_keys[1], (IMAGES, PIXELS, C), 1.0, 6.0, ((0, 16), (1, 2)), jnp.float32)
    keep_mask = draw_keep_mask(jax.random.fold_in(arg_keys[16], 71), 0)
    cotangent = scatter_about(arg_keys[3], (IMAGES, LAT, D), 1.0, 6.0, ((0, 16), (1, 2)), jnp.float32)
    square_weights = draw_square_weights(jax.random.fold_in(arg_keys[16], 71), 0)
    square_first = draw_square_first(jax.random.fold_in(arg_keys[16], 71), 0)
    square_second = draw_square_second(jax.random.fold_in(arg_keys[16], 71), 0)
    pixel_weights = draw_pixel_weights(jax.random.fold_in(arg_keys[16], 71), 0)
    pixel_first = draw_pixel_first(jax.random.fold_in(arg_keys[16], 71), 0)
    pixel_second = draw_pixel_second(jax.random.fold_in(arg_keys[16], 71), 0)
    latent_vectors = draw_latent_vectors(jax.random.fold_in(arg_keys[16], 71), 0)
    latent_first = draw_latent_first(jax.random.fold_in(arg_keys[16], 71), 0)
    latent_second = draw_latent_second(jax.random.fold_in(arg_keys[16], 71), 0)
    pixel_norm = draw_pixel_norm(jax.random.fold_in(arg_keys[16], 71), 0)
    pixel_norm_first = draw_pixel_norm_first(jax.random.fold_in(arg_keys[16], 71), 0)
    pixel_norm_second = draw_pixel_norm_second(jax.random.fold_in(arg_keys[16], 71), 0)
    return dict(latents=latents, pixels=pixels, keep_mask=keep_mask, cotangent=cotangent, square_weights=square_weights, square_first=square_first, square_second=square_second, pixel_weights=pixel_weights, pixel_first=pixel_first, pixel_second=pixel_second, latent_vectors=latent_vectors, latent_first=latent_first, latent_second=latent_second, pixel_norm=pixel_norm, pixel_norm_first=pixel_norm_first, pixel_norm_second=pixel_norm_second)


@jax.custom_vjp
def low(v):
    return lax.optimization_barrier(v.astype(jnp.bfloat16)).astype(jnp.float32)

@jax.custom_vjp
def low_back(v):
    return v

def low_keep(v):
    return (low(v), None)

def low_pass(kept, grad):
    return (grad,)

def back_keep(v):
    return (v, None)

def back_low(kept, grad):
    return (low(grad),)
low.defvjp(low_keep, low_pass)
low_back.defvjp(back_keep, back_low)
norm_epsilon = 1e-05
beta_one = 0.9
beta_two = 0.999
decay_rate = 0.01
epsilon = 1e-06
learn_rate = 0.25
vector_rate = 1.0
masked_score = -1e+30
gelu_coeff = 0.7978845608028654

def product(left, right):
    return jnp.dot(left, right, precision=lax.Precision.HIGHEST, preferred_element_type=jnp.float32)

def layer_norm(values, gain, shift):
    center = values - lax.optimization_barrier(jnp.mean(values, axis=-1, keepdims=True))
    spread = lax.optimization_barrier(jnp.mean(center * center, axis=-1, keepdims=True))
    return center * lax.rsqrt(spread + norm_epsilon) * gain + shift

def gelu(hidden):
    return 0.5 * hidden * (1.0 + jnp.tanh(gelu_coeff * (hidden + 0.044715 * hidden * hidden * hidden)))

def adam_moments(grad, first, second):
    first_new = beta_one * first + (1.0 - beta_one) * grad
    second_new = beta_two * second + (1.0 - beta_two) * grad * grad
    ratio = first_new / (1.0 - beta_one ** STEP) / (jnp.sqrt(second_new / (1.0 - beta_two ** STEP)) + epsilon)
    return (first_new, second_new, ratio)

def reference(latents, pixels, keep_mask, cotangent, square_weights, square_first, square_second, pixel_weights, pixel_first, pixel_second, latent_vectors, latent_first, latent_second, pixel_norm, pixel_norm_first, pixel_norm_second):
    scale = D ** (-0.5)

    def forward(square, matrices, vectors, norm_params, latent_all, pixel_all):
        query_weight = low(square[0])
        attend_weight = low(square[1])
        up_weight = low(square[2])
        down_weight = low(square[3])
        key_weight = low(matrices[0])
        value_weight = low(matrices[1])

        def image_block(inputs):
            latent, pixel, mask = inputs
            normed = low(layer_norm(latent, vectors[0], vectors[1]))
            query = low(low_back(product(normed, query_weight)))
            pixel_normed = low(layer_norm(pixel, norm_params[0], norm_params[1]))
            keys = low(product(pixel_normed, key_weight))
            values = low(product(pixel_normed, value_weight))
            scores = low_back(product(query, keys.T))
            scores = jnp.where(mask[None, :] > 0, scores * scale, masked_score)
            top = lax.optimization_barrier(jnp.max(scores, axis=-1, keepdims=True))
            expo = jnp.exp(scores - top)
            attn = low(expo / lax.optimization_barrier(jnp.sum(expo, axis=-1, keepdims=True)))
            attended = low(low_back(product(attn, values)))
            middle = latent + low_back(product(attended, attend_weight))
            mixed = low(layer_norm(middle, vectors[2], vectors[3]))
            hidden = low_back(product(mixed, up_weight) + vectors[4])
            active = low(gelu(hidden))
            return middle + low_back(product(active, down_weight) + vectors[5])
        return lax.map(jax.checkpoint(image_block), (latent_all, pixel_all, keep_mask))
    latents_out, pull = jax.vjp(forward, square_weights, pixel_weights, latent_vectors, pixel_norm, latents, pixels)
    square_grad, pixel_weight_grad, latent_vector_grad, pixel_norm_grad, latents_grad, pixels_grad = pull(cotangent)
    square_first_new, square_second_new, square_ratio = adam_moments(square_grad, square_first, square_second)
    pixel_first_new, pixel_second_new, pixel_ratio = adam_moments(pixel_weight_grad, pixel_first, pixel_second)
    square_update = square_ratio + decay_rate * square_weights
    pixel_update = pixel_ratio + decay_rate * pixel_weights
    weight_norm = jnp.sqrt(jnp.concatenate([lax.optimization_barrier(jnp.sum(square_weights * square_weights, axis=(1, 2))), lax.optimization_barrier(jnp.sum(pixel_weights * pixel_weights, axis=(1, 2)))]))
    update_norm = jnp.sqrt(jnp.concatenate([lax.optimization_barrier(jnp.sum(square_update * square_update, axis=(1, 2))), lax.optimization_barrier(jnp.sum(pixel_update * pixel_update, axis=(1, 2)))]))
    trust = weight_norm / (update_norm + epsilon)
    square_new = square_weights - learn_rate * trust[:4, None, None] * square_update
    pixel_new = pixel_weights - learn_rate * trust[4:, None, None] * pixel_update
    latent_first_new, latent_second_new, latent_ratio = adam_moments(latent_vector_grad, latent_first, latent_second)
    latent_vectors_new = latent_vectors - vector_rate * latent_ratio
    pixel_norm_first_new, pixel_norm_second_new, norm_ratio = adam_moments(pixel_norm_grad, pixel_norm_first, pixel_norm_second)
    pixel_norm_new = pixel_norm - vector_rate * norm_ratio
    matrix_norms = jnp.stack([weight_norm, update_norm, trust])
    return (latents_out, latents_grad, pixels_grad, square_grad, square_first_new, square_second_new, square_new, square_new.astype(jnp.bfloat16), pixel_weight_grad, pixel_first_new, pixel_second_new, pixel_new, pixel_new.astype(jnp.bfloat16), latent_first_new, latent_second_new, latent_vectors_new, pixel_norm_first_new, pixel_norm_second_new, pixel_norm_new, matrix_norms)
```

```python
import jax
import jax.numpy as jnp
from jax import lax
from jax.sharding import PartitionSpec as P

STEP = 10


norm_epsilon = 1e-05
beta_one = 0.9
beta_two = 0.999
decay_rate = 0.01
epsilon = 1e-06
learn_rate = 0.25
vector_rate = 1.0
masked_score = -1e30
gelu_coeff = 0.7978845608028654


def layer_norm(values, gain, shift):
    center = values - jnp.mean(values, axis=-1, keepdims=True)
    spread = jnp.mean(center * center, axis=-1, keepdims=True)
    return center * lax.rsqrt(spread + norm_epsilon) * gain + shift


def gelu(hidden):
    return (
        0.5 * hidden * (1.0 + jnp.tanh(gelu_coeff * (hidden + 0.044715 * hidden * hidden * hidden)))
    )


def adam_moments(grad, first, second):
    first_new = beta_one * first + (1.0 - beta_one) * grad
    second_new = beta_two * second + (1.0 - beta_two) * grad * grad
    ratio = (
        first_new
        / (1.0 - beta_one**STEP)
        / (jnp.sqrt(second_new / (1.0 - beta_two**STEP)) + epsilon)
    )
    return (first_new, second_new, ratio)


def local(
    latents,
    pixels,
    keep_mask,
    cotangent,
    square_weights,
    square_first,
    square_second,
    pixel_weights,
    pixel_first,
    pixel_second,
    latent_vectors,
    latent_first,
    latent_second,
    pixel_norm,
    pixel_norm_first,
    pixel_norm_second,
):
    half = jnp.bfloat16
    single = jnp.float32
    width = latents.shape[2]
    feats = pixels.shape[2]
    scale = width ** (-0.5)
    shard_width = square_weights.shape[2]
    rank = lax.axis_index("seq")
    cores = lax.axis_size("seq")
    groups = lax.axis_size("dp")
    part = width // cores

    def dot(left, right, dims):
        return lax.dot_general(left, right, ((dims[0], dims[1]), ((), ())), preferred_element_type=single)

    square_rows = jnp.transpose(square_weights, (0, 2, 1)).astype(half)
    pixel_rows = jnp.transpose(pixel_weights, (0, 2, 1)).astype(half)
    pixel_rows = jnp.pad(pixel_rows, ((0, 0), (0, 0), (0, width // 2 - feats)))
    packed = jnp.concatenate([square_rows.reshape(-1, width), pixel_rows.reshape(-1, width)])
    count = packed.shape[0] // cores
    mine = lax.dynamic_slice_in_dim(packed, rank * count, count, 0)
    gathered = lax.all_gather(mine, ("dp", "seq"), axis=0, tiled=True)
    gathered = gathered.reshape(groups, 5 * shard_width, width)
    square_whole = (
        gathered[:, : 4 * shard_width].reshape(groups, 4, shard_width, width).transpose(1, 0, 2, 3).reshape(4, width, width)
    )
    pixel_whole = (
        gathered[:, 4 * shard_width :].reshape(groups, 2, shard_width, width // 2).transpose(1, 0, 2, 3).reshape(2, width, width // 2)
    )[:, :, :feats]
    query_t, attend_t, up_t, down_t = [square_whole[i] for i in range(4)]
    key_t, value_t = pixel_whole[0], pixel_whole[1]

    latents_all = lax.all_gather(latents[0], "seq", axis=0, tiled=True)
    cotangent_all = lax.all_gather(cotangent[0], "seq", axis=0, tiled=True)
    rows = latents_all.shape[0]
    own = rows // cores

    pixel_normed = layer_norm(pixels[0], pixel_norm[0], pixel_norm[1]).astype(half)
    kept = keep_mask[0][None, :] > 0
    normed = layer_norm(latents_all, latent_vectors[0], latent_vectors[1]).astype(half)
    query = dot(normed, query_t, ((1,), (1,))).astype(half)
    query_pix = dot(query, key_t, ((1,), (0,))).astype(half)
    scores = jnp.where(kept, dot(query_pix, pixel_normed, ((1,), (1,))) * scale, masked_score)
    top = jnp.max(scores, axis=-1, keepdims=True)
    expo = jnp.exp(scores - top)
    denom = jnp.sum(expo, axis=-1, keepdims=True)
    mixed_pix = dot(expo.astype(half), pixel_normed, ((1,), (0,)))
    sent = jnp.concatenate([mixed_pix, top, denom], axis=1)
    other = lax.ppermute(sent, "seq", [(0, 1), (1, 0)])
    top_all = jnp.maximum(top, other[:, feats : feats + 1])
    here = jnp.exp(top - top_all)
    there = jnp.exp(other[:, feats : feats + 1] - top_all)
    denom_all = denom * here + other[:, feats + 1 :] * there
    value_mix = ((mixed_pix * here + other[:, :feats] * there) / denom_all).astype(half)
    attended_f = dot(value_mix, value_t, ((1,), (1,)))
    attended = attended_f.astype(half)
    middle = latents_all + dot(attended, attend_t, ((1,), (1,)))
    mixed = layer_norm(middle, latent_vectors[2], latent_vectors[3]).astype(half)
    hidden = dot(mixed, up_t, ((1,), (1,))) + latent_vectors[4]
    active = gelu(hidden).astype(half)
    take = lambda a: lax.dynamic_slice_in_dim(a, rank * own, own, 0)
    latents_out = take(middle) + dot(take(active), down_t, ((1,), (1,))) + latent_vectors[5]

    out_half = cotangent_all.astype(half)
    down_bias = jnp.sum(out_half.astype(single), axis=0)
    active_grad = dot(out_half, down_t, ((1,), (0,)))
    hidden_grad = jax.vjp(gelu, hidden)[1](active_grad)[0].astype(half)
    up_bias = jnp.sum(hidden_grad.astype(single), axis=0)
    mixed_grad = dot(hidden_grad, up_t, ((1,), (0,)))
    middle_norm, gain_two, shift_two = jax.vjp(
        layer_norm, middle, latent_vectors[2], latent_vectors[3]
    )[1](mixed_grad)
    middle_grad = cotangent_all + middle_norm
    middle_half = middle_grad.astype(half)
    attended_grad = dot(middle_half, attend_t, ((1,), (0,))).astype(half)
    grad_pix = dot(attended_grad, value_t, ((1,), (0,))).astype(half)
    inner = jnp.sum(attended_f * attended_grad.astype(single), axis=-1, keepdims=True)

    attn = jnp.exp(scores - top_all) / denom_all
    weight_grad = dot(grad_pix, pixel_normed, ((1,), (1,)))
    score_grad = (attn * (weight_grad - inner) * scale).astype(half)
    score_pix = dot(score_grad, pixel_normed, ((1,), (0,)))
    score_pix = (score_pix + lax.ppermute(score_pix, "seq", [(0, 1), (1, 0)])).astype(half)
    pixel_normed_grad = dot(score_grad, query_pix, ((0,), (0,))) + dot(attn.astype(half), grad_pix, ((0,), (0,)))
    pixels_grad, pixel_gain, pixel_shift = jax.vjp(
        layer_norm, pixels[0], pixel_norm[0], pixel_norm[1]
    )[1](pixel_normed_grad)
    query_grad = dot(score_pix, key_t, ((1,), (1,))).astype(half)
    normed_grad = dot(query_grad, query_t, ((1,), (0,)))
    latent_norm, gain_one, shift_one = jax.vjp(
        layer_norm, latents_all, latent_vectors[0], latent_vectors[1]
    )[1](normed_grad)
    latents_grad = take(middle_grad + latent_norm)

    cut = lambda a: lax.dynamic_slice_in_dim(a, rank * part, part, 1)
    square_terms = jnp.stack(
        [
            dot(query_grad, cut(normed), ((0,), (0,))),
            dot(middle_half, cut(attended), ((0,), (0,))),
            dot(hidden_grad, cut(mixed), ((0,), (0,))),
            dot(out_half, cut(active), ((0,), (0,))),
        ]
    )
    first = rank == 0
    pixel_terms = dot(jnp.where(first, query, attended_grad), jnp.where(first, score_pix, value_mix), ((0,), (0,)))
    square_terms = square_terms.reshape(4, groups, shard_width, part).transpose(1, 0, 2, 3).reshape(-1, part)
    pixel_terms = jnp.pad(pixel_terms, ((0, 0), (0, part - feats)))
    pixel_terms = pixel_terms.reshape(groups, shard_width, part)
    terms = jnp.concatenate([square_terms.reshape(groups, -1, part), pixel_terms], axis=1).reshape(-1, part).astype(half)
    summed = lax.psum_scatter(terms, "dp", scatter_dimension=0, tiled=True).astype(half)
    both = lax.all_gather(summed, "seq", axis=0).astype(single)
    square_grad = both[:, : 4 * shard_width].reshape(2, 4, shard_width, part).transpose(1, 0, 3, 2).reshape(4, width, shard_width)
    pixel_weight_grad = both[:, 4 * shard_width :, :feats].transpose(0, 2, 1)

    latent_vector_grad = lax.psum(
        jnp.stack([gain_one, shift_one, gain_two, shift_two, up_bias, down_bias]), "dp"
    )
    pixel_norm_grad = lax.psum(jnp.stack([pixel_gain, pixel_shift]), ("dp", "seq"))
    square_first_new, square_second_new, square_ratio = adam_moments(
        square_grad, square_first, square_second
    )
    pixel_first_new, pixel_second_new, pixel_ratio = adam_moments(
        pixel_weight_grad, pixel_first, pixel_second
    )
    square_update = square_ratio + decay_rate * square_weights
    pixel_update = pixel_ratio + decay_rate * pixel_weights
    squares = jnp.concatenate(
        [
            jnp.sum(square_weights * square_weights, axis=(1, 2)),
            jnp.sum(pixel_weights * pixel_weights, axis=(1, 2)),
            jnp.sum(square_update * square_update, axis=(1, 2)),
            jnp.sum(pixel_update * pixel_update, axis=(1, 2)),
        ]
    )
    sums = lax.psum(squares, "dp")
    weight_norm = jnp.sqrt(sums[:6])
    update_norm = jnp.sqrt(sums[6:])
    trust = weight_norm / (update_norm + epsilon)
    square_new = square_weights - learn_rate * trust[:4, None, None] * square_update
    pixel_new = pixel_weights - learn_rate * trust[4:, None, None] * pixel_update
    latent_first_new, latent_second_new, latent_ratio = adam_moments(
        latent_vector_grad, latent_first, latent_second
    )
    latent_vectors_new = latent_vectors - vector_rate * latent_ratio
    pixel_norm_first_new, pixel_norm_second_new, norm_ratio = adam_moments(
        pixel_norm_grad, pixel_norm_first, pixel_norm_second
    )
    pixel_norm_new = pixel_norm - vector_rate * norm_ratio
    matrix_norms = jnp.stack([weight_norm, update_norm, trust])
    return (
        latents_out[None],
        latents_grad[None],
        pixels_grad[None],
        square_grad,
        square_first_new,
        square_second_new,
        square_new,
        square_new.astype(half),
        pixel_weight_grad,
        pixel_first_new,
        pixel_second_new,
        pixel_new,
        pixel_new.astype(half),
        latent_first_new,
        latent_second_new,
        latent_vectors_new,
        pixel_norm_first_new,
        pixel_norm_second_new,
        pixel_norm_new,
        matrix_norms,
    )


def solution(mesh):
    return jax.shard_map(
        local,
        mesh=mesh,
        in_specs=(
            P("dp", "seq", None),
            P("dp", "seq", None),
            P("dp", "seq"),
            P("dp", "seq", None),
            P(None, None, "dp"),
            P(None, None, "dp"),
            P(None, None, "dp"),
            P(None, None, "dp"),
            P(None, None, "dp"),
            P(None, None, "dp"),
            P(),
            P(),
            P(),
            P(),
            P(),
            P(),
        ),
        out_specs=(
            P("dp", "seq", None),
            P("dp", "seq", None),
            P("dp", "seq", None),
            P(None, None, "dp"),
            P(None, None, "dp"),
            P(None, None, "dp"),
            P(None, None, "dp"),
            P(None, None, "dp"),
            P(None, None, "dp"),
            P(None, None, "dp"),
            P(None, None, "dp"),
            P(None, None, "dp"),
            P(None, None, "dp"),
            P(),
            P(),
            P(),
            P(),
            P(),
            P(),
            P(),
        ),
        check_vma=False,
    )
```

```python
import functools

import jax
import jax.numpy as jnp
from jax import lax
from jax.experimental import pallas as pl
from jax.experimental.pallas import tpu as pltpu
from jax.sharding import PartitionSpec as P

STEP = 10


norm_epsilon = 1e-05
beta_one = 0.9
beta_two = 0.999
decay_rate = 0.01
epsilon = 1e-06
learn_rate = 0.25
vector_rate = 1.0
masked_score = -1e30
gelu_coeff = 0.7978845608028654


def layer_norm(values, gain, shift):
    center = values - jnp.mean(values, axis=-1, keepdims=True)
    spread = jnp.mean(center * center, axis=-1, keepdims=True)
    return center * lax.rsqrt(spread + norm_epsilon) * gain + shift


def gelu(hidden):
    return (
        0.5 * hidden * (1.0 + jnp.tanh(gelu_coeff * (hidden + 0.044715 * hidden * hidden * hidden)))
    )


def adam_moments(grad, first, second):
    first_new = beta_one * first + (1.0 - beta_one) * grad
    second_new = beta_two * second + (1.0 - beta_two) * grad * grad
    ratio = (
        first_new
        / (1.0 - beta_one**STEP)
        / (jnp.sqrt(second_new / (1.0 - beta_two**STEP)) + epsilon)
    )
    return (first_new, second_new, ratio)


half = jnp.bfloat16
single = jnp.float32
swap = [(0, 1), (1, 0)]


def dot(left, right, over_left, over_right):
    return lax.dot_general(left, right, (((over_left,), (over_right,)), ((), ())), preferred_element_type=single)


def flip(array, mask):
    return lax.ppermute(array, "dp", [(i, i ^ mask) for i in range(lax.axis_size("dp"))])


def trade(array):
    return lax.ppermute(array, "seq", swap)


def gather_blocks(block):
    got = [None] * 16
    got[0] = block
    got[8] = flip(got[0], 8)
    got[4] = flip(got[0], 4)
    got[1] = flip(got[0], 1)
    got[2] = flip(got[0], 2)
    got[3] = flip(got[2], 1)
    got[12] = flip(got[8], 4)
    got[5] = flip(got[4], 1)
    got[6] = flip(got[4], 2)
    got[9] = flip(got[8], 1)
    got[10] = flip(got[8], 2)
    got[7] = flip(got[5], 2)
    got[11] = flip(got[10], 1)
    got[13] = flip(got[12], 1)
    got[14] = flip(got[12], 2)
    got[15] = flip(got[13], 2)
    return got


def place_kernel(matrices, spot_ref, *refs):
    blocks, outs, sems = refs[:32], refs[32:-1], refs[-1]
    me, core = spot_ref[0], spot_ref[1]
    rows = outs[0].shape[0] // 16
    lanes = blocks[0].shape[1]
    copies = []
    for o in range(16):
        chip = lax.bitwise_xor(me, o)
        for h in range(2):
            side = lax.bitwise_xor(core, h)
            block = blocks[2 * o + h]
            for m in range(matrices):
                copies.append(
                    (
                        block.at[pl.ds(m * rows, rows)],
                        outs[m].at[
                            pl.ds(pl.multiple_of(chip * rows, rows), rows),
                            pl.ds(pl.multiple_of(side * lanes, lanes), lanes),
                        ],
                    )
                )
            copies.append(
                (
                    block.at[pl.ds(matrices * rows, rows // 2)],
                    outs[matrices].at[pl.ds(pl.multiple_of(chip * rows + side * (rows // 2), rows // 2), rows // 2)],
                )
            )
    started = []
    for i, (source, target) in enumerate(copies):
        copy = pltpu.make_async_copy(source, target, sems.at[i])
        copy.start()
        started.append(copy)
    for copy in started:
        copy.wait()


def place(spot, blocks, matrices, width):
    lanes = blocks[0].shape[1]
    shapes = [(width, width)] * matrices + [(width, lanes)]
    return pl.pallas_call(
        functools.partial(place_kernel, matrices),
        out_shape=[jax.ShapeDtypeStruct(shape, half) for shape in shapes],
        in_specs=[pl.BlockSpec(memory_space=pltpu.SMEM)] + [pl.BlockSpec(memory_space=pl.ANY)] * 32,
        out_specs=[pl.BlockSpec(memory_space=pl.ANY)] * len(shapes),
        scratch_shapes=[pltpu.SemaphoreType.DMA((32 * (matrices + 1),))],
        name="place",
    )(spot, *blocks)


def whole_matrices(squares, pixel, spot):
    matrices, shard, width = squares.shape
    part = width // 2
    core = lax.axis_index("seq")
    groups = lax.axis_size("dp")
    block = jnp.concatenate(
        [
            lax.dynamic_slice_in_dim(squares, core * part, part, 2).reshape(-1, part),
            lax.dynamic_slice_in_dim(pixel, core * (shard // 2), shard // 2, 0),
        ]
    )
    if groups == 16 and shard % 32 == 0:
        blocks = []
        for got in gather_blocks(block):
            blocks += [got, trade(got)]
        return place(spot, blocks, matrices, width)
    every = lax.all_gather(block, ("dp", "seq"), axis=0).reshape(groups, 2, -1, part)
    result = [
        every[:, :, m * shard : (m + 1) * shard].transpose(0, 2, 1, 3).reshape(width, width) for m in range(matrices)
    ]
    return result + [every[:, :, matrices * shard :].reshape(width, part)]


def fold(kept, sent, mask):
    return kept + flip(sent.astype(half), mask).astype(single)


def scatter_sum(terms):
    groups, rows, lanes = terms.shape
    me = lax.axis_index("dp")
    if groups != 16:
        return lax.psum_scatter(terms.astype(half), "dp", scatter_dimension=0, tiled=True)[0].astype(single)
    cube = terms.reshape(2, 2, 2, 2, rows, lanes)
    bits = [lax.rem(lax.div(me, 2**b), 2) for b in range(4)]

    def step(held, axis, bit):
        kept = lax.dynamic_index_in_dim(held, bits[bit], axis, keepdims=False)
        sent = lax.dynamic_index_in_dim(held, 1 - bits[bit], axis, keepdims=False)
        return fold(kept, sent, 2**bit)

    a, b = cube[..., : rows // 2, :], cube[..., rows // 2 :, :]
    a, b = step(a, 3, 0), step(b, 2, 1)
    a, b = step(a, 2, 1), step(b, 2, 0)
    held = jnp.concatenate([a, b], axis=-2)
    held = step(held, 1, 2)
    return step(held, 0, 3)


def sum_all(array, seq):
    if seq:
        array = array + trade(array)
    mask = 1
    while mask < lax.axis_size("dp"):
        array = array + flip(array, mask)
        mask *= 2
    return array


def norm_parts(values):
    center = values - jnp.mean(values, axis=-1, keepdims=True)
    spread = jnp.mean(center * center, axis=-1, keepdims=True)
    inverse = lax.rsqrt(spread + norm_epsilon)
    return center * inverse, inverse


def norm_back(grad, gain, unit, inverse):
    scaled = grad * gain
    return inverse * (
        scaled - jnp.mean(scaled, axis=-1, keepdims=True) - unit * jnp.mean(scaled * unit, axis=-1, keepdims=True)
    )


def local(
    latents,
    pixels,
    keep_mask,
    cotangent,
    square_weights,
    square_first,
    square_second,
    pixel_weights,
    pixel_first,
    pixel_second,
    latent_vectors,
    latent_first,
    latent_second,
    pixel_norm,
    pixel_norm_first,
    pixel_norm_second,
):
    width = latents.shape[2]
    feats = pixels.shape[2]
    scale = width ** (-0.5)
    shard_width = square_weights.shape[2]
    rank = lax.axis_index("seq")
    groups = lax.axis_size("dp")
    part = width // 2
    spot = jnp.stack([lax.axis_index("dp"), rank]).astype(jnp.int32)

    square_rows = jnp.transpose(square_weights, (0, 2, 1))
    pixel_rows = jnp.transpose(pixel_weights, (0, 2, 1))
    square_half = square_rows.astype(half)
    pixel_half = jnp.pad(pixel_rows.astype(half), ((0, 0), (0, 0), (0, part - feats)))
    query_t, key_t = whole_matrices(square_half[:1], pixel_half[0], spot)
    attend_t, up_t, down_t, value_t = whole_matrices(square_half[1:], pixel_half[1], spot)
    key_t, value_t = key_t[:, :feats], value_t[:, :feats]

    own = latents.shape[1]

    def with_other(array):
        return jnp.concatenate([array, trade(array)])

    def swapped(array):
        return jnp.concatenate([array[own:], array[:own]])

    latents_all = with_other(latents[0])
    cotangent_all = with_other(cotangent[0])

    pixel_unit, pixel_inverse = norm_parts(pixels[0])
    pixel_normed = (pixel_unit * pixel_norm[0] + pixel_norm[1]).astype(half)
    kept = keep_mask[0][None, :] > 0
    unit_one, inverse_one = norm_parts(latents_all)
    normed = (unit_one * latent_vectors[0] + latent_vectors[1]).astype(half)
    query = dot(normed, query_t, 1, 1).astype(half)
    query_pix = dot(query, key_t, 1, 0).astype(half)
    scores = jnp.where(kept, dot(query_pix, pixel_normed, 1, 1) * scale, masked_score)
    top = jnp.max(scores, axis=-1, keepdims=True)
    expo = jnp.exp(scores - top)
    denom = jnp.sum(expo, axis=-1, keepdims=True)
    mixed_pix = dot(expo.astype(half), pixel_normed, 1, 0)
    other = swapped(trade(jnp.concatenate([mixed_pix, top, denom], axis=1)))
    top_all = jnp.maximum(top, other[:, feats : feats + 1])
    here = jnp.exp(top - top_all)
    there = jnp.exp(other[:, feats : feats + 1] - top_all)
    denom_all = denom * here + other[:, feats + 1 :] * there
    value_mix = ((mixed_pix * here + other[:, :feats] * there) / denom_all).astype(half)
    attended_f = dot(value_mix, value_t, 1, 1)
    attended = attended_f.astype(half)
    middle = latents_all + dot(attended, attend_t, 1, 1)
    unit_two, inverse_two = norm_parts(middle)
    mixed = (unit_two * latent_vectors[2] + latent_vectors[3]).astype(half)
    hidden = dot(mixed, up_t, 1, 1) + latent_vectors[4]
    active = gelu(hidden).astype(half)
    latents_out = middle[:own] + dot(active[:own], down_t, 1, 1) + latent_vectors[5]

    out_half = cotangent_all.astype(half)
    active_grad = dot(out_half, down_t, 1, 0)
    hidden_grad = jax.vjp(gelu, hidden)[1](active_grad)[0].astype(half)
    mixed_grad = dot(hidden_grad, up_t, 1, 0)
    middle_grad = cotangent_all + norm_back(mixed_grad, latent_vectors[2], unit_two, inverse_two)
    middle_half = middle_grad.astype(half)
    attended_grad = dot(middle_half, attend_t, 1, 0).astype(half)
    grad_pix = dot(attended_grad, value_t, 1, 0).astype(half)
    inner = jnp.sum(attended_f * attended_grad.astype(single), axis=-1, keepdims=True)

    attn = jnp.exp(scores - top_all) / denom_all
    weight_grad = dot(grad_pix, pixel_normed, 1, 1)
    score_grad = (attn * (weight_grad - inner) * scale).astype(half)
    score_pix = dot(score_grad, pixel_normed, 1, 0)
    score_pix = (score_pix + swapped(trade(score_pix))).astype(half)
    pixel_normed_grad = dot(score_grad, query_pix, 0, 0) + dot(attn.astype(half), grad_pix, 0, 0)
    pixels_grad = norm_back(pixel_normed_grad, pixel_norm[0], pixel_unit, pixel_inverse)
    query_grad = dot(score_pix, key_t, 1, 1).astype(half)
    normed_grad = dot(query_grad[:own], query_t, 1, 0)
    latents_grad = middle_grad[:own] + norm_back(normed_grad, latent_vectors[0], unit_one[:own], inverse_one[:own])

    def cut(array):
        return lax.dynamic_slice_in_dim(array, rank * part, part, 1)

    def square_term(grad, value):
        return dot(grad, cut(value), 0, 0).reshape(groups, shard_width, part)

    early = scatter_sum(
        jnp.concatenate(
            [square_term(middle_half, attended), square_term(hidden_grad, mixed), square_term(out_half, active)], axis=1
        )
    )
    first = rank == 0
    pixel_term = dot(jnp.where(first, query, attended_grad), jnp.where(first, score_pix, value_mix), 0, 0)
    pixel_term = jnp.pad(pixel_term, ((0, 0), (0, part - feats))).reshape(groups, shard_width, part)
    late = scatter_sum(jnp.concatenate([square_term(query_grad, normed), pixel_term], axis=1))

    def joined(array):
        other = trade(array)
        low = jnp.where(first, array, other)
        high = jnp.where(first, other, array)
        return low, high

    early_low, early_high = joined(early)
    late_low, late_high = joined(late)
    early_whole = jnp.concatenate([early_low, early_high], axis=1).reshape(3, shard_width, width)
    late_square = jnp.concatenate([late_low[:shard_width], late_high[:shard_width]], axis=1)[None]
    square_grad = jnp.transpose(jnp.concatenate([late_square, early_whole]), (0, 2, 1))
    pixel_weight_grad = jnp.transpose(
        jnp.stack([late_low[shard_width:, :feats], late_high[shard_width:, :feats]]), (0, 2, 1)
    )

    vector_terms = jnp.stack(
        [
            jnp.sum(normed_grad * unit_one[:own], axis=0),
            jnp.sum(normed_grad, axis=0),
            jnp.sum(mixed_grad[:own] * unit_two[:own], axis=0),
            jnp.sum(mixed_grad[:own], axis=0),
            jnp.sum(hidden_grad[:own].astype(single), axis=0),
            jnp.sum(out_half[:own].astype(single), axis=0),
        ]
    )
    norm_terms = jnp.stack([jnp.sum(pixel_normed_grad * pixel_unit, axis=0), jnp.sum(pixel_normed_grad, axis=0)])
    norm_terms = jnp.pad(norm_terms, ((0, 0), (0, width - feats)))
    vector_sums = sum_all(jnp.concatenate([vector_terms, norm_terms]), True)
    latent_vector_grad, pixel_norm_grad = vector_sums[:6], vector_sums[6:, :feats]
    square_first_new, square_second_new, square_ratio = adam_moments(
        square_grad, square_first, square_second
    )
    pixel_first_new, pixel_second_new, pixel_ratio = adam_moments(
        pixel_weight_grad, pixel_first, pixel_second
    )
    square_update = square_ratio + decay_rate * square_weights
    pixel_update = pixel_ratio + decay_rate * pixel_weights
    weight_squares = jnp.concatenate(
        [jnp.sum(square_weights * square_weights, axis=(1, 2)), jnp.sum(pixel_weights * pixel_weights, axis=(1, 2))]
    )
    update_squares = jnp.concatenate(
        [jnp.sum(square_update * square_update, axis=(1, 2)), jnp.sum(pixel_update * pixel_update, axis=(1, 2))]
    )
    weight_norm = jnp.sqrt(sum_all(weight_squares, False))
    update_norm = jnp.sqrt(sum_all(update_squares, False))
    trust = weight_norm / (update_norm + epsilon)
    square_new = square_weights - learn_rate * trust[:4, None, None] * square_update
    pixel_new = pixel_weights - learn_rate * trust[4:, None, None] * pixel_update
    latent_first_new, latent_second_new, latent_ratio = adam_moments(
        latent_vector_grad, latent_first, latent_second
    )
    latent_vectors_new = latent_vectors - vector_rate * latent_ratio
    pixel_norm_first_new, pixel_norm_second_new, norm_ratio = adam_moments(
        pixel_norm_grad, pixel_norm_first, pixel_norm_second
    )
    pixel_norm_new = pixel_norm - vector_rate * norm_ratio
    matrix_norms = jnp.stack([weight_norm, update_norm, trust])
    return (
        latents_out[None],
        latents_grad[None],
        pixels_grad[None],
        square_grad,
        square_first_new,
        square_second_new,
        square_new,
        square_new.astype(half),
        pixel_weight_grad,
        pixel_first_new,
        pixel_second_new,
        pixel_new,
        pixel_new.astype(half),
        latent_first_new,
        latent_second_new,
        latent_vectors_new,
        pixel_norm_first_new,
        pixel_norm_second_new,
        pixel_norm_new,
        matrix_norms,
    )


def solution(mesh):
    return jax.shard_map(
        local,
        mesh=mesh,
        in_specs=(
            P("dp", "seq", None),
            P("dp", "seq", None),
            P("dp", "seq"),
            P("dp", "seq", None),
            P(None, None, "dp"),
            P(None, None, "dp"),
            P(None, None, "dp"),
            P(None, None, "dp"),
            P(None, None, "dp"),
            P(None, None, "dp"),
            P(),
            P(),
            P(),
            P(),
            P(),
            P(),
        ),
        out_specs=(
            P("dp", "seq", None),
            P("dp", "seq", None),
            P("dp", "seq", None),
            P(None, None, "dp"),
            P(None, None, "dp"),
            P(None, None, "dp"),
            P(None, None, "dp"),
            P(None, None, "dp"),
            P(None, None, "dp"),
            P(None, None, "dp"),
            P(None, None, "dp"),
            P(None, None, "dp"),
            P(None, None, "dp"),
            P(),
            P(),
            P(),
            P(),
            P(),
            P(),
            P(),
        ),
        check_vma=False,
    )
```

```python
import functools

import jax
import jax.numpy as jnp
from jax import lax
from jax.experimental import pallas as pl
from jax.experimental.pallas import tpu as pltpu
from jax.sharding import PartitionSpec as P

STEP = 10


norm_epsilon = 1e-05
beta_one = 0.9
beta_two = 0.999
decay_rate = 0.01
epsilon = 1e-06
learn_rate = 0.25
vector_rate = 1.0
masked_score = -1e30
gelu_coeff = 0.7978845608028654


def adam_moments(grad, first, second):
    first_new = beta_one * first + (1.0 - beta_one) * grad
    second_new = beta_two * second + (1.0 - beta_two) * grad * grad
    ratio = (
        first_new
        / (1.0 - beta_one**STEP)
        / (jnp.sqrt(second_new / (1.0 - beta_two**STEP)) + epsilon)
    )
    return (first_new, second_new, ratio)

half = jnp.bfloat16
single = jnp.float32
swap = [(0, 1), (1, 0)]
main, rest = 256, 128
whole = pl.BlockSpec(memory_space=pltpu.VMEM)
remote = pl.BlockSpec(memory_space=pl.ANY)
scalars = pl.BlockSpec(memory_space=pltpu.SMEM)
params = pltpu.CompilerParams(vmem_limit_bytes=56 * 2**20)


def shape(dims, dtype):
    return jax.ShapeDtypeStruct(dims, dtype)


def contract(left, right, over_left, over_right):
    return lax.dot_general(left, right, (((over_left,), (over_right,)), ((), ())), preferred_element_type=single)


def nn(left, right):
    return contract(left, right, 1, 0)


def nt(left, right):
    return contract(left, right, 1, 1)


def tn(left, right):
    return contract(left, right, 0, 0)


def flip(array, mask):
    return lax.ppermute(array, "dp", [(i, i ^ mask) for i in range(lax.axis_size("dp"))])


def trade(array):
    return lax.ppermute(array, "seq", swap)


def special(groups, shard):
    return groups == 16 and shard % 32 == 0


def gather_blocks(block):
    got = [None] * 16
    got[0] = block
    got[8] = flip(got[0], 8)
    got[4] = flip(got[0], 4)
    got[1] = flip(got[0], 1)
    got[2] = flip(got[0], 2)
    got[3] = flip(got[2], 1)
    got[12] = flip(got[8], 4)
    got[5] = flip(got[4], 1)
    got[6] = flip(got[4], 2)
    got[9] = flip(got[8], 1)
    got[10] = flip(got[8], 2)
    got[7] = flip(got[5], 2)
    got[11] = flip(got[10], 1)
    got[13] = flip(got[12], 1)
    got[14] = flip(got[12], 2)
    got[15] = flip(got[13], 2)
    return got


def gather_matrices(squares, pixel):
    matrices, shard, width = squares.shape
    part = width // 2
    core = lax.axis_index("seq")
    groups = lax.axis_size("dp")
    block = jnp.concatenate(
        [lax.dynamic_slice_in_dim(squares[m], core * part, part, 1) for m in range(matrices)]
        + [lax.dynamic_slice_in_dim(pixel, core * main, main, 1)],
        axis=1,
    )
    if special(groups, shard):
        blocks = []
        for got in gather_blocks(block):
            blocks += [got, trade(got)]
        return blocks
    every = lax.all_gather(block, ("dp", "seq"), axis=0).reshape(groups, 2, shard, -1)
    return [every.transpose(1, 0, 2, 3).reshape(2, groups * shard, -1)]


def load_blocks(spot, blocks, target, sems):
    copies = []
    if len(blocks) == 1:
        copies.append(pltpu.make_async_copy(blocks[0], target, sems.at[0]))
    else:
        for i, block in enumerate(blocks):
            rows = block.shape[0]
            chip = lax.bitwise_xor(spot[0], i // 2)
            side = lax.bitwise_xor(spot[1], i % 2)
            place = target.at[side, pl.ds(pl.multiple_of(chip * rows, rows), rows)]
            copies.append(pltpu.make_async_copy(block, place, sems.at[i]))
    for copy in copies:
        copy.start()
    return copies


def store_terms(spot, terms, outs):
    if len(outs) == 1:
        outs[0][...] = terms[...].astype(half)
        return
    send_a, keep_a, send_b, keep_b = outs
    rows = terms.shape[0] // 16
    for o in range(16):
        chip = lax.bitwise_xor(spot[0], o)
        upper = terms[pl.ds(pl.multiple_of(chip * rows, rows), rows // 2), :].astype(half)
        lower = terms[pl.ds(pl.multiple_of(chip * rows + rows // 2, rows // 2), rows // 2), :].astype(half)
        (send_a if o & 1 else keep_a)[o // 2] = upper
        (send_b if o & 2 else keep_b)[(o // 4) * 2 + o % 2] = lower


def term_shapes(groups, shard, lanes):
    if special(groups, shard):
        return [shape((8, shard // 2, lanes), half)] * 4
    return [shape((groups * shard, lanes), half)]


def scatter_sum(terms, groups):
    if len(terms) == 1:
        return lax.psum_scatter(terms[0], "dp", scatter_dimension=0, tiled=True).astype(single)
    send_a, keep_a, send_b, keep_b = terms

    def split(array):
        array = array.reshape(-1, 2, *array.shape[1:])
        return array[:, 0], array[:, 1].astype(half)

    def add(kept, got):
        return kept.astype(single) + got.astype(single)

    a, b = add(keep_a, flip(send_a, 1)), add(keep_b, flip(send_b, 2))
    (keep_a, send_a), (keep_b, send_b) = split(a), split(b)
    a, b = add(keep_a, flip(send_a, 2)), add(keep_b, flip(send_b, 1))
    held = jnp.concatenate([a, b], axis=1)
    kept, sent = split(held)
    held = add(kept, flip(sent, 4))
    kept, sent = split(held)
    return add(kept, flip(sent, 8))[0]


def sum_all(array, seq):
    if seq:
        array = array + trade(array)
    mask = 1
    size = lax.axis_size("dp")
    while mask < size:
        if mask * 2 < size:
            one, two, three = flip(array, mask), flip(array, 2 * mask), flip(array, 3 * mask)
            array = (array + one) + (two + three)
            mask *= 4
        else:
            array = array + flip(array, mask)
            mask *= 2
    return array


def standard(values):
    center = values - jnp.mean(values, axis=-1, keepdims=True)
    inverse = lax.rsqrt(jnp.mean(center * center, axis=-1, keepdims=True) + norm_epsilon)
    return center * inverse, inverse


def standard_back(grad, gain, unit, inverse):
    scaled = grad * gain
    return inverse * (
        scaled - jnp.mean(scaled, axis=-1, keepdims=True) - unit * jnp.mean(scaled * unit, axis=-1, keepdims=True)
    )


def pixel_kernel(pixels, gain, shift, normed, stats, held, tail, sem):
    copy = pltpu.make_async_copy(pixels.at[:, 0, :], held, sem)
    copy.start()
    feats = held.shape[0]
    step = 256
    over = feats - main
    tail[...] = jnp.zeros_like(tail)
    copy.wait()

    @pl.loop(0, held.shape[1] // step)
    def _(i):
        lanes = pl.ds(pl.multiple_of(i * step, step), step)
        first, last = held[pl.ds(0, main), lanes], held[pl.ds(main, over), lanes]
        mean = (jnp.sum(first, axis=0, keepdims=True) + jnp.sum(last, axis=0, keepdims=True)) / feats
        first, last = first - mean, last - mean
        spread = (
            jnp.sum(first * first, axis=0, keepdims=True) + jnp.sum(last * last, axis=0, keepdims=True)
        ) / feats
        inverse = lax.rsqrt(spread + norm_epsilon)
        normed[pl.ds(0, main), lanes] = (first * inverse * gain[pl.ds(0, main)] + shift[pl.ds(0, main)]).astype(half)
        tail[pl.ds(0, over), :] = last * inverse * gain[pl.ds(main, over)] + shift[pl.ds(main, over)]
        normed[pl.ds(main, rest), lanes] = tail[...].astype(half)
        stats[0:1, lanes] = mean
        stats[1:2, lanes] = inverse


def norm_pixels(pixels, gain, shift):
    feats, _, count = pixels.shape
    return pl.pallas_call(
        pixel_kernel,
        out_shape=[shape((main + rest, count), half), shape((2, count), single)],
        in_specs=[remote, whole, whole],
        out_specs=[whole] * 2,
        scratch_shapes=[pltpu.VMEM((feats, count), single), pltpu.VMEM((rest, 256), single), pltpu.SemaphoreType.DMA],
        compiler_params=params,
        name="norm_pixels",
    )(pixels, gain, shift)


def latent_kernel(mine, theirs, vectors, normed):
    for t, source in enumerate((mine, theirs)):
        rows = source.shape[0]
        unit, _ = standard(source[...])
        normed[pl.ds(t * rows, rows), :] = (unit * vectors[0:1, :] + vectors[1:2, :]).astype(half)


def norm_latents(mine, theirs, vectors):
    return pl.pallas_call(
        latent_kernel,
        out_shape=shape((2 * mine.shape[0], mine.shape[1]), half),
        in_specs=[whole] * 3,
        out_specs=whole,
        compiler_params=params,
        name="norm_latents",
    )(mine, theirs, vectors)


def attend_kernel(count, scale, feats, spot, *refs):
    blocks = refs[:count]
    normed, pixels, keep, query, query_pix, sent, weights, sems = refs[count:]
    copies = load_blocks(spot, blocks, weights, sems)
    for copy in copies:
        copy.wait()
    part = normed.shape[1] // 2
    step = 256
    for t in range(normed.shape[0] // step):
        rows = pl.ds(t * step, step)
        value = nt(normed[rows, pl.ds(0, part)], weights[0, :, pl.ds(0, part)])
        value = value + nt(normed[rows, pl.ds(part, part)], weights[1, :, pl.ds(0, part)])
        value = value.astype(half)
        query[rows, :] = value
        query_pix[rows, pl.ds(0, main)] = (nn(value, weights[0, :, pl.ds(part, main)]) * scale).astype(half)
        query_pix[rows, pl.ds(main, rest)] = (nn(value, weights[1, :, pl.ds(part, rest)]) * scale).astype(half)
    tile = 128

    @pl.loop(0, normed.shape[0] // tile)
    def _(i):
        rows = pl.ds(pl.multiple_of(i * tile, tile), tile)
        scores = nn(query_pix[rows, pl.ds(0, main)], pixels[pl.ds(0, main), :])
        scores = scores + nn(query_pix[rows, pl.ds(main, rest)], pixels[pl.ds(main, rest), :])
        scores = jnp.where(keep[...] > 0, scores, masked_score)
        top = jnp.max(scores, axis=-1, keepdims=True)
        expo = jnp.exp(scores - top)
        total = jnp.sum(expo, axis=-1, keepdims=True)
        expo = expo.astype(half)
        sent[rows, pl.ds(0, main)] = nt(expo, pixels[pl.ds(0, main), :])
        last = nt(expo, pixels[pl.ds(main, rest), :])
        lane = lax.broadcasted_iota(jnp.int32, last.shape, 1)
        last = jnp.where(lane == feats - main, top, jnp.where(lane == feats - main + 1, total, last))
        sent[rows, pl.ds(main, rest)] = last


def attend(spot, blocks, normed, pixels, keep, scale, feats):
    rows, width = normed.shape
    lanes = blocks[0].shape[-1]
    return pl.pallas_call(
        functools.partial(attend_kernel, len(blocks), scale, feats),
        out_shape=[shape((rows, width), half), shape((rows, main + rest), half), shape((rows, main + rest), single)],
        in_specs=[scalars] + [remote] * len(blocks) + [whole] * 3,
        out_specs=[whole] * 3,
        scratch_shapes=[pltpu.VMEM((2, width, lanes), half), pltpu.SemaphoreType.DMA((len(blocks),))],
        compiler_params=params,
        name="attend",
    )(spot, *blocks, normed, pixels, keep)


def chain_kernel(count, terms_count, feats, spot, *refs):
    blocks, refs = refs[:count], refs[count:]
    (mine, theirs, latent_mine, latent_theirs, cot_mine, cot_theirs, vectors), refs = refs[:7], refs[7:]
    (latents_out, middle_grad, grad_pix, stats, sums), refs = refs[:5], refs[5:]
    term_outs, refs = refs[:terms_count], refs[terms_count:]
    weights, attended, middle_half, mixed, hidden_grad, active, out_half, attended_grad, value_mix, wide, terms, sems = refs
    copies = load_blocks(spot, blocks, weights, sems)
    for copy in copies:
        copy.wait()
    rows_all, width = attended.shape
    step = rows_all // 2
    part = width // 2

    def into(value, m):
        lanes = pl.ds(m * part, part)
        return nt(value[:, :part], weights[0, :, lanes]) + nt(value[:, part:], weights[1, :, lanes])

    def back(value, m, target):
        lanes = pl.ds(m * part, part)
        target[:, pl.ds(0, part)] = nn(value, weights[0, :, lanes])
        target[:, pl.ds(part, part)] = nn(value, weights[1, :, lanes])
        return target[...]

    sums[...] = jnp.zeros_like(sums)
    value_mix[...] = jnp.zeros_like(value_mix)
    for t in range(2):
        rows, other = pl.ds(t * step, step), pl.ds((1 - t) * step, step)
        latents, cotangent = (latent_mine, cot_mine) if t == 0 else (latent_theirs, cot_theirs)
        here, there = mine[rows, :], theirs[other, :]
        top_here, top_there = here[:, feats : feats + 1], there[:, feats : feats + 1]
        top = jnp.maximum(top_here, top_there)
        scale_here, scale_there = jnp.exp(top_here - top), jnp.exp(top_there - top)
        total = here[:, feats + 1 : feats + 2] * scale_here + there[:, feats + 1 : feats + 2] * scale_there
        mix = (here * scale_here + there * scale_there) / total
        lane = lax.broadcasted_iota(jnp.int32, mix.shape, 1)
        mix = jnp.where(lane < feats, mix, 0.0).astype(half)
        value_mix[rows, pl.ds(0, main + rest)] = mix
        attended_f = nt(mix[:, :main], weights[0, :, pl.ds(3 * part, main)])
        attended_f = attended_f + nt(mix[:, main:], weights[1, :, pl.ds(3 * part, rest)])
        wide[...] = attended_f
        value = attended_f.astype(half)
        attended[rows, :] = value
        middle = latents[...] + into(value, 0)
        unit, inverse = standard(middle)
        value = (unit * vectors[2:3, :] + vectors[3:4, :]).astype(half)
        mixed[rows, :] = value
        hidden = into(value, 1) + vectors[4:5, :]
        curve = jnp.tanh(gelu_coeff * (hidden + 0.044715 * hidden * hidden * hidden))
        value = (0.5 * hidden * (1.0 + curve)).astype(half)
        active[rows, :] = value
        if t == 0:
            latents_out[...] = middle + into(value, 2) + vectors[5:6, :]
        slope = 0.5 * (1.0 + curve) + 0.5 * hidden * (1.0 - curve * curve) * gelu_coeff * (
            1.0 + 3.0 * 0.044715 * hidden * hidden
        )
        value = cotangent[...].astype(half)
        out_half[rows, :] = value
        if t == 0:
            sums[5:6, :] = jnp.sum(value.astype(single), axis=0, keepdims=True)
        scratch = terms.at[pl.ds(0, step), pl.ds(0, width)]
        value = (back(value, 2, scratch) * slope).astype(half)
        hidden_grad[rows, :] = value
        if t == 0:
            sums[4:5, :] = jnp.sum(value.astype(single), axis=0, keepdims=True)
        mixed_grad = back(value, 1, scratch)
        if t == 0:
            sums[2:3, :] = jnp.sum(mixed_grad * unit, axis=0, keepdims=True)
            sums[3:4, :] = jnp.sum(mixed_grad, axis=0, keepdims=True)
        grad = cotangent[...] + standard_back(mixed_grad, vectors[2:3, :], unit, inverse)
        if t == 0:
            middle_grad[...] = grad
        value = grad.astype(half)
        middle_half[rows, :] = value
        value = back(value, 0, scratch).astype(half)
        attended_grad[rows, :] = value
        inner = jnp.sum(wide[...] * value.astype(single), axis=-1, keepdims=True)
        grad_pix[rows, pl.ds(0, main)] = nn(value, weights[0, :, pl.ds(3 * part, main)]).astype(half)
        grad_pix[rows, pl.ds(main, rest)] = nn(value, weights[1, :, pl.ds(3 * part, rest)]).astype(half)
        lane = lax.broadcasted_iota(jnp.int32, (step, 128), 1)
        stats[rows, :] = jnp.where(lane == 0, top + jnp.log(total), inner)
    side = pl.ds(pl.multiple_of(spot[1] * part, part), part)
    for m, (grad, value) in enumerate(((middle_half, attended), (hidden_grad, mixed), (out_half, active))):
        terms[:, pl.ds(m * part, part)] = tn(grad[...], value[:, side])
    side = pl.ds(pl.multiple_of(spot[1] * main, main), main)
    terms[:, pl.ds(3 * part, main)] = tn(attended_grad[...], value_mix[:, side])
    store_terms(spot, terms, term_outs)


def chain(spot, blocks, mine, theirs, latents, cotangents, vectors, feats, groups):
    rows, width = mine.shape[0], vectors.shape[1]
    lanes = blocks[0].shape[-1]
    outs = term_shapes(groups, width // groups, lanes)
    bits = pltpu.VMEM((rows, width), half)
    result = pl.pallas_call(
        functools.partial(chain_kernel, len(blocks), len(outs), feats),
        out_shape=[
            shape((rows // 2, width), single),
            shape((rows // 2, width), single),
            shape((rows, main + rest), half),
            shape((rows, 128), single),
            shape((8, width), single),
        ]
        + outs,
        in_specs=[scalars] + [remote] * len(blocks) + [whole] * 7,
        out_specs=[whole] * (5 + len(outs)),
        scratch_shapes=[pltpu.VMEM((2, width, lanes), half)]
        + [bits] * 7
        + [
            pltpu.VMEM((rows, 2 * main), half),
            pltpu.VMEM((rows // 2, width), single),
            pltpu.VMEM((width, lanes), single),
            pltpu.SemaphoreType.DMA((len(blocks),)),
        ],
        compiler_params=params,
        name="chain",
    )(spot, *blocks, mine, theirs, *latents, *cotangents, vectors)
    return result[:5], result[5:]


def pixel_back_kernel(
    scale, query_pix, grad_pix, stats, normed, keep, pixels, gain, pixel_stats, score_pix, pixels_grad, sums, held, made, query_t, grad_t, slope, shift, sem, sems
):
    copy = pltpu.make_async_copy(pixels.at[:, 0, :], held, sem)
    copy.start()
    feats, count = held.shape
    over = feats - main
    step = 512
    query_t[...] = jnp.transpose(query_pix[...].astype(single)).astype(half)
    grad_t[...] = jnp.transpose(grad_pix[...].astype(single)).astype(half)
    score_pix[...] = jnp.zeros_like(score_pix)
    slope[...] = jnp.zeros_like(slope)
    shift[...] = jnp.zeros_like(shift)
    log_total, inner = stats[:, 0:1], stats[:, 1:2]
    copy.wait()

    @pl.loop(0, count // step)
    def _(i):
        lanes = pl.ds(pl.multiple_of(i * step, step), step)
        first, last = normed[pl.ds(0, main), lanes], normed[pl.ds(main, rest), lanes]
        scores = nn(query_pix[:, pl.ds(0, main)], first) + nn(query_pix[:, pl.ds(main, rest)], last)
        weight_grad = nn(grad_pix[:, pl.ds(0, main)], first) + nn(grad_pix[:, pl.ds(main, rest)], last)
        attn = jnp.exp(jnp.where(keep[:, lanes] > 0, scores, masked_score) - log_total)
        score_grad = (attn * (weight_grad - inner)).astype(half)
        attn = attn.astype(half)
        score_pix[:, pl.ds(0, main)] += nt(score_grad, first)
        score_pix[:, pl.ds(main, rest)] += nt(score_grad, last)
        grad = nn(query_t[...], score_grad) + nn(grad_t[...], attn)
        mean, inverse = pixel_stats[0:1, lanes], pixel_stats[1:2, lanes]
        unit_a = (held[pl.ds(0, main), lanes] - mean) * inverse
        unit_b = (held[pl.ds(main, over), lanes] - mean) * inverse
        grad_a, grad_b = grad[:main], grad[main : main + over]
        for rows, g, u in ((pl.ds(0, main), grad_a, unit_a), (pl.ds(main, over), grad_b, unit_b)):
            product = g * u
            slope[rows, :] += sum(product[:, 128 * j : 128 * j + 128] for j in range(step // 128))
            shift[rows, :] += sum(g[:, 128 * j : 128 * j + 128] for j in range(step // 128))
        scaled_a, scaled_b = grad_a * gain[pl.ds(0, main)], grad_b * gain[pl.ds(main, over)]
        flat = (jnp.sum(scaled_a, axis=0, keepdims=True) + jnp.sum(scaled_b, axis=0, keepdims=True)) / feats
        along = (
            jnp.sum(scaled_a * unit_a, axis=0, keepdims=True) + jnp.sum(scaled_b * unit_b, axis=0, keepdims=True)
        ) / feats
        made[pl.ds(0, main), lanes] = inverse * (scaled_a - flat - unit_a * along)
        made[pl.ds(main, over), lanes] = inverse * (scaled_b - flat - unit_b * along)
        pltpu.make_async_copy(made.at[:, lanes], pixels_grad.at[:, 0, lanes], sems.at[i]).start()

    score_pix[...] = score_pix[...] * scale
    lane = lax.broadcasted_iota(jnp.int32, (feats, 128), 1)
    sums[...] = jnp.where(
        lane == 0,
        jnp.sum(slope[...], axis=-1, keepdims=True),
        jnp.sum(shift[...], axis=-1, keepdims=True),
    )

    @pl.loop(0, count // step)
    def _(i):
        lanes = pl.ds(pl.multiple_of(i * step, step), step)
        pltpu.make_async_copy(made.at[:, lanes], pixels_grad.at[:, 0, lanes], sems.at[i]).wait()


def pixel_back(query_pix, grad_pix, stats, normed, keep, pixels, gain, pixel_stats, scale):
    feats, _, count = pixels.shape
    rows = query_pix.shape[0]
    big = pltpu.VMEM((feats, count), single)
    return pl.pallas_call(
        functools.partial(pixel_back_kernel, scale),
        out_shape=[shape((rows, main + rest), single), shape(pixels.shape, single), shape((feats, 128), single)],
        in_specs=[whole] * 5 + [remote, whole, whole],
        out_specs=[whole, remote, whole],
        scratch_shapes=[
            big,
            big,
            pltpu.VMEM((main + rest, rows), half),
            pltpu.VMEM((main + rest, rows), half),
            pltpu.VMEM((feats, 128), single),
            pltpu.VMEM((feats, 128), single),
            pltpu.SemaphoreType.DMA,
            pltpu.SemaphoreType.DMA((count // 512,)),
        ],
        compiler_params=params,
        name="pixel_back",
    )(query_pix, grad_pix, stats, normed, keep, pixels, gain, pixel_stats)


def query_back_kernel(count, terms_count, spot, *refs):
    blocks, refs = refs[:count], refs[count:]
    (mine, theirs, query, normed, latents, middle_grad, vectors), refs = refs[:7], refs[7:]
    (latents_grad, sums), refs = refs[:2], refs[2:]
    term_outs, refs = refs[:terms_count], refs[terms_count:]
    weights, score_pix, query_grad, wide, terms, sems = refs
    copies = load_blocks(spot, blocks, weights, sems)
    rows_all, width = query.shape
    step = rows_all // 2
    part = width // 2
    score_pix[:, pl.ds(main + rest, rest)] = jnp.zeros((rows_all, rest), half)
    for t in range(2):
        rows, other = pl.ds(t * step, step), pl.ds((1 - t) * step, step)
        score_pix[rows, pl.ds(0, main + rest)] = (mine[rows, :] + theirs[other, :]).astype(half)
    for copy in copies:
        copy.wait()
    for t in range(2):
        rows = pl.ds(t * step, step)
        value = nt(score_pix[rows, pl.ds(0, main)], weights[0, :, pl.ds(part, main)])
        value = value + nt(score_pix[rows, pl.ds(main, rest)], weights[1, :, pl.ds(part, rest)])
        query_grad[rows, :] = value.astype(half)
    side = pl.ds(pl.multiple_of(spot[1] * part, part), part)
    terms[:, pl.ds(0, part)] = tn(query_grad[...], normed[:, side])
    side = pl.ds(pl.multiple_of(spot[1] * main, main), main)
    terms[:, pl.ds(part, main)] = tn(query[...], score_pix[:, side])
    store_terms(spot, terms, term_outs)
    value = query_grad[pl.ds(0, step), :]
    wide[:, pl.ds(0, part)] = nn(value, weights[0, :, pl.ds(0, part)])
    wide[:, pl.ds(part, part)] = nn(value, weights[1, :, pl.ds(0, part)])
    unit, inverse = standard(latents[...])
    grad = wide[...]
    latents_grad[...] = middle_grad[...] + standard_back(grad, vectors[0:1, :], unit, inverse)
    sums[...] = jnp.zeros_like(sums)
    sums[0:1, :] = jnp.sum(grad * unit, axis=0, keepdims=True)
    sums[1:2, :] = jnp.sum(grad, axis=0, keepdims=True)


def query_back(spot, blocks, mine, theirs, query, normed, latents, middle_grad, vectors, groups):
    rows, width = query.shape
    lanes = blocks[0].shape[-1]
    outs = term_shapes(groups, width // groups, lanes)
    result = pl.pallas_call(
        functools.partial(query_back_kernel, len(blocks), len(outs)),
        out_shape=[shape((rows // 2, width), single), shape((8, width), single)] + outs,
        in_specs=[scalars] + [remote] * len(blocks) + [whole] * 7,
        out_specs=[whole] * (2 + len(outs)),
        scratch_shapes=[
            pltpu.VMEM((2, width, lanes), half),
            pltpu.VMEM((rows, 2 * main), half),
            pltpu.VMEM((rows, width), half),
            pltpu.VMEM((rows // 2, width), single),
            pltpu.VMEM((width, lanes), single),
            pltpu.SemaphoreType.DMA((len(blocks),)),
        ],
        compiler_params=params,
        name="query_back",
    )(spot, *blocks, mine, theirs, query, normed, latents, middle_grad, vectors)
    return result[:2], result[2:]


def local(
    latents,
    pixels,
    keep_mask,
    cotangent,
    square_weights,
    square_first,
    square_second,
    pixel_weights,
    pixel_first,
    pixel_second,
    latent_vectors,
    latent_first,
    latent_second,
    pixel_norm,
    pixel_norm_first,
    pixel_norm_second,
):
    width = latents.shape[2]
    feats = pixels.shape[2]
    scale = width ** (-0.5)
    shard_width = square_weights.shape[2]
    rank = lax.axis_index("seq")
    groups = lax.axis_size("dp")
    part = width // 2
    spot = jnp.stack([lax.axis_index("dp"), rank]).astype(jnp.int32)

    def turned(array):
        return jnp.transpose(array, (0, 2, 1))

    square_p, square_m, square_v = turned(square_weights), turned(square_first), turned(square_second)
    pixel_p, pixel_m, pixel_v = turned(pixel_weights), turned(pixel_first), turned(pixel_second)
    square_copy = square_p.astype(half)
    pixel_copy = jnp.pad(pixel_p.astype(half), ((0, 0), (0, 0), (0, 2 * main - feats)))
    early_blocks = gather_matrices(square_copy[:1], pixel_copy[0])
    late_blocks = gather_matrices(square_copy[1:], pixel_copy[1])

    latents_two = (latents[0], trade(latents[0]))
    cotangent_two = (cotangent[0], trade(cotangent[0]))
    pixels_t = jnp.transpose(pixels, (2, 0, 1))
    gain, shift = pixel_norm[0][:, None], pixel_norm[1][:, None]
    pixel_normed, pixel_stats = norm_pixels(pixels_t, gain, shift)
    normed = norm_latents(*latents_two, latent_vectors)
    query, query_pix, sent = attend(spot, early_blocks, normed, pixel_normed, keep_mask, scale, feats)
    (latents_out, middle_grad, grad_pix, stats, chain_sums), early_terms = chain(
        spot, late_blocks, sent, trade(sent), latents_two, cotangent_two, latent_vectors, feats, groups
    )
    score_pix, pixels_grad, pixel_sums = pixel_back(
        query_pix, grad_pix, stats, pixel_normed, keep_mask, pixels_t, gain, pixel_stats, scale
    )
    (latents_grad, query_sums), late_terms = query_back(
        spot, early_blocks, score_pix, trade(score_pix), query, normed, latents[0], middle_grad, latent_vectors, groups
    )
    early = scatter_sum(early_terms, groups)
    late = scatter_sum(late_terms, groups)

    first = rank == 0

    def joined(array):
        other = trade(array)
        return jnp.where(first, array, other), jnp.where(first, other, array)

    early_low, early_high = joined(early)
    late_low, late_high = joined(late)

    def square(low, high, m):
        return jnp.concatenate([low[:, m * part : (m + 1) * part], high[:, m * part : (m + 1) * part]], axis=1)

    def pixel(low, high, m):
        return jnp.concatenate(
            [low[:, m * part : m * part + main], high[:, m * part : m * part + feats - main]], axis=1
        )

    square_grad = jnp.stack([square(late_low, late_high, 0)] + [square(early_low, early_high, m) for m in range(3)])
    pixel_weight_grad = jnp.stack([pixel(late_low, late_high, 1), pixel(early_low, early_high, 3)])

    norm_terms = jnp.pad(jnp.transpose(pixel_sums[:, :2]), ((6, 0), (0, width - feats)))
    vector_sums = sum_all(chain_sums + query_sums + norm_terms, True)
    latent_vector_grad, pixel_norm_grad = vector_sums[:6], vector_sums[6:, :feats]
    square_first_new, square_second_new, square_ratio = adam_moments(square_grad, square_m, square_v)
    pixel_first_new, pixel_second_new, pixel_ratio = adam_moments(pixel_weight_grad, pixel_m, pixel_v)
    square_update = square_ratio + decay_rate * square_p
    pixel_update = pixel_ratio + decay_rate * pixel_p
    weight_squares = jnp.concatenate(
        [jnp.sum(square_p * square_p, axis=(1, 2)), jnp.sum(pixel_p * pixel_p, axis=(1, 2))]
    )
    update_squares = jnp.concatenate(
        [jnp.sum(square_update * square_update, axis=(1, 2)), jnp.sum(pixel_update * pixel_update, axis=(1, 2))]
    )
    square_sums = sum_all(jnp.concatenate([weight_squares, update_squares]), False)
    weight_norm = jnp.sqrt(square_sums[:6])
    update_norm = jnp.sqrt(square_sums[6:])
    trust = weight_norm / (update_norm + epsilon)
    square_new = square_p - learn_rate * trust[:4, None, None] * square_update
    pixel_new = pixel_p - learn_rate * trust[4:, None, None] * pixel_update
    latent_first_new, latent_second_new, latent_ratio = adam_moments(latent_vector_grad, latent_first, latent_second)
    latent_vectors_new = latent_vectors - vector_rate * latent_ratio
    pixel_norm_first_new, pixel_norm_second_new, norm_ratio = adam_moments(
        pixel_norm_grad, pixel_norm_first, pixel_norm_second
    )
    pixel_norm_new = pixel_norm - vector_rate * norm_ratio
    matrix_norms = jnp.stack([weight_norm, update_norm, trust])
    return (
        latents_out[None],
        latents_grad[None],
        jnp.transpose(pixels_grad, (1, 2, 0)),
        turned(square_grad),
        turned(square_first_new),
        turned(square_second_new),
        turned(square_new),
        turned(square_new.astype(half)),
        turned(pixel_weight_grad),
        turned(pixel_first_new),
        turned(pixel_second_new),
        turned(pixel_new),
        turned(pixel_new.astype(half)),
        latent_first_new,
        latent_second_new,
        latent_vectors_new,
        pixel_norm_first_new,
        pixel_norm_second_new,
        pixel_norm_new,
        matrix_norms,
    )


def solution(mesh):
    return jax.shard_map(
        local,
        mesh=mesh,
        in_specs=(
            P("dp", "seq", None),
            P("dp", "seq", None),
            P("dp", "seq"),
            P("dp", "seq", None),
            P(None, None, "dp"),
            P(None, None, "dp"),
            P(None, None, "dp"),
            P(None, None, "dp"),
            P(None, None, "dp"),
            P(None, None, "dp"),
            P(),
            P(),
            P(),
            P(),
            P(),
            P(),
        ),
        out_specs=(
            P("dp", "seq", None),
            P("dp", "seq", None),
            P("dp", "seq", None),
            P(None, None, "dp"),
            P(None, None, "dp"),
            P(None, None, "dp"),
            P(None, None, "dp"),
            P(None, None, "dp"),
            P(None, None, "dp"),
            P(None, None, "dp"),
            P(None, None, "dp"),
            P(None, None, "dp"),
            P(None, None, "dp"),
            P(),
            P(),
            P(),
            P(),
            P(),
            P(),
            P(),
        ),
        check_vma=False,
    )
```

```python
import functools

import jax
import jax.numpy as jnp
from jax import lax
from jax.experimental import pallas as pl
from jax.experimental.pallas import tpu as pltpu
from jax.sharding import PartitionSpec as P

STEP = 10


norm_epsilon = 1e-05
beta_one = 0.9
beta_two = 0.999
decay_rate = 0.01
epsilon = 1e-06
learn_rate = 0.25
vector_rate = 1.0
masked_score = -1e30
gelu_coeff = 0.7978845608028654


def adam_moments(grad, first, second):
    first_new = beta_one * first + (1.0 - beta_one) * grad
    second_new = beta_two * second + (1.0 - beta_two) * grad * grad
    ratio = (
        first_new
        / (1.0 - beta_one**STEP)
        / (jnp.sqrt(second_new / (1.0 - beta_two**STEP)) + epsilon)
    )
    return (first_new, second_new, ratio)

half = jnp.bfloat16
single = jnp.float32
swap = [(0, 1), (1, 0)]
main, rest = 256, 128
whole = pl.BlockSpec(memory_space=pltpu.VMEM)
remote = pl.BlockSpec(memory_space=pl.ANY)
scalars = pl.BlockSpec(memory_space=pltpu.SMEM)
params = pltpu.CompilerParams(vmem_limit_bytes=56 * 2**20)


def cost(micros):
    return pl.CostEstimate(flops=int(micros * 1.1e9), bytes_accessed=1024, transcendentals=0)


def shape(dims, dtype):
    return jax.ShapeDtypeStruct(dims, dtype)


def contract(left, right, over_left, over_right):
    return lax.dot_general(left, right, (((over_left,), (over_right,)), ((), ())), preferred_element_type=single)


def nn(left, right):
    return contract(left, right, 1, 0)


def nt(left, right):
    return contract(left, right, 1, 1)


def tn(left, right):
    return contract(left, right, 0, 0)


def flip(array, mask):
    return lax.ppermute(array, "dp", [(i, i ^ mask) for i in range(lax.axis_size("dp"))])


def trade(array):
    return lax.ppermute(array, "seq", swap)


def special(groups, shard):
    return groups == 16 and shard % 32 == 0


def tie_kernel(*refs):
    pass


def tie(arrays, *after):
    return pl.pallas_call(
        tie_kernel,
        out_shape=[shape(a.shape, a.dtype) for a in arrays],
        in_specs=[remote] * (len(arrays) + len(after)),
        out_specs=[remote] * len(arrays),
        input_output_aliases={i: i for i in range(len(arrays))},
        cost_estimate=cost(0.1),
        name="tie",
    )(*arrays, *after)


def stack_kernel(plan, *refs):
    outs = refs[len(refs) - len(plan) :]
    for out, parts in zip(outs, plan):
        rows = out.shape[0] // len(parts)
        for i, (source, part) in enumerate(parts):
            out[pl.ds(i * rows, rows), :] = refs[source][pl.ds(part * rows, rows), :]


def stack(arrays, rows, plan, *after):
    lanes, dtype = arrays[0].shape[1], arrays[0].dtype
    return pl.pallas_call(
        functools.partial(stack_kernel, plan),
        out_shape=[shape((rows * len(parts), lanes), dtype) for parts in plan],
        in_specs=[whole] * len(arrays) + [remote] * len(after),
        out_specs=[whole] * len(plan),
        compiler_params=params,
        cost_estimate=cost(1.5),
        name="stack",
    )(*arrays, *after)


def gather_blocks(block, early, late):
    rows = block.shape[0]
    first = [flip(block, o) for o in (8, 4, 3, 2, 1)]
    plan = (((2, 0), (0, 0)), ((1, 0), (0, 0)), ((5, 0), (0, 0), (1, 0), (2, 0), (3, 0), (4, 0)))
    across, both, gathered = stack([*first, block], rows, plan, early)
    second = [flip(across, 4), flip(both, 2), flip(both, 1)]
    seven, twelve, twelve_ten = stack(second, rows, (((0, 0),), ((0, 1),), ((0, 1), (1, 1))), late)
    third = [flip(seven, 8), flip(twelve, 2), flip(twelve_ten, 1)]
    return [
        ((0, 8, 4, 3, 2, 1), gathered),
        ((7, 12), second[0]),
        ((6, 10), second[1]),
        ((5, 9), second[2]),
        ((15,), third[0]),
        ((14,), third[1]),
        ((13, 11), third[2]),
    ]


def pack_kernel(feats, spot, squares, pixels, block):
    side = spot[1]
    part = squares.shape[2] // 2
    lanes = pl.ds(pl.multiple_of(side * part, part), part)
    over = feats - main

    def pixel(m):
        last = pixels[m, :, pl.ds(main, over)]
        last = jnp.concatenate([last, jnp.zeros((last.shape[0], main - over), single)], axis=1)
        return jnp.where(side == 0, pixels[m, :, pl.ds(0, main)], last).astype(half)

    block[:, pl.ds(0, part)] = squares[0, :, lanes].astype(half)
    block[:, pl.ds(part, main)] = pixel(0)
    for m in range(1, 4):
        block[:, pl.ds(m * part + main, part)] = squares[m, :, lanes].astype(half)
    block[:, pl.ds(4 * part + main, main)] = pixel(1)


def pack(spot, squares, pixels):
    _, shard, width = squares.shape
    return pl.pallas_call(
        functools.partial(pack_kernel, pixels.shape[2]),
        out_shape=shape((shard, 4 * (width // 2) + 2 * main), half),
        in_specs=[scalars, whole, whole],
        out_specs=whole,
        compiler_params=params,
        cost_estimate=cost(2),
        name="pack",
    )(spot, squares, pixels)


def gather_matrices(block, early, late):
    groups = lax.axis_size("dp")
    shard = block.shape[0]
    if special(groups, shard):
        arrays, layout = [], []
        for positions, array in gather_blocks(block, early, late):
            arrays += [array, trade(array)]
            layout += [(positions, 0), (positions, 1)]
        return arrays, tuple(layout)
    every = lax.all_gather(block, ("dp", "seq"), axis=0).reshape(groups, 2, shard, -1)
    return [every.transpose(1, 0, 2, 3).reshape(2, groups * shard, -1)], ()


def load_blocks(spot, blocks, layout, target, first, sems):
    copies = []
    lanes = pl.ds(first, target.shape[2])
    if not layout:
        copies.append(pltpu.make_async_copy(blocks[0].at[:, :, lanes], target, sems.at[0]))
    for block, (positions, turn) in zip(blocks, layout):
        rows = block.shape[0] // len(positions)
        side = lax.bitwise_xor(spot[1], turn)
        for i, o in enumerate(positions):
            chip = lax.bitwise_xor(spot[0], o)
            place = target.at[side, pl.ds(pl.multiple_of(chip * rows, rows), rows)]
            copies.append(pltpu.make_async_copy(block.at[pl.ds(i * rows, rows), lanes], place, sems.at[len(copies)]))
    for copy in copies:
        copy.start()
    return copies


written = ((13, 11), (14,), (15,), (5, 9), (6, 10), (7, 12), (1,), (2,), (3,), (4,), (8,), (0,))


def store_terms(spot, terms, outs):
    if len(outs) == 1:
        outs[0][...] = terms[...].astype(half)
        return
    for positions, out in zip(written, outs):
        rows = terms.shape[0] // 16
        for i, o in enumerate(positions):
            chip = lax.bitwise_xor(spot[0], o)
            out[pl.ds(i * rows, rows), :] = terms[pl.ds(pl.multiple_of(chip * rows, rows), rows), :].astype(half)


def term_shapes(groups, shard, lanes):
    if special(groups, shard):
        return [shape((len(positions) * shard, lanes), half) for positions in written]
    return [shape((groups * shard, lanes), half)]


def send_first(terms, *after):
    if len(terms) == 1:
        return None
    got = [flip(terms[0], 1), flip(terms[1], 2), flip(terms[2], 8)]
    return tie(got, *after) if after else got


def send_second(terms, got, *after):
    if len(terms) == 1:
        return None
    rows = terms[-1].shape[0]

    def added(array, *more):
        total = array[rows:].astype(single)
        for other in more[0]:
            total = total + other.astype(single)
        first = array[:rows].astype(single)
        for other in more[1]:
            first = first + other.astype(single)
        return jnp.concatenate([first.astype(half), total.astype(half)])

    twelve, ten = got[0][:rows], got[0][rows:]
    got = [
        flip(terms[3], 1),
        flip(added(terms[4], [ten], []), 2),
        flip(added(terms[5], [twelve, got[1]], [got[2]]), 4),
    ]
    return tie(got, *after) if after else got


def send_third(terms, got):
    if len(terms) == 1:
        return [lax.psum_scatter(terms[0], "dp", scatter_dimension=0, tiled=True)]
    rows = terms[-1].shape[0]
    one, two, three, four, eight, _ = [term.astype(single) for term in terms[6:]]
    x, y, z = [array.astype(single) for array in got]
    sent = [
        (eight + x[rows:] + y[rows:] + z[rows:], 8),
        (four + x[:rows] + y[:rows], 4),
        (three + z[:rows], 3),
        (two, 2),
        (one, 1),
    ]
    return [flip(array.astype(half), mask) for array, mask in sent]


def sum_own(terms, got):
    if len(terms) > 1:
        got = [terms[-1], *got]
    total = got[0].astype(single)
    for array in got[1:]:
        total = total + array.astype(single)
    return total


def sum_all(array):
    mask = 1
    size = lax.axis_size("dp")
    while mask < size:
        if mask * 2 < size:
            one, two, three = flip(array, mask), flip(array, 2 * mask), flip(array, 3 * mask)
            array = (array + one) + (two + three)
            mask *= 4
        else:
            array = array + flip(array, mask)
            mask *= 2
    return array


def standard(values):
    center = values - jnp.mean(values, axis=-1, keepdims=True)
    inverse = lax.rsqrt(jnp.mean(center * center, axis=-1, keepdims=True) + norm_epsilon)
    return center * inverse, inverse


def standard_back(grad, gain, unit, inverse):
    scaled = grad * gain
    return inverse * (
        scaled - jnp.mean(scaled, axis=-1, keepdims=True) - unit * jnp.mean(scaled * unit, axis=-1, keepdims=True)
    )


def pixel_kernel(pixels, gain, shift, normed, stats, held, tail, sem):
    copy = pltpu.make_async_copy(pixels.at[:, 0, :], held, sem)
    copy.start()
    feats = held.shape[0]
    step = 256
    over = feats - main
    tail[...] = jnp.zeros_like(tail)
    copy.wait()

    @pl.loop(0, held.shape[1] // step)
    def _(i):
        lanes = pl.ds(pl.multiple_of(i * step, step), step)
        first, last = held[pl.ds(0, main), lanes], held[pl.ds(main, over), lanes]
        mean = (jnp.sum(first, axis=0, keepdims=True) + jnp.sum(last, axis=0, keepdims=True)) / feats
        first, last = first - mean, last - mean
        spread = (
            jnp.sum(first * first, axis=0, keepdims=True) + jnp.sum(last * last, axis=0, keepdims=True)
        ) / feats
        inverse = lax.rsqrt(spread + norm_epsilon)
        normed[pl.ds(0, main), lanes] = (first * inverse * gain[pl.ds(0, main)] + shift[pl.ds(0, main)]).astype(half)
        tail[pl.ds(0, over), :] = last * inverse * gain[pl.ds(main, over)] + shift[pl.ds(main, over)]
        normed[pl.ds(main, rest), lanes] = tail[...].astype(half)
        stats[0:1, lanes] = mean
        stats[1:2, lanes] = inverse


def norm_pixels(pixels, gain, shift):
    feats, _, count = pixels.shape
    return pl.pallas_call(
        pixel_kernel,
        out_shape=[shape((main + rest, count), half), shape((2, count), single)],
        in_specs=[remote, whole, whole],
        out_specs=[whole] * 2,
        scratch_shapes=[pltpu.VMEM((feats, count), single), pltpu.VMEM((rest, 256), single), pltpu.SemaphoreType.DMA],
        compiler_params=params,
        cost_estimate=cost(7),
        name="norm_pixels",
    )(pixels, gain, shift)


def latent_kernel(latents, vectors, normed):
    unit, _ = standard(latents[...])
    normed[...] = (unit * vectors[0:1, :] + vectors[1:2, :]).astype(half)


def norm_latents(latents, vectors):
    return pl.pallas_call(
        latent_kernel,
        out_shape=shape(latents.shape, half),
        in_specs=[whole] * 2,
        out_specs=whole,
        compiler_params=params,
        cost_estimate=cost(2),
        name="norm_latents",
    )(latents, vectors)


def attend_kernel(count, layout, scale, feats, spot, *refs):
    blocks = refs[:count]
    mine, theirs, pixels, keep, query, query_pix, sent, weights, sems = refs[count:]
    copies = load_blocks(spot, blocks, layout, weights, 0, sems)
    for copy in copies:
        copy.wait()
    step, part = mine.shape[0], mine.shape[1] // 2
    for t, normed in enumerate((mine, theirs)):
        rows = pl.ds(t * step, step)
        value = nt(normed[:, pl.ds(0, part)], weights[0, :, pl.ds(0, part)])
        value = value + nt(normed[:, pl.ds(part, part)], weights[1, :, pl.ds(0, part)])
        value = value.astype(half)
        query[rows, :] = value
        query_pix[rows, pl.ds(0, main)] = (nn(value, weights[0, :, pl.ds(part, main)]) * scale).astype(half)
        query_pix[rows, pl.ds(main, rest)] = (nn(value, weights[1, :, pl.ds(part, rest)]) * scale).astype(half)
    tile = 128

    @pl.loop(0, query.shape[0] // tile)
    def _(i):
        rows = pl.ds(pl.multiple_of(i * tile, tile), tile)
        scores = nn(query_pix[rows, :], pixels[...])
        scores = jnp.where(keep[...] > 0, scores, masked_score)
        top = jnp.max(scores, axis=-1, keepdims=True)
        expo = jnp.exp(scores - top)
        total = jnp.sum(expo, axis=-1, keepdims=True)
        expo = expo.astype(half)
        value = nt(expo, pixels[...])
        lane = lax.broadcasted_iota(jnp.int32, value.shape, 1)
        sent[rows, :] = jnp.where(lane == feats, top, jnp.where(lane == feats + 1, total, value))


def attend(spot, gathered, normed, pixels, keep, scale, feats):
    blocks, layout = gathered
    rows, width = 2 * normed[0].shape[0], normed[0].shape[1]
    lanes = width // 2 + main
    return pl.pallas_call(
        functools.partial(attend_kernel, len(blocks), layout, scale, feats),
        out_shape=[shape((rows, width), half), shape((rows, main + rest), half), shape((rows, main + rest), single)],
        in_specs=[scalars] + [remote] * len(blocks) + [whole] * 4,
        out_specs=[whole] * 3,
        scratch_shapes=[pltpu.VMEM((2, width, lanes), half), pltpu.SemaphoreType.DMA((32,))],
        compiler_params=params,
        cost_estimate=cost(14),
        name="attend",
    )(spot, *blocks, *normed, pixels, keep)


def chain_kernel(count, layout, terms_count, feats, spot, *refs):
    blocks, refs = refs[:count], refs[count:]
    (mine, theirs, latent_mine, latent_theirs, cot_mine, cot_theirs, vectors), refs = refs[:7], refs[7:]
    (latents_out, middle_grad, grad_pix, stats, sums), refs = refs[:5], refs[5:]
    term_outs, refs = refs[:terms_count], refs[terms_count:]
    weights, attended, middle_half, mixed, hidden_grad, active, out_half, attended_grad, value_mix, wide, terms, sems = refs
    copies = load_blocks(spot, blocks, layout, weights, blocks[0].shape[-1] - weights.shape[2], sems)
    for copy in copies:
        copy.wait()
    rows_all, width = attended.shape
    step = rows_all // 2
    part = width // 2

    def into(value, m):
        lanes = pl.ds(m * part, part)
        return nt(value[:, :part], weights[0, :, lanes]) + nt(value[:, part:], weights[1, :, lanes])

    def back(value, m, target):
        lanes = pl.ds(m * part, part)
        target[:, pl.ds(0, part)] = nn(value, weights[0, :, lanes])
        target[:, pl.ds(part, part)] = nn(value, weights[1, :, lanes])
        return target[...]

    sums[...] = jnp.zeros_like(sums)
    value_mix[...] = jnp.zeros_like(value_mix)
    for t in range(2):
        rows, other = pl.ds(t * step, step), pl.ds((1 - t) * step, step)
        latents, cotangent = (latent_mine, cot_mine) if t == 0 else (latent_theirs, cot_theirs)
        here, there = mine[rows, :], theirs[other, :]
        top_here, top_there = here[:, feats : feats + 1], there[:, feats : feats + 1]
        top = jnp.maximum(top_here, top_there)
        scale_here, scale_there = jnp.exp(top_here - top), jnp.exp(top_there - top)
        total = here[:, feats + 1 : feats + 2] * scale_here + there[:, feats + 1 : feats + 2] * scale_there
        mix = (here * scale_here + there * scale_there) / total
        lane = lax.broadcasted_iota(jnp.int32, mix.shape, 1)
        mix = jnp.where(lane < feats, mix, 0.0).astype(half)
        value_mix[rows, pl.ds(0, main + rest)] = mix
        attended_f = nt(mix[:, :main], weights[0, :, pl.ds(3 * part, main)])
        attended_f = attended_f + nt(mix[:, main:], weights[1, :, pl.ds(3 * part, rest)])
        wide[...] = attended_f
        value = attended_f.astype(half)
        attended[rows, :] = value
        middle = latents[...] + into(value, 0)
        unit, inverse = standard(middle)
        value = (unit * vectors[2:3, :] + vectors[3:4, :]).astype(half)
        mixed[rows, :] = value
        hidden = into(value, 1) + vectors[4:5, :]
        curve = jnp.tanh(gelu_coeff * (hidden + 0.044715 * hidden * hidden * hidden))
        value = (0.5 * hidden * (1.0 + curve)).astype(half)
        active[rows, :] = value
        if t == 0:
            latents_out[...] = middle + into(value, 2) + vectors[5:6, :]
        slope = 0.5 * (1.0 + curve) + 0.5 * hidden * (1.0 - curve * curve) * gelu_coeff * (
            1.0 + 3.0 * 0.044715 * hidden * hidden
        )
        value = cotangent[...].astype(half)
        out_half[rows, :] = value
        if t == 0:
            sums[5:6, :] = jnp.sum(value.astype(single), axis=0, keepdims=True)
        scratch = terms.at[pl.ds(0, step), pl.ds(0, width)]
        value = (back(value, 2, scratch) * slope).astype(half)
        hidden_grad[rows, :] = value
        if t == 0:
            sums[4:5, :] = jnp.sum(value.astype(single), axis=0, keepdims=True)
        mixed_grad = back(value, 1, scratch)
        if t == 0:
            sums[2:3, :] = jnp.sum(mixed_grad * unit, axis=0, keepdims=True)
            sums[3:4, :] = jnp.sum(mixed_grad, axis=0, keepdims=True)
        grad = cotangent[...] + standard_back(mixed_grad, vectors[2:3, :], unit, inverse)
        if t == 0:
            middle_grad[...] = grad
        value = grad.astype(half)
        middle_half[rows, :] = value
        value = back(value, 0, scratch).astype(half)
        attended_grad[rows, :] = value
        inner = jnp.sum(wide[...] * value.astype(single), axis=-1, keepdims=True)
        grad_pix[rows, pl.ds(0, main)] = nn(value, weights[0, :, pl.ds(3 * part, main)]).astype(half)
        grad_pix[rows, pl.ds(main, rest)] = nn(value, weights[1, :, pl.ds(3 * part, rest)]).astype(half)
        lane = lax.broadcasted_iota(jnp.int32, (step, 128), 1)
        stats[rows, :] = jnp.where(lane == 0, top + jnp.log(total), inner)
    side = pl.ds(pl.multiple_of(spot[1] * part, part), part)
    for m, (grad, value) in enumerate(((middle_half, attended), (hidden_grad, mixed), (out_half, active))):
        terms[:, pl.ds(m * part, part)] = tn(grad[...], value[:, side])
    side = pl.ds(pl.multiple_of(spot[1] * main, main), main)
    terms[:, pl.ds(3 * part, main)] = tn(attended_grad[...], value_mix[:, side])
    store_terms(spot, terms, term_outs)


def chain(spot, gathered, mine, theirs, latents, cotangents, vectors, feats, groups):
    blocks, layout = gathered
    rows, width = mine.shape[0], vectors.shape[1]
    lanes = 3 * (width // 2) + main
    outs = term_shapes(groups, width // groups, lanes)
    bits = pltpu.VMEM((rows, width), half)
    result = pl.pallas_call(
        functools.partial(chain_kernel, len(blocks), layout, len(outs), feats),
        out_shape=[
            shape((rows // 2, width), single),
            shape((rows // 2, width), single),
            shape((rows, main + rest), half),
            shape((rows, 128), single),
            shape((8, width), single),
        ]
        + outs,
        in_specs=[scalars] + [remote] * len(blocks) + [whole] * 7,
        out_specs=[whole] * (5 + len(outs)),
        scratch_shapes=[pltpu.VMEM((2, width, lanes), half)]
        + [bits] * 7
        + [
            pltpu.VMEM((rows, 2 * main), half),
            pltpu.VMEM((rows // 2, width), single),
            pltpu.VMEM((width, lanes), single),
            pltpu.SemaphoreType.DMA((32,)),
        ],
        compiler_params=params,
        cost_estimate=cost(20),
        name="chain",
    )(spot, *blocks, mine, theirs, *latents, *cotangents, vectors)
    return result[:5], result[5:]


def pixel_back_kernel(scale, turn, turns, *refs):
    (query_pix, grad_pix, stats, normed, keep, pixels, gain, pixel_stats), refs = refs[:8], refs[8:]
    if turn > 0:
        (score_before, sums_before, _), refs = refs[:3], refs[3:]
    score_pix, sums, pixels_grad, held, made, query_t, grad_t, slope, shift, sem, sems = refs
    origin = turn * held.shape[1]
    copy = pltpu.make_async_copy(pixels.at[:, 0, pl.ds(origin, held.shape[1])], held, sem)
    copy.start()
    feats, count = held.shape
    over = feats - main
    step = 512
    query_t[...] = jnp.transpose(query_pix[...].astype(single)).astype(half)
    grad_t[...] = jnp.transpose(grad_pix[...].astype(single)).astype(half)
    score_pix[...] = score_before[...] if turn > 0 else jnp.zeros_like(score_pix)
    slope[...] = jnp.zeros_like(slope)
    shift[...] = jnp.zeros_like(shift)
    log_total, inner = stats[:, 0:1], stats[:, 1:2]
    copy.wait()

    @pl.loop(0, count // step)
    def _(i):
        here = pl.ds(pl.multiple_of(i * step, step), step)
        lanes = pl.ds(pl.multiple_of(origin + i * step, step), step)
        values = normed[:, lanes]
        scores = nn(query_pix[...], values)
        weight_grad = nn(grad_pix[...], values)
        attn = jnp.exp(jnp.where(keep[:, lanes] > 0, scores, masked_score) - log_total)
        score_grad = (attn * (weight_grad - inner)).astype(half)
        attn = attn.astype(half)
        score_pix[...] += nt(score_grad, values)
        grad = nn(query_t[...], score_grad) + nn(grad_t[...], attn)
        mean, inverse = pixel_stats[0:1, lanes], pixel_stats[1:2, lanes]
        unit_a = (held[pl.ds(0, main), here] - mean) * inverse
        unit_b = (held[pl.ds(main, over), here] - mean) * inverse
        grad_a, grad_b = grad[:main], grad[main : main + over]
        for rows, g, u in ((pl.ds(0, main), grad_a, unit_a), (pl.ds(main, over), grad_b, unit_b)):
            product = g * u
            slope[rows, :] += sum(product[:, 128 * j : 128 * j + 128] for j in range(step // 128))
            shift[rows, :] += sum(g[:, 128 * j : 128 * j + 128] for j in range(step // 128))
        scaled_a, scaled_b = grad_a * gain[pl.ds(0, main)], grad_b * gain[pl.ds(main, over)]
        flat = (jnp.sum(scaled_a, axis=0, keepdims=True) + jnp.sum(scaled_b, axis=0, keepdims=True)) / feats
        along = (
            jnp.sum(scaled_a * unit_a, axis=0, keepdims=True) + jnp.sum(scaled_b * unit_b, axis=0, keepdims=True)
        ) / feats
        made[pl.ds(0, main), here] = inverse * (scaled_a - flat - unit_a * along)
        made[pl.ds(main, over), here] = inverse * (scaled_b - flat - unit_b * along)
        pltpu.make_async_copy(made.at[:, here], pixels_grad.at[:, 0, lanes], sems.at[i]).start()

    if turn == turns - 1:
        score_pix[...] = score_pix[...] * scale
    lane = lax.broadcasted_iota(jnp.int32, (feats, 128), 1)
    both = jnp.where(
        lane == 0,
        jnp.sum(slope[...], axis=-1, keepdims=True),
        jnp.sum(shift[...], axis=-1, keepdims=True),
    )
    sums[...] = both + sums_before[...] if turn > 0 else both

    @pl.loop(0, count // step)
    def _(i):
        here = pl.ds(pl.multiple_of(i * step, step), step)
        lanes = pl.ds(pl.multiple_of(origin + i * step, step), step)
        pltpu.make_async_copy(made.at[:, here], pixels_grad.at[:, 0, lanes], sems.at[i]).wait()


def pixel_back(query_pix, grad_pix, stats, normed, keep, pixels, gain, pixel_stats, scale, turn, turns, before):
    feats, _, count = pixels.shape
    rows = query_pix.shape[0]
    held = pltpu.VMEM((feats, count // turns), single)
    return pl.pallas_call(
        functools.partial(pixel_back_kernel, scale, turn, turns),
        out_shape=[shape((rows, main + rest), single), shape((feats, 128), single), shape(pixels.shape, single)],
        in_specs=[whole] * 5 + [remote, whole, whole] + [whole, whole, remote][: len(before)],
        out_specs=[whole, whole, remote],
        scratch_shapes=[
            held,
            held,
            pltpu.VMEM((main + rest, rows), half),
            pltpu.VMEM((main + rest, rows), half),
            pltpu.VMEM((feats, 128), single),
            pltpu.VMEM((feats, 128), single),
            pltpu.SemaphoreType.DMA,
            pltpu.SemaphoreType.DMA((count // turns // 512,)),
        ],
        input_output_aliases={10: 2} if before else {},
        compiler_params=params,
        cost_estimate=cost(18 / turns),
        name="pixel_back",
    )(query_pix, grad_pix, stats, normed, keep, pixels, gain, pixel_stats, *before)


def query_back_kernel(count, layout, terms_count, spot, *refs):
    blocks, refs = refs[:count], refs[count:]
    (mine, theirs, query, normed_mine, normed_theirs, latents, middle_grad, vectors), refs = refs[:8], refs[8:]
    (latents_grad, sums), refs = refs[:2], refs[2:]
    term_outs, refs = refs[:terms_count], refs[terms_count:]
    weights, score_pix, query_grad, wide, terms, sems = refs
    copies = load_blocks(spot, blocks, layout, weights, 0, sems)
    rows_all, width = query.shape
    step = rows_all // 2
    part = width // 2
    score_pix[:, pl.ds(main + rest, rest)] = jnp.zeros((rows_all, rest), half)
    for t in range(2):
        rows, other = pl.ds(t * step, step), pl.ds((1 - t) * step, step)
        score_pix[rows, pl.ds(0, main + rest)] = (mine[rows, :] + theirs[other, :]).astype(half)
    for copy in copies:
        copy.wait()
    for t in range(2):
        rows = pl.ds(t * step, step)
        value = nt(score_pix[rows, pl.ds(0, main)], weights[0, :, pl.ds(part, main)])
        value = value + nt(score_pix[rows, pl.ds(main, rest)], weights[1, :, pl.ds(part, rest)])
        query_grad[rows, :] = value.astype(half)
    side = pl.ds(pl.multiple_of(spot[1] * part, part), part)
    value = tn(query_grad[pl.ds(0, step), :], normed_mine[:, side])
    terms[:, pl.ds(0, part)] = value + tn(query_grad[pl.ds(step, step), :], normed_theirs[:, side])
    side = pl.ds(pl.multiple_of(spot[1] * main, main), main)
    terms[:, pl.ds(part, main)] = tn(query[...], score_pix[:, side])
    store_terms(spot, terms, term_outs)
    value = query_grad[pl.ds(0, step), :]
    wide[:, pl.ds(0, part)] = nn(value, weights[0, :, pl.ds(0, part)])
    wide[:, pl.ds(part, part)] = nn(value, weights[1, :, pl.ds(0, part)])
    unit, inverse = standard(latents[...])
    grad = wide[...]
    latents_grad[...] = middle_grad[...] + standard_back(grad, vectors[0:1, :], unit, inverse)
    sums[...] = jnp.zeros_like(sums)
    sums[0:1, :] = jnp.sum(grad * unit, axis=0, keepdims=True)
    sums[1:2, :] = jnp.sum(grad, axis=0, keepdims=True)


def query_back(spot, gathered, mine, theirs, query, normed, latents, middle_grad, vectors, groups):
    blocks, layout = gathered
    rows, width = query.shape
    lanes = width // 2 + main
    outs = term_shapes(groups, width // groups, lanes)
    result = pl.pallas_call(
        functools.partial(query_back_kernel, len(blocks), layout, len(outs)),
        out_shape=[shape((rows // 2, width), single), shape((8, width), single)] + outs,
        in_specs=[scalars] + [remote] * len(blocks) + [whole] * 8,
        out_specs=[whole] * (2 + len(outs)),
        scratch_shapes=[
            pltpu.VMEM((2, width, lanes), half),
            pltpu.VMEM((rows, 2 * main), half),
            pltpu.VMEM((rows, width), half),
            pltpu.VMEM((rows // 2, width), single),
            pltpu.VMEM((width, lanes), single),
            pltpu.SemaphoreType.DMA((32,)),
        ],
        compiler_params=params,
        cost_estimate=cost(9),
        name="query_back",
    )(spot, *blocks, mine, theirs, query, *normed, latents, middle_grad, vectors)
    return result[:2], result[2:]


def moments_kernel(feats, *refs):
    spot, late_mine, late_theirs, early_mine, early_theirs, vectors, *refs = refs
    square_p, square_m, square_v, pixel_p, pixel_m, pixel_v, *refs = refs
    square_outs, pixel_outs, sums = refs[:4], refs[4:8], refs[8]
    width = square_p.shape[2]
    part = width // 2
    first = spot[1] == 0
    lane = lax.broadcasted_iota(jnp.int32, (1, width), 1)
    row = jnp.zeros((1, width), single)
    for m in range(6):
        mine, theirs = (late_mine, late_theirs) if m in (0, 4) else (early_mine, early_theirs)
        if m < 4:
            lanes = pl.ds(max(m - 1, 0) * part, part)
            sides, outs, k = (pl.ds(0, part), pl.ds(part, part)), square_outs, m
            params_now, first_now, second_now = square_p, square_m, square_v
        else:
            lanes = pl.ds(part if m == 4 else 3 * part, main)
            sides, outs, k = (pl.ds(0, main), pl.ds(main, feats - main)), pixel_outs, m - 4
            params_now, first_now, second_now = pixel_p, pixel_m, pixel_v
        own, other = mine[:, lanes], theirs[:, lanes]
        weight_total, update_total = jnp.zeros((1, 1), single), jnp.zeros((1, 1), single)
        for side, grad in zip(sides, (jnp.where(first, own, other), jnp.where(first, other, own))):
            grad = grad[:, : side.size]
            weight = params_now[k, :, side]
            first_new, second_new, ratio = adam_moments(grad, first_now[k, :, side], second_now[k, :, side])
            update = ratio + decay_rate * weight
            for out, value in zip(outs, (grad, first_new, second_new, update)):
                out[k, :, side] = value
            weight_total = weight_total + jnp.sum(weight * weight, keepdims=True)
            update_total = update_total + jnp.sum(update * update, keepdims=True)
        row = row + jnp.where(lane == m, weight_total, jnp.where(lane == 6 + m, update_total, 0.0))
    sums[...] = jnp.zeros_like(sums)
    sums[pl.ds(0, 8), :] = vectors[...]
    sums[8:9, :] = row


def moments(spot, late, early, vectors, square, pixel):
    big, small = shape(square[0].shape, single), shape(pixel[0].shape, single)
    return pl.pallas_call(
        functools.partial(moments_kernel, pixel[0].shape[2]),
        out_shape=[big] * 4 + [small] * 4 + [shape((16, big.shape[2]), single)],
        in_specs=[scalars] + [whole] * 11,
        out_specs=[whole] * 9,
        compiler_params=params,
        cost_estimate=cost(5),
        name="moments",
    )(spot, *late, *early, vectors, *square, *pixel)


def apply_kernel(sums, square_p, square_u, pixel_p, pixel_u, *refs):
    states, outs = refs[:6], refs[6:]
    square_new, square_copy, pixel_new, pixel_copy, norms, *news = outs
    weight_norm, update_norm = jnp.sqrt(sums[8:9, 0:6]), jnp.sqrt(sums[8:9, 6:12])
    trust = weight_norm / (update_norm + epsilon)
    for row, value in enumerate((weight_norm, update_norm, trust)):
        norms[row : row + 1, :] = value
    for m in range(6):
        k, weight, update, new, copy = (
            (m, square_p, square_u, square_new, square_copy)
            if m < 4
            else (m - 4, pixel_p, pixel_u, pixel_new, pixel_copy)
        )
        value = weight[k] - learn_rate * trust[:, m : m + 1] * update[k]
        new[k] = value
        copy[k] = value.astype(half)
    feats = states[3].shape[1]
    for grad, (value, first, second), out in (
        (sums[0:6, :], states[:3], news[:3]),
        (sums[6:8, 0:feats], states[3:], news[3:]),
    ):
        first_new, second_new, ratio = adam_moments(grad, first[...], second[...])
        out[0][...] = value[...] - vector_rate * ratio
        out[1][...] = first_new
        out[2][...] = second_new


def apply(sums, square_p, square_u, pixel_p, pixel_u, vectors, norms):
    outs = [(square_p, single), (square_p, half), (pixel_p, single), (pixel_p, half)]
    states = [*vectors, *norms]
    return pl.pallas_call(
        apply_kernel,
        out_shape=[shape(a.shape, dtype) for a, dtype in outs]
        + [shape((3, 6), single)]
        + [shape(a.shape, single) for a in states],
        in_specs=[whole] * 11,
        out_specs=[whole] * 11,
        compiler_params=params,
        cost_estimate=cost(4),
        name="apply",
    )(sums, square_p, square_u, pixel_p, pixel_u, *states)


def local(
    latents,
    pixels,
    keep_mask,
    cotangent,
    square_weights,
    square_first,
    square_second,
    pixel_weights,
    pixel_first,
    pixel_second,
    latent_vectors,
    latent_first,
    latent_second,
    pixel_norm,
    pixel_norm_first,
    pixel_norm_second,
):
    width = latents.shape[2]
    feats = pixels.shape[2]
    scale = width ** (-0.5)
    rank = lax.axis_index("seq")
    groups = lax.axis_size("dp")
    spot = jnp.stack([lax.axis_index("dp"), rank]).astype(jnp.int32)

    def turned(array):
        return jnp.transpose(array, (0, 2, 1))

    square = [turned(array) for array in (square_weights, square_first, square_second)]
    pixel = [turned(array) for array in (pixel_weights, pixel_first, pixel_second)]

    latents_two = (latents[0], trade(latents[0]))
    cotangent_two = (cotangent[0], trade(cotangent[0]))
    pixels_t = jnp.transpose(pixels, (2, 0, 1))
    gain, shift = pixel_norm[0][:, None], pixel_norm[1][:, None]
    pixel_normed, pixel_stats = norm_pixels(pixels_t, gain, shift)
    normed = norm_latents(latents[0], latent_vectors)
    normed = (normed, trade(normed))
    blocks = gather_matrices(pack(spot, square[0], pixel[0]), pixel_normed, normed[0])
    query, query_pix, sent = attend(spot, blocks, normed, pixel_normed, keep_mask, scale, feats)
    (latents_out, middle_grad, grad_pix, stats, chain_sums), early_terms = chain(
        spot, blocks, sent, trade(sent), latents_two, cotangent_two, latent_vectors, feats, groups
    )
    pixel_args = (query_pix, grad_pix, stats, pixel_normed, keep_mask, pixels_t, gain, pixel_stats, scale)
    turn_one = pixel_back(*pixel_args, 0, 2, ())
    if len(early_terms) > 1:
        *early_got, score_pix = tie([*send_first(early_terms), turn_one[0]], turn_one[1])
        turn_two = pixel_back(*pixel_args, 1, 2, [score_pix, *turn_one[1:]])
        early_got = send_second(early_terms, early_got, turn_two[0])
    else:
        turn_two, early_got = pixel_back(*pixel_args, 1, 2, turn_one), None
    score_pix, pixel_sums, pixels_grad = turn_two
    (latents_grad, query_sums), late_terms = query_back(
        spot, blocks, score_pix, trade(score_pix), query, normed, latents[0], middle_grad, latent_vectors, groups
    )
    early_got = send_third(early_terms, early_got)
    if len(late_terms) > 1:
        tied = tie([*late_terms[:3], *early_got], late_terms[3])
        late_terms, early_got = [*tied[:3], *late_terms[3:]], tied[3:]
    early = sum_own(early_terms, early_got)
    late = sum_own(late_terms, send_third(late_terms, send_second(late_terms, send_first(late_terms))))

    norm_terms = jnp.pad(jnp.transpose(pixel_sums[:, :2]), ((6, 0), (0, width - feats)))
    vector_terms = chain_sums + query_sums + norm_terms
    vector_terms = vector_terms + trade(vector_terms)
    square_grad, square_first_new, square_second_new, square_u, *rest_outs = moments(
        spot, (late, trade(late)), (early, trade(early)), vector_terms, square, pixel
    )
    pixel_weight_grad, pixel_first_new, pixel_second_new, pixel_u, sums = rest_outs
    square_new, square_copy, pixel_new, pixel_copy, matrix_norms, *news = apply(
        sum_all(sums),
        square[0],
        square_u,
        pixel[0],
        pixel_u,
        (latent_vectors, latent_first, latent_second),
        (pixel_norm, pixel_norm_first, pixel_norm_second),
    )
    latent_vectors_new, latent_first_new, latent_second_new = news[:3]
    pixel_norm_new, pixel_norm_first_new, pixel_norm_second_new = news[3:]
    return (
        latents_out[None],
        latents_grad[None],
        jnp.transpose(pixels_grad, (1, 2, 0)),
        turned(square_grad),
        turned(square_first_new),
        turned(square_second_new),
        turned(square_new),
        turned(square_copy),
        turned(pixel_weight_grad),
        turned(pixel_first_new),
        turned(pixel_second_new),
        turned(pixel_new),
        turned(pixel_copy),
        latent_first_new,
        latent_second_new,
        latent_vectors_new,
        pixel_norm_first_new,
        pixel_norm_second_new,
        pixel_norm_new,
        matrix_norms,
    )


def solution(mesh):
    return jax.shard_map(
        local,
        mesh=mesh,
        in_specs=(
            P("dp", "seq", None),
            P("dp", "seq", None),
            P("dp", "seq"),
            P("dp", "seq", None),
            P(None, None, "dp"),
            P(None, None, "dp"),
            P(None, None, "dp"),
            P(None, None, "dp"),
            P(None, None, "dp"),
            P(None, None, "dp"),
            P(),
            P(),
            P(),
            P(),
            P(),
            P(),
        ),
        out_specs=(
            P("dp", "seq", None),
            P("dp", "seq", None),
            P("dp", "seq", None),
            P(None, None, "dp"),
            P(None, None, "dp"),
            P(None, None, "dp"),
            P(None, None, "dp"),
            P(None, None, "dp"),
            P(None, None, "dp"),
            P(None, None, "dp"),
            P(None, None, "dp"),
            P(None, None, "dp"),
            P(None, None, "dp"),
            P(),
            P(),
            P(),
            P(),
            P(),
            P(),
            P(),
        ),
        check_vma=False,
    )
```

```python
import functools

import jax
import jax.numpy as jnp
from jax import lax
from jax.experimental import pallas as pl
from jax.experimental.pallas import tpu as pltpu
from jax.sharding import PartitionSpec as P

STEP = 10


norm_epsilon = 1e-05
beta_one = 0.9
beta_two = 0.999
decay_rate = 0.01
epsilon = 1e-06
learn_rate = 0.25
vector_rate = 1.0
masked_score = -1e30
gelu_coeff = 0.7978845608028654


def adam_moments(grad, first, second):
    first_new = beta_one * first + (1.0 - beta_one) * grad
    second_new = beta_two * second + (1.0 - beta_two) * grad * grad
    ratio = (
        first_new
        / (1.0 - beta_one**STEP)
        / (jnp.sqrt(second_new / (1.0 - beta_two**STEP)) + epsilon)
    )
    return (first_new, second_new, ratio)

half = jnp.bfloat16
single = jnp.float32
swap = [(0, 1), (1, 0)]
main, rest = 256, 128
whole = pl.BlockSpec(memory_space=pltpu.VMEM)
remote = pl.BlockSpec(memory_space=pl.ANY)
scalars = pl.BlockSpec(memory_space=pltpu.SMEM)
params = pltpu.CompilerParams(vmem_limit_bytes=56 * 2**20)
params_all = pltpu.CompilerParams(vmem_limit_bytes=63 * 2**20)


def cost(micros):
    return pl.CostEstimate(flops=int(micros * 1.1e9), bytes_accessed=1024, transcendentals=0)


def shape(dims, dtype):
    return jax.ShapeDtypeStruct(dims, dtype)


def contract(left, right, over_left, over_right):
    return lax.dot_general(left, right, (((over_left,), (over_right,)), ((), ())), preferred_element_type=single)


def nn(left, right):
    return contract(left, right, 1, 0)


def nt(left, right):
    return contract(left, right, 1, 1)


def tn(left, right):
    return contract(left, right, 0, 0)


def flip(array, mask):
    return lax.ppermute(array, "dp", [(i, i ^ mask) for i in range(lax.axis_size("dp"))])


def trade(array):
    return lax.ppermute(array, "seq", swap)


def special(groups, shard):
    return groups == 16 and shard % 32 == 0


def tie_kernel(*refs):
    pass


def tie(arrays, *after):
    return pl.pallas_call(
        tie_kernel,
        out_shape=[shape(a.shape, a.dtype) for a in arrays],
        in_specs=[remote] * (len(arrays) + len(after)),
        out_specs=[remote] * len(arrays),
        input_output_aliases={i: i for i in range(len(arrays))},
        cost_estimate=cost(0.1),
        name="tie",
    )(*arrays, *after)


def stack_kernel(plan, *refs):
    outs = refs[len(refs) - len(plan) :]
    for out, parts in zip(outs, plan):
        rows = out.shape[0] // len(parts)
        for i, (source, part) in enumerate(parts):
            out[pl.ds(i * rows, rows), :] = refs[source][pl.ds(part * rows, rows), :]


def stack(arrays, rows, plan, *after):
    lanes, dtype = arrays[0].shape[1], arrays[0].dtype
    return pl.pallas_call(
        functools.partial(stack_kernel, plan),
        out_shape=[shape((rows * len(parts), lanes), dtype) for parts in plan],
        in_specs=[whole] * len(arrays) + [remote] * len(after),
        out_specs=[whole] * len(plan),
        compiler_params=params,
        cost_estimate=cost(1.5),
        name="stack",
    )(*arrays, *after)


def gather_blocks(block, early, late):
    rows = block.shape[0]
    one, two, four, three, eight = [flip(block, o) for o in (1, 2, 4, 3, 8)]
    across, both = stack([three, four, eight], rows, (((0, 0), (2, 0)), ((1, 0), (2, 0))), early)
    (gathered,) = stack([block, eight, four, three, two, one], rows, (tuple((i, 0) for i in range(6)),))
    second = [flip(across, 4), flip(both, 2), flip(both, 1)]
    seven, twelve, twelve_ten = stack(second[:2], rows, (((0, 0),), ((0, 1),), ((0, 1), (1, 1))), second[2], late)
    third = [flip(seven, 8), flip(twelve, 2), flip(twelve_ten, 1)]
    return [
        ((0, 8, 4, 3, 2, 1), gathered),
        ((7, 12), second[0]),
        ((6, 10), second[1]),
        ((5, 9), second[2]),
        ((15,), third[0]),
        ((14,), third[1]),
        ((13, 11), third[2]),
    ]


def pack_kernel(feats, spot, squares, pixels, block):
    side = spot[1]
    part = squares.shape[2] // 2
    lanes = pl.ds(pl.multiple_of(side * part, part), part)
    over = feats - main

    def pixel(m):
        last = pixels[m, :, pl.ds(main, over)]
        last = jnp.concatenate([last, jnp.zeros((last.shape[0], main - over), single)], axis=1)
        return jnp.where(side == 0, pixels[m, :, pl.ds(0, main)], last).astype(half)

    block[:, pl.ds(0, part)] = squares[0, :, lanes].astype(half)
    block[:, pl.ds(part, main)] = pixel(0)
    block[:, pl.ds(part + main, main)] = pixel(1)
    for m in range(1, 4):
        block[:, pl.ds(m * part + 2 * main, part)] = squares[m, :, lanes].astype(half)


def pack(spot, squares, pixels):
    _, shard, width = squares.shape
    return pl.pallas_call(
        functools.partial(pack_kernel, pixels.shape[2]),
        out_shape=shape((shard, 4 * (width // 2) + 2 * main), half),
        in_specs=[scalars, whole, whole],
        out_specs=whole,
        compiler_params=params,
        cost_estimate=cost(2),
        name="pack",
    )(spot, squares, pixels)


def gather_matrices(block, early, late):
    groups = lax.axis_size("dp")
    shard = block.shape[0]
    if special(groups, shard):
        arrays, layout = [], []
        for positions, array in gather_blocks(block, early, late):
            arrays += [array, trade(array)]
            layout += [(positions, 0), (positions, 1)]
        return arrays, tuple(layout)
    every = lax.all_gather(block, ("dp", "seq"), axis=0).reshape(groups, 2, shard, -1)
    return [every.transpose(1, 0, 2, 3).reshape(2, groups * shard, -1)], ()


def copy_all(pairs, sems, first=0):
    copies = [pltpu.make_async_copy(source, target, sems.at[first + i]) for i, (source, target) in enumerate(pairs)]
    for copy in copies:
        copy.start()
    return copies


def wait_all(copies):
    for copy in copies:
        copy.wait()


def load_blocks(spot, blocks, layout, target, first, sems, base=0):
    pairs = []
    lanes = pl.ds(first, target.shape[2])
    if not layout:
        pairs.append((blocks[0].at[:, :, lanes], target))
    for block, (positions, turn) in zip(blocks, layout):
        rows = block.shape[0] // len(positions)
        side = lax.bitwise_xor(spot[1], turn)
        for i, o in enumerate(positions):
            chip = lax.bitwise_xor(spot[0], o)
            place = target.at[side, pl.ds(pl.multiple_of(chip * rows, rows), rows)]
            pairs.append((block.at[pl.ds(i * rows, rows), lanes], place))
    return copy_all(pairs, sems, base)


written = ((13, 11), (14,), (15,), (5, 9), (6, 10), (7, 12), (1,), (2,), (3,), (4,), (8,), (0,))


def store_terms(spot, terms, outs, start, count, sems, base):
    lanes = pl.ds(start, count)
    if len(outs) == 1:
        return copy_all([(terms.at[:, lanes], outs[0].at[:, lanes])], sems, base)
    pairs = []
    rows = terms.shape[0] // 16
    for positions, out in zip(written, outs):
        for i, o in enumerate(positions):
            chip = lax.bitwise_xor(spot[0], o)
            source = terms.at[pl.ds(pl.multiple_of(chip * rows, rows), rows), lanes]
            pairs.append((source, out.at[pl.ds(i * rows, rows), lanes]))
    return copy_all(pairs, sems, base)


def term_shapes(groups, shard, lanes):
    if special(groups, shard):
        return [shape((len(positions) * shard, lanes), half) for positions in written]
    return [shape((groups * shard, lanes), half)]


def send_first(terms, *after):
    if len(terms) == 1:
        return None
    got = [flip(terms[0], 1), flip(terms[1], 2), flip(terms[2], 8)]
    return tie(got, *after) if after else got


def send_second(terms, got, *after):
    if len(terms) == 1:
        return None
    rows = terms[-1].shape[0]

    def added(array, *more):
        total = array[rows:].astype(single)
        for other in more[0]:
            total = total + other.astype(single)
        first = array[:rows].astype(single)
        for other in more[1]:
            first = first + other.astype(single)
        return jnp.concatenate([first.astype(half), total.astype(half)])

    twelve, ten = got[0][:rows], got[0][rows:]
    got = [
        flip(terms[3], 1),
        flip(added(terms[4], [ten], []), 2),
        flip(added(terms[5], [twelve, got[1]], [got[2]]), 4),
    ]
    return tie(got, *after) if after else got


def send_third(terms, got):
    if len(terms) == 1:
        return [lax.psum_scatter(terms[0], "dp", scatter_dimension=0, tiled=True)]
    rows = terms[-1].shape[0]
    one, two = terms[6:8]
    three, four, eight = [term.astype(single) for term in terms[8:11]]
    upper = [array[:rows].astype(single) for array in got]
    lower = [array[rows:].astype(single) for array in got]
    sent = [
        (one, 1),
        (two, 2),
        (four + upper[0] + upper[1], 4),
        (three + upper[2], 3),
        (eight + lower[0] + lower[1] + lower[2], 8),
    ]
    return [flip(array.astype(half), mask) for array, mask in sent]


def sum_own(terms, got):
    if len(terms) > 1:
        got = [terms[-1], *got]
    total = got[0].astype(single)
    for array in got[1:]:
        total = total + array.astype(single)
    return total


def sum_all(array):
    mask = 1
    size = lax.axis_size("dp")
    while mask < size:
        if mask * 2 < size:
            one, two, three = flip(array, mask), flip(array, 2 * mask), flip(array, 3 * mask)
            array = (array + one) + (two + three)
            mask *= 4
        else:
            array = array + flip(array, mask)
            mask *= 2
    return array


def standard(values):
    center = values - jnp.mean(values, axis=-1, keepdims=True)
    inverse = lax.rsqrt(jnp.mean(center * center, axis=-1, keepdims=True) + norm_epsilon)
    return center * inverse, inverse


def standard_back(grad, gain, unit, inverse):
    scaled = grad * gain
    return inverse * (
        scaled - jnp.mean(scaled, axis=-1, keepdims=True) - unit * jnp.mean(scaled * unit, axis=-1, keepdims=True)
    )


def pixel_kernel(pixels, gain, shift, normed, stats, held, tail, sem):
    copy = pltpu.make_async_copy(pixels.at[:, 0, :], held, sem)
    copy.start()
    feats = held.shape[0]
    step = 256
    over = feats - main
    tail[...] = jnp.zeros_like(tail)
    copy.wait()

    @pl.loop(0, held.shape[1] // step)
    def _(i):
        lanes = pl.ds(pl.multiple_of(i * step, step), step)
        first, last = held[pl.ds(0, main), lanes], held[pl.ds(main, over), lanes]
        mean = (jnp.sum(first, axis=0, keepdims=True) + jnp.sum(last, axis=0, keepdims=True)) / feats
        first, last = first - mean, last - mean
        spread = (
            jnp.sum(first * first, axis=0, keepdims=True) + jnp.sum(last * last, axis=0, keepdims=True)
        ) / feats
        inverse = lax.rsqrt(spread + norm_epsilon)
        normed[pl.ds(0, main), lanes] = (first * inverse * gain[pl.ds(0, main)] + shift[pl.ds(0, main)]).astype(half)
        tail[pl.ds(0, over), :] = last * inverse * gain[pl.ds(main, over)] + shift[pl.ds(main, over)]
        normed[pl.ds(main, rest), lanes] = tail[...].astype(half)
        stats[0:1, lanes] = mean
        stats[1:2, lanes] = inverse


def norm_pixels(pixels, gain, shift):
    feats, _, count = pixels.shape
    return pl.pallas_call(
        pixel_kernel,
        out_shape=[shape((main + rest, count), half), shape((2, count), single)],
        in_specs=[remote, whole, whole],
        out_specs=[whole] * 2,
        scratch_shapes=[pltpu.VMEM((feats, count), single), pltpu.VMEM((rest, 256), single), pltpu.SemaphoreType.DMA],
        compiler_params=params,
        cost_estimate=cost(7),
        name="norm_pixels",
    )(pixels, gain, shift)


def latent_kernel(latents, vectors, normed):
    unit, _ = standard(latents[...])
    normed[...] = (unit * vectors[0:1, :] + vectors[1:2, :]).astype(half)


def norm_latents(latents, vectors):
    return pl.pallas_call(
        latent_kernel,
        out_shape=shape(latents.shape, half),
        in_specs=[whole] * 2,
        out_specs=whole,
        compiler_params=params,
        cost_estimate=cost(2),
        name="norm_latents",
    )(latents, vectors)


def attend_kernel(count, layout, scale, feats, spot, *refs):
    blocks = refs[:count]
    mine, theirs, pixels_in, keep, query_out, query_pix, sent, *refs = refs[count:]
    weights, normed, pixels, query, scores, sems, more = refs
    copies = copy_all([(mine, normed.at[0]), (theirs, normed.at[1])], more)
    copies += load_blocks(spot, blocks, layout, weights, 0, sems)
    wait_all(copies)
    late = copy_all([(pixels_in, pixels)], more, 2)
    step, part = mine.shape[0], mine.shape[1] // 2
    for t in range(2):
        rows = pl.ds(t * step, step)
        value = nt(normed[t, :, pl.ds(0, part)], weights[0, :, pl.ds(0, part)])
        value = value + nt(normed[t, :, pl.ds(part, part)], weights[1, :, pl.ds(0, part)])
        value = value.astype(half)
        query[rows, :] = value
        query_pix[rows, pl.ds(0, main)] = (nn(value, weights[0, :, pl.ds(part, main)]) * scale).astype(half)
        query_pix[rows, pl.ds(main, rest)] = (nn(value, weights[1, :, pl.ds(part, rest)]) * scale).astype(half)
    wait_all(late)
    late = copy_all([(query, query_out)], more, 2)
    step = 512
    peak = None
    for j in range(pixels.shape[1] // step):
        lanes = pl.ds(j * step, step)
        value = nn(query_pix[...], pixels[:, lanes])
        value = jnp.where(keep[:, lanes] > 0, value, masked_score)
        scores[:, lanes] = value
        for k in range(step // 128):
            some = value[:, 128 * k : 128 * k + 128]
            peak = some if peak is None else jnp.maximum(peak, some)
    top = jnp.max(peak, axis=-1, keepdims=True)
    total = jnp.zeros_like(peak)
    mix = None
    for j in range(pixels.shape[1] // step):
        lanes = pl.ds(j * step, step)
        value = jnp.exp(scores[:, lanes] - top)
        for k in range(step // 128):
            total = total + value[:, 128 * k : 128 * k + 128]
        value = nt(value.astype(half), pixels[:, lanes])
        mix = value if mix is None else mix + value
    total = jnp.sum(total, axis=-1, keepdims=True)
    lane = lax.broadcasted_iota(jnp.int32, mix.shape, 1)
    sent[...] = jnp.where(lane == feats, top, jnp.where(lane == feats + 1, total, mix))
    wait_all(late)


def attend(spot, gathered, normed, pixels, keep, scale, feats):
    blocks, layout = gathered
    rows, width = 2 * normed[0].shape[0], normed[0].shape[1]
    lanes = width // 2 + main
    return pl.pallas_call(
        functools.partial(attend_kernel, len(blocks), layout, scale, feats),
        out_shape=[shape((rows, width), half), shape((rows, main + rest), half), shape((rows, main + rest), single)],
        in_specs=[scalars] + [remote] * (len(blocks) + 3) + [whole],
        out_specs=[remote, whole, whole],
        scratch_shapes=[
            pltpu.VMEM((2, width, lanes), half),
            pltpu.VMEM((2, rows // 2, width), half),
            pltpu.VMEM(pixels.shape, half),
            pltpu.VMEM((rows, width), half),
            pltpu.VMEM((rows, pixels.shape[1]), single),
            pltpu.SemaphoreType.DMA((32,)),
            pltpu.SemaphoreType.DMA((3,)),
        ],
        compiler_params=params_all,
        cost_estimate=cost(11),
        name="attend",
    )(spot, *blocks, *normed, pixels, keep)


def chain_kernel(count, layout, terms_count, feats, spot, *refs):
    blocks, refs = refs[:count], refs[count:]
    mine, theirs, latent_mine, latent_theirs, cot_mine, cot_theirs, vectors, *refs = refs
    latents_out, middle_grad, grad_pix, stats, sums, *refs = refs
    term_outs, refs = refs[:terms_count], refs[terms_count:]
    near, far, latents_in, cot_in, mixes, *refs = refs
    attended, middle_half, mixed, hidden_grad, active, out_half, attended_grad, value_mix, *refs = refs
    wide, out_wide, grad_wide, scratch, terms, sems, store_sems, more = refs
    rows_all, width = attended.shape
    step = rows_all // 2
    part = width // 2
    ready = copy_all([(mine, mixes.at[0]), (theirs, mixes.at[1])], more)
    ready += load_blocks(spot, blocks, layout, near, part + main, sems)
    ready_latents = copy_all([(latent_mine, latents_in.at[0]), (latent_theirs, latents_in.at[1])], more, 2)
    matrices = ((near, main), (far, 0), (far, part))
    leaving = []
    pair = range(2)
    rows = [pl.ds(t * step, step) for t in pair]

    def into(value, m):
        source, start = matrices[m]
        lanes = pl.ds(start, part)
        return nt(value[:, :part], source[0, :, lanes]) + nt(value[:, part:], source[1, :, lanes])

    def back(value, m, target):
        source, start = matrices[m]
        lanes = pl.ds(start, part)
        target[:, pl.ds(0, part)] = nn(value, source[0, :, lanes])
        target[:, pl.ds(part, part)] = nn(value, source[1, :, lanes])

    side = pl.ds(pl.multiple_of(spot[1] * part, part), part)

    def term(m, grad, value):
        terms[:, pl.ds(m * part, part)] = tn(grad[...], value[:, side]).astype(half)
        return store_terms(spot, terms, term_outs, m * part, part, store_sems, 16 * m)

    sums[...] = jnp.zeros_like(sums)
    value_mix[...] = jnp.zeros_like(value_mix)
    wait_all(ready)
    ready_far = load_blocks(spot, blocks, layout, far, 2 * part + 2 * main, sems, 32)
    ready_far += copy_all([(cot_mine, cot_in.at[0]), (cot_theirs, cot_in.at[1])], more, 4)
    tops, totals, attended_f, middles, units, inverses, hiddens, curves = [[None, None] for _ in range(8)]
    for t in pair:
        here, there = mixes[0, rows[t], :], mixes[1, rows[1 - t], :]
        top_here, top_there = here[:, feats : feats + 1], there[:, feats : feats + 1]
        top = jnp.maximum(top_here, top_there)
        scale_here, scale_there = jnp.exp(top_here - top), jnp.exp(top_there - top)
        total = here[:, feats + 1 : feats + 2] * scale_here + there[:, feats + 1 : feats + 2] * scale_there
        mix = (here * scale_here + there * scale_there) / total
        lane = lax.broadcasted_iota(jnp.int32, mix.shape, 1)
        value_mix[rows[t], pl.ds(0, main + rest)] = jnp.where(lane < feats, mix, 0.0).astype(half)
        tops[t], totals[t] = top, total
    for t in pair:
        value = nt(value_mix[rows[t], pl.ds(0, main)], near[0, :, pl.ds(0, main)])
        value = value + nt(value_mix[rows[t], pl.ds(main, rest)], near[1, :, pl.ds(0, rest)])
        wide[t] = value
        attended[rows[t], :] = value.astype(half)
    wait_all(ready_latents)
    for t in pair:
        middles[t] = latents_in[t] + into(attended[rows[t], :], 0)
    for t in pair:
        units[t], inverses[t] = standard(middles[t])
        mixed[rows[t], :] = (units[t] * vectors[2:3, :] + vectors[3:4, :]).astype(half)
    wait_all(ready_far)
    for t in pair:
        value = cot_in[t].astype(half)
        out_half[rows[t], :] = value
        if t == 0:
            sums[5:6, :] = jnp.sum(value.astype(single), axis=0, keepdims=True)
    for t in pair:
        hiddens[t] = into(mixed[rows[t], :], 1) + vectors[4:5, :]
    for t in pair:
        back(out_half[rows[t], :], 2, scratch.at[t])
        hidden = hiddens[t]
        curve = jnp.tanh(gelu_coeff * (hidden + 0.044715 * hidden * hidden * hidden))
        active[rows[t], :] = (0.5 * hidden * (1.0 + curve)).astype(half)
        curves[t] = curve
    leaving += term(2, out_half, active)
    out_wide[...] = middles[0] + into(active[rows[0], :], 2) + vectors[5:6, :]
    leaving += copy_all([(out_wide, latents_out)], more)
    for t in pair:
        hidden, curve = hiddens[t], curves[t]
        slope = 0.5 * (1.0 + curve) + 0.5 * hidden * (1.0 - curve * curve) * gelu_coeff * (
            1.0 + 3.0 * 0.044715 * hidden * hidden
        )
        value = (scratch[t] * slope).astype(half)
        hidden_grad[rows[t], :] = value
        if t == 0:
            sums[4:5, :] = jnp.sum(value.astype(single), axis=0, keepdims=True)
    for t in pair:
        back(hidden_grad[rows[t], :], 1, scratch.at[t])
    leaving += term(1, hidden_grad, mixed)
    for t in pair:
        mixed_grad = scratch[t]
        if t == 0:
            sums[2:3, :] = jnp.sum(mixed_grad * units[t], axis=0, keepdims=True)
            sums[3:4, :] = jnp.sum(mixed_grad, axis=0, keepdims=True)
        grad = cot_in[t] + standard_back(mixed_grad, vectors[2:3, :], units[t], inverses[t])
        if t == 0:
            grad_wide[...] = grad
            leaving += copy_all([(grad_wide, middle_grad)], more, 1)
        middle_half[rows[t], :] = grad.astype(half)
    for t in pair:
        back(middle_half[rows[t], :], 0, scratch.at[t])
    leaving += term(0, middle_half, attended)
    for t in pair:
        value = scratch[t].astype(half)
        attended_grad[rows[t], :] = value
        inner = jnp.sum(wide[t] * value.astype(single), axis=-1, keepdims=True)
        lane = lax.broadcasted_iota(jnp.int32, (step, 128), 1)
        stats[rows[t], :] = jnp.where(lane == 0, tops[t] + jnp.log(totals[t]), inner)
    for t in pair:
        value = attended_grad[rows[t], :]
        grad_pix[rows[t], pl.ds(0, main)] = nn(value, near[0, :, pl.ds(0, main)]).astype(half)
        grad_pix[rows[t], pl.ds(main, rest)] = nn(value, near[1, :, pl.ds(0, rest)]).astype(half)
    side = pl.ds(pl.multiple_of(spot[1] * main, main), main)
    terms[:, pl.ds(3 * part, main)] = tn(attended_grad[...], value_mix[:, side]).astype(half)
    leaving += store_terms(spot, terms, term_outs, 3 * part, main, store_sems, 48)
    wait_all(leaving)


def chain(spot, gathered, mine, theirs, latents, cotangents, vectors, feats, groups):
    blocks, layout = gathered
    rows, width = mine.shape[0], vectors.shape[1]
    part = width // 2
    lanes = 3 * part + main
    outs = term_shapes(groups, width // groups, lanes)
    bits = pltpu.VMEM((rows, width), half)
    result = pl.pallas_call(
        functools.partial(chain_kernel, len(blocks), layout, len(outs), feats),
        out_shape=[
            shape((rows // 2, width), single),
            shape((rows // 2, width), single),
            shape((rows, main + rest), half),
            shape((rows, 128), single),
            shape((8, width), single),
        ]
        + outs,
        in_specs=[scalars] + [remote] * (len(blocks) + 6) + [whole],
        out_specs=[remote] * 2 + [whole] * 3 + [remote] * len(outs),
        scratch_shapes=[
            pltpu.VMEM((2, width, part + main), half),
            pltpu.VMEM((2, width, 2 * part), half),
            pltpu.VMEM((2, rows // 2, width), single),
            pltpu.VMEM((2, rows // 2, width), single),
            pltpu.VMEM((2, rows, main + rest), single),
        ]
        + [bits] * 7
        + [pltpu.VMEM((rows, 2 * main), half)]
        + [pltpu.VMEM((2, rows // 2, width), single)]
        + [pltpu.VMEM((rows // 2, width), single)] * 2
        + [pltpu.VMEM((2, rows // 2, width), single)]
        + [pltpu.VMEM((width, lanes), half)]
        + [pltpu.SemaphoreType.DMA((64,)), pltpu.SemaphoreType.DMA((64,)), pltpu.SemaphoreType.DMA((6,))],
        compiler_params=params_all,
        cost_estimate=cost(17),
        name="chain",
    )(spot, *blocks, mine, theirs, *latents, *cotangents, vectors)
    return result[:5], result[5:]


def pixel_back_kernel(scale, turn, turns, *refs):
    (query_pix, grad_pix, stats, values_in, keep, pixels, gain, pixel_stats), refs = refs[:8], refs[8:]
    if turn > 0:
        (score_before, sums_before, _), refs = refs[:3], refs[3:]
    score_pix, sums, pixels_grad, values, held, made, score_grads, query_t, grad_t, slope, shift, sems = refs
    feats, count = held.shape
    over = feats - main
    some = main + 16
    step = 512
    origin = turn * count
    here = pl.ds(origin, count)
    early = copy_all([(values_in.at[:, here], values)], sems)
    late = copy_all([(pixels.at[:, 0, here], held)], sems, 1)
    query_t[...] = jnp.transpose(query_pix[...].astype(single))[:some].astype(half)
    grad_t[...] = jnp.transpose(grad_pix[...].astype(single))[:some].astype(half)
    slope[...] = jnp.zeros_like(slope)
    shift[...] = jnp.zeros_like(shift)
    log_total, inner = stats[:, 0:1], stats[:, 1:2]
    leaving = []
    wait_all(early)

    def products(i):
        lanes = pl.ds(i * step, step)
        return nn(query_pix[...], values[:, lanes]), nn(grad_pix[...], values[:, lanes])

    def norm_back(i, grad):
        lanes, there = pl.ds(i * step, step), pl.ds(origin + i * step, step)
        mean, inverse = pixel_stats[0:1, there], pixel_stats[1:2, there]
        unit_a = (held[pl.ds(0, main), lanes] - mean) * inverse
        unit_b = (held[pl.ds(main, over), lanes] - mean) * inverse
        grad_a, grad_b = grad[:main], grad[main : main + over]
        for rows, g, u in ((pl.ds(0, main), grad_a, unit_a), (pl.ds(main, over), grad_b, unit_b)):
            product = g * u
            slope[rows, :] += sum(product[:, 128 * j : 128 * j + 128] for j in range(step // 128))
            shift[rows, :] += sum(g[:, 128 * j : 128 * j + 128] for j in range(step // 128))
        scaled_a, scaled_b = grad_a * gain[pl.ds(0, main)], grad_b * gain[pl.ds(main, over)]
        flat = (jnp.sum(scaled_a, axis=0, keepdims=True) + jnp.sum(scaled_b, axis=0, keepdims=True)) / feats
        along = (
            jnp.sum(scaled_a * unit_a, axis=0, keepdims=True) + jnp.sum(scaled_b * unit_b, axis=0, keepdims=True)
        ) / feats
        made[pl.ds(0, main), lanes] = inverse * (scaled_a - flat - unit_a * along)
        made[pl.ds(main, over), lanes] = inverse * (scaled_b - flat - unit_b * along)
        return copy_all([(made.at[:, lanes], pixels_grad.at[:, 0, there])], sems, 2 + i)

    now, before = products(0), None
    for i in range(count // step):
        scores, weight_grad = now
        if (i + 1) * step < count:
            now = products(i + 1)
        lanes = pl.ds(i * step, step)
        kept = keep[:, pl.ds(origin + i * step, step)] > 0
        attn = jnp.exp(jnp.where(kept, scores, masked_score) - log_total)
        score_grad = (attn * (weight_grad - inner)).astype(half)
        score_grads[:, lanes] = score_grad
        grad = nn(query_t[...], score_grad) + nn(grad_t[...], attn.astype(half))
        if i == 0:
            wait_all(late)
        else:
            leaving += norm_back(i - 1, before)
        before = grad
    leaving += norm_back(count // step - 1, before)
    value = nt(score_grads[...], values[...])
    if turn > 0:
        value = value + score_before[...]
    score_pix[...] = value * scale if turn == turns - 1 else value
    lane = lax.broadcasted_iota(jnp.int32, (feats, 128), 1)
    both = jnp.where(
        lane == 0,
        jnp.sum(slope[...], axis=-1, keepdims=True),
        jnp.sum(shift[...], axis=-1, keepdims=True),
    )
    sums[...] = both + sums_before[...] if turn > 0 else both
    wait_all(leaving)


def pixel_back(query_pix, grad_pix, stats, normed, keep, pixels, gain, pixel_stats, scale, turn, turns, before):
    feats, _, count = pixels.shape
    rows = query_pix.shape[0]
    held = pltpu.VMEM((feats, count // turns), single)
    return pl.pallas_call(
        functools.partial(pixel_back_kernel, scale, turn, turns),
        out_shape=[shape((rows, main + rest), single), shape((feats, 128), single), shape(pixels.shape, single)],
        in_specs=[whole] * 3 + [remote, whole, remote, whole, whole] + [whole, whole, remote][: len(before)],
        out_specs=[whole, whole, remote],
        scratch_shapes=[
            pltpu.VMEM((main + rest, count // turns), half),
            held,
            held,
            pltpu.VMEM((rows, count // turns), half),
            pltpu.VMEM((main + 16, rows), half),
            pltpu.VMEM((main + 16, rows), half),
            pltpu.VMEM((feats, 128), single),
            pltpu.VMEM((feats, 128), single),
            pltpu.SemaphoreType.DMA((2 + count // turns // 512,)),
        ],
        input_output_aliases={10: 2} if before else {},
        compiler_params=params,
        cost_estimate=cost(18 / turns),
        name="pixel_back",
    )(query_pix, grad_pix, stats, normed, keep, pixels, gain, pixel_stats, *before)


def query_back_kernel(count, layout, terms_count, spot, *refs):
    blocks, refs = refs[:count], refs[count:]
    mine, theirs, query_in, normed_mine, normed_theirs, latents_in, grad_in, vectors, *refs = refs
    latents_grad, sums, *refs = refs
    term_outs, refs = refs[:terms_count], refs[terms_count:]
    weights, score_pix, query, normed, latents, middle_grad, query_grad, wide, terms, sems, store_sems, more = refs
    ready = load_blocks(spot, blocks, layout, weights, 0, sems)
    rows_all, width = query.shape
    step = rows_all // 2
    part = width // 2
    score_pix[:, pl.ds(main + rest, rest)] = jnp.zeros((rows_all, rest), half)
    for t in range(2):
        rows, other = pl.ds(t * step, step), pl.ds((1 - t) * step, step)
        score_pix[rows, pl.ds(0, main + rest)] = (mine[rows, :] + theirs[other, :]).astype(half)
    wait_all(ready)
    later = copy_all([(normed_mine, normed.at[0]), (normed_theirs, normed.at[1]), (query_in, query)], more)
    last = copy_all([(latents_in, latents), (grad_in, middle_grad)], more, 3)
    value = nt(score_pix[:, pl.ds(0, main)], weights[0, :, pl.ds(part, main)])
    value = value + nt(score_pix[:, pl.ds(main, rest)], weights[1, :, pl.ds(part, rest)])
    query_grad[...] = value.astype(half)
    wait_all(later)
    side = pl.ds(pl.multiple_of(spot[1] * part, part), part)
    value = tn(query_grad[pl.ds(0, step), :], normed[0, :, side])
    terms[:, pl.ds(0, part)] = (value + tn(query_grad[pl.ds(step, step), :], normed[1, :, side])).astype(half)
    leaving = store_terms(spot, terms, term_outs, 0, part, store_sems, 0)
    side = pl.ds(pl.multiple_of(spot[1] * main, main), main)
    terms[:, pl.ds(part, main)] = tn(query[...], score_pix[:, side]).astype(half)
    leaving += store_terms(spot, terms, term_outs, part, main, store_sems, 16)
    value = query_grad[pl.ds(0, step), :]
    wide[:, pl.ds(0, part)] = nn(value, weights[0, :, pl.ds(0, part)])
    wide[:, pl.ds(part, part)] = nn(value, weights[1, :, pl.ds(0, part)])
    wait_all(last)
    unit, inverse = standard(latents[...])
    grad = wide[...]
    latents_grad[...] = middle_grad[...] + standard_back(grad, vectors[0:1, :], unit, inverse)
    sums[...] = jnp.zeros_like(sums)
    sums[0:1, :] = jnp.sum(grad * unit, axis=0, keepdims=True)
    sums[1:2, :] = jnp.sum(grad, axis=0, keepdims=True)
    wait_all(leaving)


def query_back(spot, gathered, mine, theirs, query, normed, latents, middle_grad, vectors, groups):
    blocks, layout = gathered
    rows, width = query.shape
    lanes = width // 2 + main
    outs = term_shapes(groups, width // groups, lanes)
    one = pltpu.VMEM((rows // 2, width), single)
    result = pl.pallas_call(
        functools.partial(query_back_kernel, len(blocks), layout, len(outs)),
        out_shape=[shape((rows // 2, width), single), shape((8, width), single)] + outs,
        in_specs=[scalars] + [remote] * len(blocks) + [whole] * 2 + [remote] * 5 + [whole],
        out_specs=[whole] * 2 + [remote] * len(outs),
        scratch_shapes=[
            pltpu.VMEM((2, width, lanes), half),
            pltpu.VMEM((rows, 2 * main), half),
            pltpu.VMEM((rows, width), half),
            pltpu.VMEM((2, rows // 2, width), half),
            one,
            one,
            pltpu.VMEM((rows, width), half),
            one,
            pltpu.VMEM((width, lanes), half),
            pltpu.SemaphoreType.DMA((32,)),
            pltpu.SemaphoreType.DMA((32,)),
            pltpu.SemaphoreType.DMA((5,)),
        ],
        compiler_params=params_all,
        cost_estimate=cost(7),
        name="query_back",
    )(spot, *blocks, mine, theirs, query, *normed, latents, middle_grad, vectors)
    return result[:2], result[2:]


def moments_kernel(feats, *refs):
    spot, late_mine, late_theirs, early_mine, early_theirs, vectors, *refs = refs
    square_p, square_m, square_v, pixel_p, pixel_m, pixel_v, *refs = refs
    square_outs, pixel_outs, sums = refs[:4], refs[4:8], refs[8]
    width = square_p.shape[2]
    part = width // 2
    first = spot[1] == 0
    lane = lax.broadcasted_iota(jnp.int32, (1, width), 1)
    row = jnp.zeros((1, width), single)
    for m in range(6):
        mine, theirs = (late_mine, late_theirs) if m in (0, 4) else (early_mine, early_theirs)
        if m < 4:
            lanes = pl.ds(max(m - 1, 0) * part, part)
            sides, outs, k = (pl.ds(0, part), pl.ds(part, part)), square_outs, m
            params_now, first_now, second_now = square_p, square_m, square_v
        else:
            lanes = pl.ds(part if m == 4 else 3 * part, main)
            sides, outs, k = (pl.ds(0, main), pl.ds(main, feats - main)), pixel_outs, m - 4
            params_now, first_now, second_now = pixel_p, pixel_m, pixel_v
        own, other = mine[:, lanes], theirs[:, lanes]
        weight_total, update_total = jnp.zeros((1, 1), single), jnp.zeros((1, 1), single)
        for side, grad in zip(sides, (jnp.where(first, own, other), jnp.where(first, other, own))):
            grad = grad[:, : side.size]
            weight = params_now[k, :, side]
            first_new, second_new, ratio = adam_moments(grad, first_now[k, :, side], second_now[k, :, side])
            update = ratio + decay_rate * weight
            for out, value in zip(outs, (grad, first_new, second_new, update)):
                out[k, :, side] = value
            weight_total = weight_total + jnp.sum(weight * weight, keepdims=True)
            update_total = update_total + jnp.sum(update * update, keepdims=True)
        row = row + jnp.where(lane == m, weight_total, jnp.where(lane == 6 + m, update_total, 0.0))
    sums[...] = jnp.zeros_like(sums)
    sums[pl.ds(0, 8), :] = vectors[...]
    sums[8:9, :] = row


def moments(spot, late, early, vectors, square, pixel):
    big, small = shape(square[0].shape, single), shape(pixel[0].shape, single)
    return pl.pallas_call(
        functools.partial(moments_kernel, pixel[0].shape[2]),
        out_shape=[big] * 4 + [small] * 4 + [shape((16, big.shape[2]), single)],
        in_specs=[scalars] + [whole] * 11,
        out_specs=[whole] * 9,
        compiler_params=params,
        cost_estimate=cost(5),
        name="moments",
    )(spot, *late, *early, vectors, *square, *pixel)


def apply_kernel(sums, square_p, square_u, pixel_p, pixel_u, *refs):
    states, outs = refs[:6], refs[6:]
    square_new, square_copy, pixel_new, pixel_copy, norms, *news = outs
    weight_norm, update_norm = jnp.sqrt(sums[8:9, 0:6]), jnp.sqrt(sums[8:9, 6:12])
    trust = weight_norm / (update_norm + epsilon)
    for row, value in enumerate((weight_norm, update_norm, trust)):
        norms[row : row + 1, :] = value
    for m in range(6):
        k, weight, update, new, copy = (
            (m, square_p, square_u, square_new, square_copy)
            if m < 4
            else (m - 4, pixel_p, pixel_u, pixel_new, pixel_copy)
        )
        value = weight[k] - learn_rate * trust[:, m : m + 1] * update[k]
        new[k] = value
        copy[k] = value.astype(half)
    feats = states[3].shape[1]
    for grad, (value, first, second), out in (
        (sums[0:6, :], states[:3], news[:3]),
        (sums[6:8, 0:feats], states[3:], news[3:]),
    ):
        first_new, second_new, ratio = adam_moments(grad, first[...], second[...])
        out[0][...] = value[...] - vector_rate * ratio
        out[1][...] = first_new
        out[2][...] = second_new


def apply(sums, square_p, square_u, pixel_p, pixel_u, vectors, norms):
    outs = [(square_p, single), (square_p, half), (pixel_p, single), (pixel_p, half)]
    states = [*vectors, *norms]
    return pl.pallas_call(
        apply_kernel,
        out_shape=[shape(a.shape, dtype) for a, dtype in outs]
        + [shape((3, 6), single)]
        + [shape(a.shape, single) for a in states],
        in_specs=[whole] * 11,
        out_specs=[whole] * 11,
        compiler_params=params,
        cost_estimate=cost(4),
        name="apply",
    )(sums, square_p, square_u, pixel_p, pixel_u, *states)


def local(
    latents,
    pixels,
    keep_mask,
    cotangent,
    square_weights,
    square_first,
    square_second,
    pixel_weights,
    pixel_first,
    pixel_second,
    latent_vectors,
    latent_first,
    latent_second,
    pixel_norm,
    pixel_norm_first,
    pixel_norm_second,
):
    width = latents.shape[2]
    feats = pixels.shape[2]
    scale = width ** (-0.5)
    rank = lax.axis_index("seq")
    groups = lax.axis_size("dp")
    spot = jnp.stack([lax.axis_index("dp"), rank]).astype(jnp.int32)

    def turned(array):
        return jnp.transpose(array, (0, 2, 1))

    square = [turned(array) for array in (square_weights, square_first, square_second)]
    pixel = [turned(array) for array in (pixel_weights, pixel_first, pixel_second)]

    latents_two = (latents[0], trade(latents[0]))
    cotangent_two = (cotangent[0], trade(cotangent[0]))
    pixels_t = jnp.transpose(pixels, (2, 0, 1))
    gain, shift = pixel_norm[0][:, None], pixel_norm[1][:, None]
    pixel_normed, pixel_stats = norm_pixels(pixels_t, gain, shift)
    normed = norm_latents(latents[0], latent_vectors)
    normed = (normed, trade(normed))
    blocks = gather_matrices(pack(spot, square[0], pixel[0]), pixel_normed, normed[0])
    query, query_pix, sent = attend(spot, blocks, normed, pixel_normed, keep_mask, scale, feats)
    (latents_out, middle_grad, grad_pix, stats, chain_sums), early_terms = chain(
        spot, blocks, sent, trade(sent), latents_two, cotangent_two, latent_vectors, feats, groups
    )
    pixel_args = (query_pix, grad_pix, stats, pixel_normed, keep_mask, pixels_t, gain, pixel_stats, scale)
    turn_one = pixel_back(*pixel_args, 0, 2, ())
    if len(early_terms) > 1:
        *early_got, score_pix = tie([*send_first(early_terms), turn_one[0]], turn_one[1])
        turn_two = pixel_back(*pixel_args, 1, 2, [score_pix, *turn_one[1:]])
        early_got = send_second(early_terms, early_got, turn_two[0])
    else:
        turn_two, early_got = pixel_back(*pixel_args, 1, 2, turn_one), None
    score_pix, pixel_sums, pixels_grad = turn_two
    (latents_grad, query_sums), late_terms = query_back(
        spot, blocks, score_pix, trade(score_pix), query, normed, latents[0], middle_grad, latent_vectors, groups
    )
    early_got = send_third(early_terms, early_got)
    if len(late_terms) > 1:
        tied = tie([*late_terms[:3], *early_got], late_terms[3])
        late_terms, early_got = [*tied[:3], *late_terms[3:]], tied[3:]
    early = sum_own(early_terms, early_got)
    late = sum_own(late_terms, send_third(late_terms, send_second(late_terms, send_first(late_terms))))

    norm_terms = jnp.pad(jnp.transpose(pixel_sums[:, :2]), ((6, 0), (0, width - feats)))
    vector_terms = chain_sums + query_sums + norm_terms
    vector_terms = vector_terms + trade(vector_terms)
    square_grad, square_first_new, square_second_new, square_u, *rest_outs = moments(
        spot, (late, trade(late)), (early, trade(early)), vector_terms, square, pixel
    )
    pixel_weight_grad, pixel_first_new, pixel_second_new, pixel_u, sums = rest_outs
    square_new, square_copy, pixel_new, pixel_copy, matrix_norms, *news = apply(
        sum_all(sums),
        square[0],
        square_u,
        pixel[0],
        pixel_u,
        (latent_vectors, latent_first, latent_second),
        (pixel_norm, pixel_norm_first, pixel_norm_second),
    )
    latent_vectors_new, latent_first_new, latent_second_new = news[:3]
    pixel_norm_new, pixel_norm_first_new, pixel_norm_second_new = news[3:]
    return (
        latents_out[None],
        latents_grad[None],
        jnp.transpose(pixels_grad, (1, 2, 0)),
        turned(square_grad),
        turned(square_first_new),
        turned(square_second_new),
        turned(square_new),
        turned(square_copy),
        turned(pixel_weight_grad),
        turned(pixel_first_new),
        turned(pixel_second_new),
        turned(pixel_new),
        turned(pixel_copy),
        latent_first_new,
        latent_second_new,
        latent_vectors_new,
        pixel_norm_first_new,
        pixel_norm_second_new,
        pixel_norm_new,
        matrix_norms,
    )


def solution(mesh):
    return jax.shard_map(
        local,
        mesh=mesh,
        in_specs=(
            P("dp", "seq", None),
            P("dp", "seq", None),
            P("dp", "seq"),
            P("dp", "seq", None),
            P(None, None, "dp"),
            P(None, None, "dp"),
            P(None, None, "dp"),
            P(None, None, "dp"),
            P(None, None, "dp"),
            P(None, None, "dp"),
            P(),
            P(),
            P(),
            P(),
            P(),
            P(),
        ),
        out_specs=(
            P("dp", "seq", None),
            P("dp", "seq", None),
            P("dp", "seq", None),
            P(None, None, "dp"),
            P(None, None, "dp"),
            P(None, None, "dp"),
            P(None, None, "dp"),
            P(None, None, "dp"),
            P(None, None, "dp"),
            P(None, None, "dp"),
            P(None, None, "dp"),
            P(None, None, "dp"),
            P(None, None, "dp"),
            P(),
            P(),
            P(),
            P(),
            P(),
            P(),
            P(),
        ),
        check_vma=False,
    )
```

```python
import functools

import jax
import jax.numpy as jnp
from jax import lax
from jax.experimental import pallas as pl
from jax.experimental.pallas import tpu as pltpu
from jax.sharding import PartitionSpec as P

STEP = 10


norm_epsilon = 1e-05
beta_one = 0.9
beta_two = 0.999
decay_rate = 0.01
epsilon = 1e-06
learn_rate = 0.25
vector_rate = 1.0
masked_score = -1e30
gelu_coeff = 0.7978845608028654


def adam_moments(grad, first, second):
    first_new = beta_one * first + (1.0 - beta_one) * grad
    second_new = beta_two * second + (1.0 - beta_two) * grad * grad
    ratio = (
        first_new
        / (1.0 - beta_one**STEP)
        / (jnp.sqrt(second_new / (1.0 - beta_two**STEP)) + epsilon)
    )
    return (first_new, second_new, ratio)

half = jnp.bfloat16
single = jnp.float32
swap = [(0, 1), (1, 0)]
main, rest = 256, 128
whole = pl.BlockSpec(memory_space=pltpu.VMEM)
remote = pl.BlockSpec(memory_space=pl.ANY)
scalars = pl.BlockSpec(memory_space=pltpu.SMEM)
params = pltpu.CompilerParams(vmem_limit_bytes=40 * 2**20)
params_most = pltpu.CompilerParams(vmem_limit_bytes=56 * 2**20)
params_all = pltpu.CompilerParams(vmem_limit_bytes=63 * 2**20)


def cost(micros):
    return pl.CostEstimate(flops=int(micros * 1.1e9), bytes_accessed=1024, transcendentals=0)


def shape(dims, dtype):
    return jax.ShapeDtypeStruct(dims, dtype)


def contract(left, right, over_left, over_right):
    return lax.dot_general(left, right, (((over_left,), (over_right,)), ((), ())), preferred_element_type=single)


def nn(left, right):
    return contract(left, right, 1, 0)


def nt(left, right):
    return contract(left, right, 1, 1)


def tn(left, right):
    return contract(left, right, 0, 0)


def flip(array, mask):
    return lax.ppermute(array, "dp", [(i, i ^ mask) for i in range(lax.axis_size("dp"))])


def trade(array):
    return lax.ppermute(array, "seq", swap)


def special(groups, shard):
    return groups == 16 and shard % 32 == 0


def tie_kernel(*refs):
    pass


def tie(arrays, *after):
    return pl.pallas_call(
        tie_kernel,
        out_shape=[shape(a.shape, a.dtype) for a in arrays],
        in_specs=[remote] * (len(arrays) + len(after)),
        out_specs=[remote] * len(arrays),
        input_output_aliases={i: i for i in range(len(arrays))},
        cost_estimate=cost(0.1),
        name="tie",
    )(*arrays, *after)


def stack_kernel(plan, *refs):
    outs = refs[len(refs) - len(plan) :]
    for out, parts in zip(outs, plan):
        rows = out.shape[0] // len(parts)
        for i, (source, part) in enumerate(parts):
            out[pl.ds(i * rows, rows), :] = refs[source][pl.ds(part * rows, rows), :]


def stack(arrays, rows, plan, *after):
    lanes, dtype = arrays[0].shape[1], arrays[0].dtype
    return pl.pallas_call(
        functools.partial(stack_kernel, plan),
        out_shape=[shape((rows * len(parts), lanes), dtype) for parts in plan],
        in_specs=[whole] * len(arrays) + [remote] * len(after),
        out_specs=[whole] * len(plan),
        compiler_params=params,
        cost_estimate=cost(1.5),
        name="stack",
    )(*arrays, *after)


def gather_blocks(block, early, late):
    rows = block.shape[0]
    one, two, four, three, eight = [flip(block, o) for o in (1, 2, 4, 3, 8)]
    across, both = stack([three, four, eight], rows, (((0, 0), (2, 0)), ((1, 0), (2, 0))), early)
    (gathered,) = stack([block, eight, four, three, two, one], rows, (tuple((i, 0) for i in range(6)),))
    second = [flip(across, 4), flip(both, 2), flip(both, 1)]
    seven, twelve, twelve_ten = stack(second[:2], rows, (((0, 0),), ((0, 1),), ((0, 1), (1, 1))), second[2], late)
    third = [flip(seven, 8), flip(twelve, 2), flip(twelve_ten, 1)]
    return [
        ((0, 8, 4, 3, 2, 1), gathered),
        ((7, 12), second[0]),
        ((6, 10), second[1]),
        ((5, 9), second[2]),
        ((15,), third[0]),
        ((14,), third[1]),
        ((13, 11), third[2]),
    ]


def pack_kernel(feats, spot, squares, pixels, block):
    side = spot[1]
    part = squares.shape[2] // 2
    lanes = pl.ds(pl.multiple_of(side * part, part), part)
    over = feats - main

    def pixel(m):
        last = pixels[m, :, pl.ds(main, over)]
        last = jnp.concatenate([last, jnp.zeros((last.shape[0], main - over), single)], axis=1)
        return jnp.where(side == 0, pixels[m, :, pl.ds(0, main)], last).astype(half)

    block[:, pl.ds(0, part)] = squares[0, :, lanes].astype(half)
    block[:, pl.ds(part, main)] = pixel(0)
    block[:, pl.ds(part + main, main)] = pixel(1)
    for m in range(1, 4):
        block[:, pl.ds(m * part + 2 * main, part)] = squares[m, :, lanes].astype(half)


def pack(spot, squares, pixels):
    _, shard, width = squares.shape
    return pl.pallas_call(
        functools.partial(pack_kernel, pixels.shape[2]),
        out_shape=shape((shard, 4 * (width // 2) + 2 * main), half),
        in_specs=[scalars, whole, whole],
        out_specs=whole,
        compiler_params=params,
        cost_estimate=cost(2),
        name="pack",
    )(spot, squares, pixels)


def gather_matrices(block, early, late):
    groups = lax.axis_size("dp")
    shard = block.shape[0]
    if special(groups, shard):
        arrays, layout = [], []
        for positions, array in gather_blocks(block, early, late):
            arrays += [array, trade(array)]
            layout += [(positions, 0), (positions, 1)]
        return arrays, tuple(layout)
    every = lax.all_gather(block, ("dp", "seq"), axis=0).reshape(groups, 2, shard, -1)
    return [every.transpose(1, 0, 2, 3).reshape(2, groups * shard, -1)], ()


def place_blocks(spot, blocks, layout, target, first):
    lanes = pl.ds(first, target.shape[2])
    if not layout:
        target[...] = blocks[0][:, :, lanes]
    for block, (positions, turn) in zip(blocks, layout):
        rows = block.shape[0] // len(positions)
        side = lax.bitwise_xor(spot[1], turn)
        for i, o in enumerate(positions):
            chip = lax.bitwise_xor(spot[0], o)
            place = pl.ds(pl.multiple_of(chip * rows, rows), rows)
            target[side, place, :] = block[pl.ds(i * rows, rows), lanes]


def copy_all(pairs, sems, first=0):
    copies = [pltpu.make_async_copy(source, target, sems.at[first + i]) for i, (source, target) in enumerate(pairs)]
    for copy in copies:
        copy.start()
    return copies


def wait_all(copies):
    for copy in copies:
        copy.wait()


def load_blocks(spot, blocks, layout, target, first, sems, base=0):
    pairs = []
    lanes = pl.ds(first, target.shape[2])
    if not layout:
        pairs.append((blocks[0].at[:, :, lanes], target))
    for block, (positions, turn) in zip(blocks, layout):
        rows = block.shape[0] // len(positions)
        side = lax.bitwise_xor(spot[1], turn)
        for i, o in enumerate(positions):
            chip = lax.bitwise_xor(spot[0], o)
            place = target.at[side, pl.ds(pl.multiple_of(chip * rows, rows), rows)]
            pairs.append((block.at[pl.ds(i * rows, rows), lanes], place))
    return copy_all(pairs, sems, base)


written = ((13, 11), (14,), (15,), (5, 9), (6, 10), (7, 12), (1,), (2,), (3,), (4,), (8,), (0,))


def store_terms(spot, terms, outs, start, count, sems, base):
    lanes = pl.ds(start, count)
    if len(outs) == 1:
        return copy_all([(terms.at[:, lanes], outs[0].at[:, lanes])], sems, base)
    pairs = []
    rows = terms.shape[0] // 16
    for positions, out in zip(written, outs):
        for i, o in enumerate(positions):
            chip = lax.bitwise_xor(spot[0], o)
            source = terms.at[pl.ds(pl.multiple_of(chip * rows, rows), rows), lanes]
            pairs.append((source, out.at[pl.ds(i * rows, rows), lanes]))
    return copy_all(pairs, sems, base)


def term_shapes(groups, shard, lanes):
    if special(groups, shard):
        return [shape((len(positions) * shard, lanes), half) for positions in written]
    return [shape((groups * shard, lanes), half)]


def send_first(terms, *after):
    if len(terms) == 1:
        return None
    got = [flip(terms[0], 1), flip(terms[1], 2), flip(terms[2], 8)]
    return tie(got, *after) if after else got


def send_second(terms, got, *after):
    if len(terms) == 1:
        return None
    rows = terms[-1].shape[0]

    def added(array, low, *high):
        total = array.astype(single)
        if low is not None:
            total = total + jnp.pad(low.astype(single), ((0, rows), (0, 0)))
        for other in high:
            total = total + jnp.pad(other.astype(single), ((rows, 0), (0, 0)))
        return total.astype(half)

    twelve, ten = got[0][:rows], got[0][rows:]
    got = [
        flip(terms[3], 1),
        flip(added(terms[4], None, ten), 2),
        flip(added(terms[5], got[2], twelve, got[1]), 4),
    ]
    return tie(got, *after) if after else got


def send_third(terms, got):
    if len(terms) == 1:
        return [lax.psum_scatter(terms[0], "dp", scatter_dimension=0, tiled=True)]
    rows = terms[-1].shape[0]
    one, two = terms[6:8]
    three, four, eight = [term.astype(single) for term in terms[8:11]]
    upper = [array[:rows].astype(single) for array in got]
    lower = [array[rows:].astype(single) for array in got]
    sent = [
        (one, 1),
        (two, 2),
        (four + upper[0] + upper[1], 4),
        (three + upper[2], 3),
        (eight + lower[0] + lower[1] + lower[2], 8),
    ]
    return [flip(array.astype(half), mask) for array, mask in sent]


def sum_own(terms, got):
    if len(terms) > 1:
        got = [terms[-1], *got]
    total = got[0].astype(single)
    for array in got[1:]:
        total = total + array.astype(single)
    return total


def sum_all(array):
    mask = 1
    size = lax.axis_size("dp")
    while mask < size:
        if mask * 2 < size:
            one, two, three = flip(array, mask), flip(array, 2 * mask), flip(array, 3 * mask)
            array = (array + one) + (two + three)
            mask *= 4
        else:
            array = array + flip(array, mask)
            mask *= 2
    return array


def standard(values):
    center = values - jnp.mean(values, axis=-1, keepdims=True)
    inverse = lax.rsqrt(jnp.mean(center * center, axis=-1, keepdims=True) + norm_epsilon)
    return center * inverse, inverse


def standard_back(grad, gain, unit, inverse):
    scaled = grad * gain
    return inverse * (
        scaled - jnp.mean(scaled, axis=-1, keepdims=True) - unit * jnp.mean(scaled * unit, axis=-1, keepdims=True)
    )


def pixel_kernel(pixels, gain, shift, normed, stats, held, tail, sem):
    copy = pltpu.make_async_copy(pixels.at[:, 0, :], held, sem)
    copy.start()
    feats = held.shape[0]
    step = 256
    over = feats - main
    tail[...] = jnp.zeros_like(tail)
    copy.wait()

    @pl.loop(0, held.shape[1] // step)
    def _(i):
        lanes = pl.ds(pl.multiple_of(i * step, step), step)
        first, last = held[pl.ds(0, main), lanes], held[pl.ds(main, over), lanes]
        mean = (jnp.sum(first, axis=0, keepdims=True) + jnp.sum(last, axis=0, keepdims=True)) / feats
        first, last = first - mean, last - mean
        spread = (
            jnp.sum(first * first, axis=0, keepdims=True) + jnp.sum(last * last, axis=0, keepdims=True)
        ) / feats
        inverse = lax.rsqrt(spread + norm_epsilon)
        normed[pl.ds(0, main), lanes] = (first * inverse * gain[pl.ds(0, main)] + shift[pl.ds(0, main)]).astype(half)
        tail[pl.ds(0, over), :] = last * inverse * gain[pl.ds(main, over)] + shift[pl.ds(main, over)]
        normed[pl.ds(main, rest), lanes] = tail[...].astype(half)
        stats[0:1, lanes] = mean
        stats[1:2, lanes] = inverse


def norm_pixels(pixels, gain, shift):
    feats, _, count = pixels.shape
    return pl.pallas_call(
        pixel_kernel,
        out_shape=[shape((main + rest, count), half), shape((2, count), single)],
        in_specs=[remote, whole, whole],
        out_specs=[whole] * 2,
        scratch_shapes=[pltpu.VMEM((feats, count), single), pltpu.VMEM((rest, 256), single), pltpu.SemaphoreType.DMA],
        compiler_params=params,
        cost_estimate=cost(7),
        name="norm_pixels",
    )(pixels, gain, shift)


def latent_kernel(latents, vectors, normed):
    unit, _ = standard(latents[...])
    normed[...] = (unit * vectors[0:1, :] + vectors[1:2, :]).astype(half)


def norm_latents(latents, vectors):
    return pl.pallas_call(
        latent_kernel,
        out_shape=shape(latents.shape, half),
        in_specs=[whole] * 2,
        out_specs=whole,
        compiler_params=params,
        cost_estimate=cost(2),
        name="norm_latents",
    )(latents, vectors)


def attend_kernel(count, layout, scale, feats, spot, *refs):
    blocks = refs[:count]
    mine, theirs, pixels_in, keep, query_out, query_pix, sent, *refs = refs[count:]
    weights, normed, pixels, query, scores, more = refs
    copies = copy_all([(mine, normed.at[0]), (theirs, normed.at[1])], more)
    late = copy_all([(pixels_in, pixels)], more, 2)
    place_blocks(spot, blocks, layout, weights, 0)
    wait_all(copies)
    step, part = mine.shape[0], mine.shape[1] // 2
    for t in range(2):
        rows = pl.ds(t * step, step)
        value = nt(normed[t, :, pl.ds(0, part)], weights[0, :, pl.ds(0, part)])
        value = value + nt(normed[t, :, pl.ds(part, part)], weights[1, :, pl.ds(0, part)])
        value = value.astype(half)
        query[rows, :] = value
        query_pix[rows, pl.ds(0, main)] = (nn(value, weights[0, :, pl.ds(part, main)]) * scale).astype(half)
        query_pix[rows, pl.ds(main, rest)] = (nn(value, weights[1, :, pl.ds(part, rest)]) * scale).astype(half)
    wait_all(late)
    late = copy_all([(query, query_out)], more, 2)
    step = 512
    peak = None
    for j in range(pixels.shape[1] // step):
        lanes = pl.ds(j * step, step)
        value = nn(query_pix[...], pixels[:, lanes])
        value = jnp.where(keep[:, lanes] > 0, value, masked_score)
        scores[:, lanes] = value
        for k in range(step // 128):
            some = value[:, 128 * k : 128 * k + 128]
            peak = some if peak is None else jnp.maximum(peak, some)
    top = jnp.max(peak, axis=-1, keepdims=True)
    total = jnp.zeros_like(peak)
    mix = None
    for j in range(pixels.shape[1] // step):
        lanes = pl.ds(j * step, step)
        value = jnp.exp(scores[:, lanes] - top)
        for k in range(step // 128):
            total = total + value[:, 128 * k : 128 * k + 128]
        value = nt(value.astype(half), pixels[:, lanes])
        mix = value if mix is None else mix + value
    total = jnp.sum(total, axis=-1, keepdims=True)
    lane = lax.broadcasted_iota(jnp.int32, mix.shape, 1)
    sent[...] = jnp.where(lane == feats, top, jnp.where(lane == feats + 1, total, mix))
    wait_all(late)


def attend(spot, gathered, normed, pixels, keep, scale, feats):
    blocks, layout = gathered
    rows, width = 2 * normed[0].shape[0], normed[0].shape[1]
    lanes = width // 2 + main
    return pl.pallas_call(
        functools.partial(attend_kernel, len(blocks), layout, scale, feats),
        out_shape=[shape((rows, width), half), shape((rows, main + rest), half), shape((rows, main + rest), single)],
        in_specs=[scalars] + [whole] * len(blocks) + [remote] * 3 + [whole],
        out_specs=[remote, whole, whole],
        scratch_shapes=[
            pltpu.VMEM((2, width, lanes), half),
            pltpu.VMEM((2, rows // 2, width), half),
            pltpu.VMEM(pixels.shape, half),
            pltpu.VMEM((rows, width), half),
            pltpu.VMEM((rows, pixels.shape[1]), single),
            pltpu.SemaphoreType.DMA((3,)),
        ],
        compiler_params=params,
        cost_estimate=cost(11),
        name="attend",
    )(spot, *blocks, *normed, pixels, keep)


def chain_kernel(count, layout, terms_count, feats, spot, *refs):
    blocks, refs = refs[:count], refs[count:]
    mine, theirs, latent_mine, latent_theirs, cot_mine, cot_theirs, vectors, *refs = refs
    latents_out, middle_grad, grad_pix, stats, sums, *refs = refs
    term_outs, refs = refs[:terms_count], refs[terms_count:]
    near, far, latents_in, cot_in, mixes, *refs = refs
    attended, middle_half, mixed, hidden_grad, active, out_half, attended_grad, value_mix, *refs = refs
    wide, out_wide, grad_wide, scratch, terms, sems, store_sems, more = refs
    rows_all, width = attended.shape
    step = rows_all // 2
    part = width // 2
    ready = copy_all([(mine, mixes.at[0]), (theirs, mixes.at[1])], more)
    ready += load_blocks(spot, blocks, layout, near, part + main, sems)
    ready_latents = copy_all([(latent_mine, latents_in.at[0]), (latent_theirs, latents_in.at[1])], more, 2)
    matrices = ((near, main), (far, 0), (far, part))
    leaving = []
    pair = range(2)
    rows = [pl.ds(t * step, step) for t in pair]

    def into(value, m):
        source, start = matrices[m]
        lanes = pl.ds(start, part)
        return nt(value[:, :part], source[0, :, lanes]) + nt(value[:, part:], source[1, :, lanes])

    def back(value, m, target):
        source, start = matrices[m]
        lanes = pl.ds(start, part)
        target[:, pl.ds(0, part)] = nn(value, source[0, :, lanes])
        target[:, pl.ds(part, part)] = nn(value, source[1, :, lanes])

    side = pl.ds(pl.multiple_of(spot[1] * part, part), part)

    def term(m, grad, value):
        terms[:, pl.ds(m * part, part)] = tn(grad[...], value[:, side]).astype(half)
        return store_terms(spot, terms, term_outs, m * part, part, store_sems, 16 * m)

    sums[...] = jnp.zeros_like(sums)
    value_mix[...] = jnp.zeros_like(value_mix)
    wait_all(ready)
    ready_far = load_blocks(spot, blocks, layout, far, 2 * part + 2 * main, sems, 32)
    ready_far += copy_all([(cot_mine, cot_in.at[0]), (cot_theirs, cot_in.at[1])], more, 4)
    tops, totals, attended_f, middles, units, inverses, hiddens, curves = [[None, None] for _ in range(8)]
    for t in pair:
        here, there = mixes[0, rows[t], :], mixes[1, rows[1 - t], :]
        top_here, top_there = here[:, feats : feats + 1], there[:, feats : feats + 1]
        top = jnp.maximum(top_here, top_there)
        scale_here, scale_there = jnp.exp(top_here - top), jnp.exp(top_there - top)
        total = here[:, feats + 1 : feats + 2] * scale_here + there[:, feats + 1 : feats + 2] * scale_there
        mix = (here * scale_here + there * scale_there) / total
        lane = lax.broadcasted_iota(jnp.int32, mix.shape, 1)
        value_mix[rows[t], pl.ds(0, main + rest)] = jnp.where(lane < feats, mix, 0.0).astype(half)
        tops[t], totals[t] = top, total
    for t in pair:
        value = nt(value_mix[rows[t], pl.ds(0, main)], near[0, :, pl.ds(0, main)])
        value = value + nt(value_mix[rows[t], pl.ds(main, rest)], near[1, :, pl.ds(0, rest)])
        wide[t] = value
        attended[rows[t], :] = value.astype(half)
    wait_all(ready_latents)
    for t in pair:
        middles[t] = latents_in[t] + into(attended[rows[t], :], 0)
    for t in pair:
        units[t], inverses[t] = standard(middles[t])
        mixed[rows[t], :] = (units[t] * vectors[2:3, :] + vectors[3:4, :]).astype(half)
    wait_all(ready_far)
    for t in pair:
        value = cot_in[t].astype(half)
        out_half[rows[t], :] = value
        if t == 0:
            sums[5:6, :] = jnp.sum(value.astype(single), axis=0, keepdims=True)
    for t in pair:
        hiddens[t] = into(mixed[rows[t], :], 1) + vectors[4:5, :]
    for t in pair:
        back(out_half[rows[t], :], 2, scratch.at[t])
        hidden = hiddens[t]
        curve = jnp.tanh(gelu_coeff * (hidden + 0.044715 * hidden * hidden * hidden))
        active[rows[t], :] = (0.5 * hidden * (1.0 + curve)).astype(half)
        curves[t] = curve
    leaving += term(2, out_half, active)
    out_wide[...] = middles[0] + into(active[rows[0], :], 2) + vectors[5:6, :]
    leaving += copy_all([(out_wide, latents_out)], more)
    for t in pair:
        hidden, curve = hiddens[t], curves[t]
        slope = 0.5 * (1.0 + curve) + 0.5 * hidden * (1.0 - curve * curve) * gelu_coeff * (
            1.0 + 3.0 * 0.044715 * hidden * hidden
        )
        value = (scratch[t] * slope).astype(half)
        hidden_grad[rows[t], :] = value
        if t == 0:
            sums[4:5, :] = jnp.sum(value.astype(single), axis=0, keepdims=True)
    for t in pair:
        back(hidden_grad[rows[t], :], 1, scratch.at[t])
    leaving += term(1, hidden_grad, mixed)
    for t in pair:
        mixed_grad = scratch[t]
        if t == 0:
            sums[2:3, :] = jnp.sum(mixed_grad * units[t], axis=0, keepdims=True)
            sums[3:4, :] = jnp.sum(mixed_grad, axis=0, keepdims=True)
        grad = cot_in[t] + standard_back(mixed_grad, vectors[2:3, :], units[t], inverses[t])
        if t == 0:
            grad_wide[...] = grad
            leaving += copy_all([(grad_wide, middle_grad)], more, 1)
        middle_half[rows[t], :] = grad.astype(half)
    for t in pair:
        back(middle_half[rows[t], :], 0, scratch.at[t])
    leaving += term(0, middle_half, attended)
    for t in pair:
        value = scratch[t].astype(half)
        attended_grad[rows[t], :] = value
        inner = jnp.sum(wide[t] * value.astype(single), axis=-1, keepdims=True)
        lane = lax.broadcasted_iota(jnp.int32, (step, 128), 1)
        stats[rows[t], :] = jnp.where(lane == 0, tops[t] + jnp.log(totals[t]), inner)
    for t in pair:
        value = attended_grad[rows[t], :]
        grad_pix[rows[t], pl.ds(0, main)] = nn(value, near[0, :, pl.ds(0, main)]).astype(half)
        grad_pix[rows[t], pl.ds(main, rest)] = nn(value, near[1, :, pl.ds(0, rest)]).astype(half)
    side = pl.ds(pl.multiple_of(spot[1] * main, main), main)
    terms[:, pl.ds(3 * part, main)] = tn(attended_grad[...], value_mix[:, side]).astype(half)
    leaving += store_terms(spot, terms, term_outs, 3 * part, main, store_sems, 48)
    wait_all(leaving)


def chain(spot, gathered, mine, theirs, latents, cotangents, vectors, feats, groups):
    blocks, layout = gathered
    rows, width = mine.shape[0], vectors.shape[1]
    part = width // 2
    lanes = 3 * part + main
    outs = term_shapes(groups, width // groups, lanes)
    bits = pltpu.VMEM((rows, width), half)
    result = pl.pallas_call(
        functools.partial(chain_kernel, len(blocks), layout, len(outs), feats),
        out_shape=[
            shape((rows // 2, width), single),
            shape((rows // 2, width), single),
            shape((rows, main + rest), half),
            shape((rows, 128), single),
            shape((8, width), single),
        ]
        + outs,
        in_specs=[scalars] + [remote] * (len(blocks) + 6) + [whole],
        out_specs=[remote] * 2 + [whole] * 3 + [remote] * len(outs),
        scratch_shapes=[
            pltpu.VMEM((2, width, part + main), half),
            pltpu.VMEM((2, width, 2 * part), half),
            pltpu.VMEM((2, rows // 2, width), single),
            pltpu.VMEM((2, rows // 2, width), single),
            pltpu.VMEM((2, rows, main + rest), single),
        ]
        + [bits] * 7
        + [pltpu.VMEM((rows, 2 * main), half)]
        + [pltpu.VMEM((2, rows // 2, width), single)]
        + [pltpu.VMEM((rows // 2, width), single)] * 2
        + [pltpu.VMEM((2, rows // 2, width), single)]
        + [pltpu.VMEM((width, lanes), half)]
        + [pltpu.SemaphoreType.DMA((64,)), pltpu.SemaphoreType.DMA((64,)), pltpu.SemaphoreType.DMA((6,))],
        compiler_params=params,
        cost_estimate=cost(17),
        name="chain",
    )(spot, *blocks, mine, theirs, *latents, *cotangents, vectors)
    return result[:5], result[5:]


def pixel_back_kernel(scale, turn, turns, *refs):
    (query_pix, grad_pix, stats, values_in, keep, pixels, gain, pixel_stats), refs = refs[:8], refs[8:]
    if turn > 0:
        (score_before, sums_before, _), refs = refs[:3], refs[3:]
    score_pix, sums, pixels_grad, values, held, made, score_grads, query_t, grad_t, slope, shift, sems = refs
    feats, count = held.shape
    over = feats - main
    some = main + 16
    step = 512
    origin = turn * count
    here = pl.ds(origin, count)
    early = copy_all([(values_in.at[:, here], values)], sems)
    late = copy_all([(pixels.at[:, 0, here], held)], sems, 1)
    query_t[...] = jnp.transpose(query_pix[...].astype(single))[:some].astype(half)
    grad_t[...] = jnp.transpose(grad_pix[...].astype(single))[:some].astype(half)
    slope[...] = jnp.zeros_like(slope)
    shift[...] = jnp.zeros_like(shift)
    log_total, inner = stats[:, 0:1], stats[:, 1:2]
    leaving = []
    wait_all(early)

    def products(i):
        lanes = pl.ds(i * step, step)
        return nn(query_pix[...], values[:, lanes]), nn(grad_pix[...], values[:, lanes])

    def norm_back(i, grad):
        lanes, there = pl.ds(i * step, step), pl.ds(origin + i * step, step)
        mean, inverse = pixel_stats[0:1, there], pixel_stats[1:2, there]
        unit_a = (held[pl.ds(0, main), lanes] - mean) * inverse
        unit_b = (held[pl.ds(main, over), lanes] - mean) * inverse
        grad_a, grad_b = grad[:main], grad[main : main + over]
        for rows, g, u in ((pl.ds(0, main), grad_a, unit_a), (pl.ds(main, over), grad_b, unit_b)):
            product = g * u
            slope[rows, :] += sum(product[:, 128 * j : 128 * j + 128] for j in range(step // 128))
            shift[rows, :] += sum(g[:, 128 * j : 128 * j + 128] for j in range(step // 128))
        scaled_a, scaled_b = grad_a * gain[pl.ds(0, main)], grad_b * gain[pl.ds(main, over)]
        flat = (jnp.sum(scaled_a, axis=0, keepdims=True) + jnp.sum(scaled_b, axis=0, keepdims=True)) / feats
        along = (
            jnp.sum(scaled_a * unit_a, axis=0, keepdims=True) + jnp.sum(scaled_b * unit_b, axis=0, keepdims=True)
        ) / feats
        made[pl.ds(0, main), lanes] = inverse * (scaled_a - flat - unit_a * along)
        made[pl.ds(main, over), lanes] = inverse * (scaled_b - flat - unit_b * along)
        return copy_all([(made.at[:, lanes], pixels_grad.at[:, 0, there])], sems, 2 + i)

    now, before = products(0), None
    for i in range(count // step):
        scores, weight_grad = now
        if (i + 1) * step < count:
            now = products(i + 1)
        lanes = pl.ds(i * step, step)
        kept = keep[:, pl.ds(origin + i * step, step)] > 0
        attn = jnp.exp(jnp.where(kept, scores, masked_score) - log_total)
        score_grad = (attn * (weight_grad - inner)).astype(half)
        score_grads[:, lanes] = score_grad
        grad = nn(query_t[...], score_grad) + nn(grad_t[...], attn.astype(half))
        if i == 0:
            wait_all(late)
        else:
            leaving += norm_back(i - 1, before)
        before = grad
    leaving += norm_back(count // step - 1, before)
    value = nt(score_grads[...], values[...])
    if turn > 0:
        value = value + score_before[...]
    score_pix[...] = value * scale if turn == turns - 1 else value
    lane = lax.broadcasted_iota(jnp.int32, (feats, 128), 1)
    both = jnp.where(
        lane == 0,
        jnp.sum(slope[...], axis=-1, keepdims=True),
        jnp.sum(shift[...], axis=-1, keepdims=True),
    )
    sums[...] = both + sums_before[...] if turn > 0 else both
    wait_all(leaving)


def pixel_back(query_pix, grad_pix, stats, normed, keep, pixels, gain, pixel_stats, scale, turn, turns, before):
    feats, _, count = pixels.shape
    rows = query_pix.shape[0]
    held = pltpu.VMEM((feats, count // turns), single)
    return pl.pallas_call(
        functools.partial(pixel_back_kernel, scale, turn, turns),
        out_shape=[shape((rows, main + rest), single), shape((feats, 128), single), shape(pixels.shape, single)],
        in_specs=[whole] * 3 + [remote, whole, remote, whole, whole] + [whole, whole, remote][: len(before)],
        out_specs=[whole, whole, remote],
        scratch_shapes=[
            pltpu.VMEM((main + rest, count // turns), half),
            held,
            held,
            pltpu.VMEM((rows, count // turns), half),
            pltpu.VMEM((main + 16, rows), half),
            pltpu.VMEM((main + 16, rows), half),
            pltpu.VMEM((feats, 128), single),
            pltpu.VMEM((feats, 128), single),
            pltpu.SemaphoreType.DMA((2 + count // turns // 512,)),
        ],
        input_output_aliases={10: 2} if before else {},
        compiler_params=params_most,
        cost_estimate=cost(18 / turns),
        name="pixel_back",
    )(query_pix, grad_pix, stats, normed, keep, pixels, gain, pixel_stats, *before)


def query_back_kernel(count, layout, terms_count, spot, *refs):
    blocks, refs = refs[:count], refs[count:]
    mine, theirs, query_in, normed_mine, normed_theirs, latents_in, grad_in, vectors, *refs = refs
    latents_grad, sums, *refs = refs
    term_outs, refs = refs[:terms_count], refs[terms_count:]
    weights, score_pix, query, normed, latents, middle_grad, query_grad, wide, terms, sems, store_sems, more = refs
    ready = load_blocks(spot, blocks, layout, weights, 0, sems)
    rows_all, width = query.shape
    step = rows_all // 2
    part = width // 2
    score_pix[:, pl.ds(main + rest, rest)] = jnp.zeros((rows_all, rest), half)
    for t in range(2):
        rows, other = pl.ds(t * step, step), pl.ds((1 - t) * step, step)
        score_pix[rows, pl.ds(0, main + rest)] = (mine[rows, :] + theirs[other, :]).astype(half)
    wait_all(ready)
    later = copy_all([(normed_mine, normed.at[0]), (normed_theirs, normed.at[1]), (query_in, query)], more)
    last = copy_all([(latents_in, latents), (grad_in, middle_grad)], more, 3)
    value = nt(score_pix[:, pl.ds(0, main)], weights[0, :, pl.ds(part, main)])
    value = value + nt(score_pix[:, pl.ds(main, rest)], weights[1, :, pl.ds(part, rest)])
    query_grad[...] = value.astype(half)
    wait_all(later)
    side = pl.ds(pl.multiple_of(spot[1] * part, part), part)
    value = tn(query_grad[pl.ds(0, step), :], normed[0, :, side])
    terms[:, pl.ds(0, part)] = (value + tn(query_grad[pl.ds(step, step), :], normed[1, :, side])).astype(half)
    leaving = store_terms(spot, terms, term_outs, 0, part, store_sems, 0)
    side = pl.ds(pl.multiple_of(spot[1] * main, main), main)
    terms[:, pl.ds(part, main)] = tn(query[...], score_pix[:, side]).astype(half)
    leaving += store_terms(spot, terms, term_outs, part, main, store_sems, 16)
    value = query_grad[pl.ds(0, step), :]
    wide[:, pl.ds(0, part)] = nn(value, weights[0, :, pl.ds(0, part)])
    wide[:, pl.ds(part, part)] = nn(value, weights[1, :, pl.ds(0, part)])
    wait_all(last)
    unit, inverse = standard(latents[...])
    grad = wide[...]
    latents_grad[...] = middle_grad[...] + standard_back(grad, vectors[0:1, :], unit, inverse)
    sums[...] = jnp.zeros_like(sums)
    sums[0:1, :] = jnp.sum(grad * unit, axis=0, keepdims=True)
    sums[1:2, :] = jnp.sum(grad, axis=0, keepdims=True)
    wait_all(leaving)


def query_back(spot, gathered, mine, theirs, query, normed, latents, middle_grad, vectors, groups):
    blocks, layout = gathered
    rows, width = query.shape
    lanes = width // 2 + main
    outs = term_shapes(groups, width // groups, lanes)
    one = pltpu.VMEM((rows // 2, width), single)
    result = pl.pallas_call(
        functools.partial(query_back_kernel, len(blocks), layout, len(outs)),
        out_shape=[shape((rows // 2, width), single), shape((8, width), single)] + outs,
        in_specs=[scalars] + [remote] * len(blocks) + [whole] * 2 + [remote] * 5 + [whole],
        out_specs=[whole] * 2 + [remote] * len(outs),
        scratch_shapes=[
            pltpu.VMEM((2, width, lanes), half),
            pltpu.VMEM((rows, 2 * main), half),
            pltpu.VMEM((rows, width), half),
            pltpu.VMEM((2, rows // 2, width), half),
            one,
            one,
            pltpu.VMEM((rows, width), half),
            one,
            pltpu.VMEM((width, lanes), half),
            pltpu.SemaphoreType.DMA((32,)),
            pltpu.SemaphoreType.DMA((32,)),
            pltpu.SemaphoreType.DMA((5,)),
        ],
        compiler_params=params_all,
        cost_estimate=cost(7),
        name="query_back",
    )(spot, *blocks, mine, theirs, query, *normed, latents, middle_grad, vectors)
    return result[:2], result[2:]


def moments_kernel(feats, *refs):
    spot, late_mine, late_theirs, early_mine, early_theirs, vectors, *refs = refs
    square_p, square_m, square_v, pixel_p, pixel_m, pixel_v, *refs = refs
    square_outs, pixel_outs, sums = refs[:4], refs[4:8], refs[8]
    width = square_p.shape[2]
    part = width // 2
    first = spot[1] == 0
    lane = lax.broadcasted_iota(jnp.int32, (1, width), 1)
    row = jnp.zeros((1, width), single)
    for m in range(6):
        mine, theirs = (late_mine, late_theirs) if m in (0, 4) else (early_mine, early_theirs)
        if m < 4:
            lanes = pl.ds(max(m - 1, 0) * part, part)
            sides, outs, k = (pl.ds(0, part), pl.ds(part, part)), square_outs, m
            params_now, first_now, second_now = square_p, square_m, square_v
        else:
            lanes = pl.ds(part if m == 4 else 3 * part, main)
            sides, outs, k = (pl.ds(0, main), pl.ds(main, feats - main)), pixel_outs, m - 4
            params_now, first_now, second_now = pixel_p, pixel_m, pixel_v
        own, other = mine[:, lanes], theirs[:, lanes]
        weight_total, update_total = jnp.zeros((1, 1), single), jnp.zeros((1, 1), single)
        for side, grad in zip(sides, (jnp.where(first, own, other), jnp.where(first, other, own))):
            grad = grad[:, : side.size]
            weight = params_now[k, :, side]
            first_new, second_new, ratio = adam_moments(grad, first_now[k, :, side], second_now[k, :, side])
            update = ratio + decay_rate * weight
            for out, value in zip(outs, (grad, first_new, second_new, update)):
                out[k, :, side] = value
            weight_total = weight_total + jnp.sum(weight * weight, keepdims=True)
            update_total = update_total + jnp.sum(update * update, keepdims=True)
        row = row + jnp.where(lane == part + m, weight_total, jnp.where(lane == part + 6 + m, update_total, 0.0))
    sums[...] = vectors[...]
    sums[7:8, pl.ds(part, part)] = row[:, part:]


def moments(spot, late, early, vectors, square, pixel):
    big, small = shape(square[0].shape, single), shape(pixel[0].shape, single)
    return pl.pallas_call(
        functools.partial(moments_kernel, pixel[0].shape[2]),
        out_shape=[big] * 4 + [small] * 4 + [shape((8, big.shape[2]), single)],
        in_specs=[scalars] + [whole] * 11,
        out_specs=[whole] * 9,
        compiler_params=params,
        cost_estimate=cost(5),
        name="moments",
    )(spot, *late, *early, vectors, *square, *pixel)


def apply_kernel(sums, square_p, square_u, pixel_p, pixel_u, *refs):
    states, outs = refs[:6], refs[6:]
    square_new, square_copy, pixel_new, pixel_copy, norms, *news = outs
    part = sums.shape[1] // 2
    squares = sums[7:8, pl.ds(part, 128)]
    weight_norm, update_norm = jnp.sqrt(squares[:, 0:6]), jnp.sqrt(squares[:, 6:12])
    trust = weight_norm / (update_norm + epsilon)
    for row, value in enumerate((weight_norm, update_norm, trust)):
        norms[row : row + 1, :] = value
    for m in range(6):
        k, weight, update, new, copy = (
            (m, square_p, square_u, square_new, square_copy)
            if m < 4
            else (m - 4, pixel_p, pixel_u, pixel_new, pixel_copy)
        )
        value = weight[k] - learn_rate * trust[:, m : m + 1] * update[k]
        new[k] = value
        copy[k] = value.astype(half)
    feats = states[3].shape[1]
    for grad, (value, first, second), out in (
        (sums[0:6, :], states[:3], news[:3]),
        (sums[6:8, 0:feats], states[3:], news[3:]),
    ):
        first_new, second_new, ratio = adam_moments(grad, first[...], second[...])
        out[0][...] = value[...] - vector_rate * ratio
        out[1][...] = first_new
        out[2][...] = second_new


def apply(sums, square_p, square_u, pixel_p, pixel_u, vectors, norms):
    outs = [(square_p, single), (square_p, half), (pixel_p, single), (pixel_p, half)]
    states = [*vectors, *norms]
    return pl.pallas_call(
        apply_kernel,
        out_shape=[shape(a.shape, dtype) for a, dtype in outs]
        + [shape((3, 6), single)]
        + [shape(a.shape, single) for a in states],
        in_specs=[whole] * 11,
        out_specs=[whole] * 11,
        compiler_params=params,
        cost_estimate=cost(4),
        name="apply",
    )(sums, square_p, square_u, pixel_p, pixel_u, *states)


def local(
    latents,
    pixels,
    keep_mask,
    cotangent,
    square_weights,
    square_first,
    square_second,
    pixel_weights,
    pixel_first,
    pixel_second,
    latent_vectors,
    latent_first,
    latent_second,
    pixel_norm,
    pixel_norm_first,
    pixel_norm_second,
):
    width = latents.shape[2]
    feats = pixels.shape[2]
    scale = width ** (-0.5)
    rank = lax.axis_index("seq")
    groups = lax.axis_size("dp")
    spot = jnp.stack([lax.axis_index("dp"), rank]).astype(jnp.int32)

    def turned(array):
        return jnp.transpose(array, (0, 2, 1))

    square = [turned(array) for array in (square_weights, square_first, square_second)]
    pixel = [turned(array) for array in (pixel_weights, pixel_first, pixel_second)]

    latents_two = (latents[0], trade(latents[0]))
    cotangent_two = (cotangent[0], trade(cotangent[0]))
    pixels_t = jnp.transpose(pixels, (2, 0, 1))
    gain, shift = pixel_norm[0][:, None], pixel_norm[1][:, None]
    pixel_normed, pixel_stats = norm_pixels(pixels_t, gain, shift)
    normed = norm_latents(latents[0], latent_vectors)
    normed = (normed, trade(normed))
    blocks = gather_matrices(pack(spot, square[0], pixel[0]), pixel_normed, normed[0])
    query, query_pix, sent = attend(spot, blocks, normed, pixel_normed, keep_mask, scale, feats)
    (latents_out, middle_grad, grad_pix, stats, chain_sums), early_terms = chain(
        spot, blocks, sent, trade(sent), latents_two, cotangent_two, latent_vectors, feats, groups
    )
    pixel_args = (query_pix, grad_pix, stats, pixel_normed, keep_mask, pixels_t, gain, pixel_stats, scale)
    turn_one = pixel_back(*pixel_args, 0, 2, ())
    if len(early_terms) > 1:
        *early_got, score_pix = tie([*send_first(early_terms), turn_one[0]], turn_one[1])
        turn_two = pixel_back(*pixel_args, 1, 2, [score_pix, *turn_one[1:]])
        early_got = send_second(early_terms, early_got, turn_two[0])
    else:
        turn_two, early_got = pixel_back(*pixel_args, 1, 2, turn_one), None
    score_pix, pixel_sums, pixels_grad = turn_two
    (latents_grad, query_sums), late_terms = query_back(
        spot, blocks, score_pix, trade(score_pix), query, normed, latents[0], middle_grad, latent_vectors, groups
    )
    early_got = send_third(early_terms, early_got)
    if len(late_terms) > 1:
        tied = tie([*late_terms[:3], *early_got], late_terms[3])
        late_terms, early_got = [*tied[:3], *late_terms[3:]], tied[3:]
    early = sum_own(early_terms, early_got)
    late = sum_own(late_terms, send_third(late_terms, send_second(late_terms, send_first(late_terms))))

    norm_terms = jnp.pad(jnp.transpose(pixel_sums[:, :2]), ((6, 0), (0, width - feats)))
    vector_terms = chain_sums + query_sums + norm_terms
    vector_terms = vector_terms + trade(vector_terms)
    square_grad, square_first_new, square_second_new, square_u, *rest_outs = moments(
        spot, (late, trade(late)), (early, trade(early)), vector_terms, square, pixel
    )
    pixel_weight_grad, pixel_first_new, pixel_second_new, pixel_u, sums = rest_outs
    square_new, square_copy, pixel_new, pixel_copy, matrix_norms, *news = apply(
        sum_all(sums),
        square[0],
        square_u,
        pixel[0],
        pixel_u,
        (latent_vectors, latent_first, latent_second),
        (pixel_norm, pixel_norm_first, pixel_norm_second),
    )
    latent_vectors_new, latent_first_new, latent_second_new = news[:3]
    pixel_norm_new, pixel_norm_first_new, pixel_norm_second_new = news[3:]
    return (
        latents_out[None],
        latents_grad[None],
        jnp.transpose(pixels_grad, (1, 2, 0)),
        turned(square_grad),
        turned(square_first_new),
        turned(square_second_new),
        turned(square_new),
        turned(square_copy),
        turned(pixel_weight_grad),
        turned(pixel_first_new),
        turned(pixel_second_new),
        turned(pixel_new),
        turned(pixel_copy),
        latent_first_new,
        latent_second_new,
        latent_vectors_new,
        pixel_norm_first_new,
        pixel_norm_second_new,
        pixel_norm_new,
        matrix_norms,
    )


def solution(mesh):
    return jax.shard_map(
        local,
        mesh=mesh,
        in_specs=(
            P("dp", "seq", None),
            P("dp", "seq", None),
            P("dp", "seq"),
            P("dp", "seq", None),
            P(None, None, "dp"),
            P(None, None, "dp"),
            P(None, None, "dp"),
            P(None, None, "dp"),
            P(None, None, "dp"),
            P(None, None, "dp"),
            P(),
            P(),
            P(),
            P(),
            P(),
            P(),
        ),
        out_specs=(
            P("dp", "seq", None),
            P("dp", "seq", None),
            P("dp", "seq", None),
            P(None, None, "dp"),
            P(None, None, "dp"),
            P(None, None, "dp"),
            P(None, None, "dp"),
            P(None, None, "dp"),
            P(None, None, "dp"),
            P(None, None, "dp"),
            P(None, None, "dp"),
            P(None, None, "dp"),
            P(None, None, "dp"),
            P(),
            P(),
            P(),
            P(),
            P(),
            P(),
            P(),
        ),
        check_vma=False,
    )
```

```python
import functools

import jax
import jax.numpy as jnp
from jax import lax
from jax.experimental import pallas as pl
from jax.experimental.pallas import tpu as pltpu
from jax.sharding import PartitionSpec as P

STEP = 10


norm_epsilon = 1e-05
beta_one = 0.9
beta_two = 0.999
decay_rate = 0.01
epsilon = 1e-06
learn_rate = 0.25
vector_rate = 1.0
masked_score = -1e30
gelu_coeff = 0.7978845608028654


def adam_moments(grad, first, second):
    first_new = beta_one * first + (1.0 - beta_one) * grad
    second_new = beta_two * second + (1.0 - beta_two) * grad * grad
    ratio = (
        first_new
        / (1.0 - beta_one**STEP)
        / (jnp.sqrt(second_new / (1.0 - beta_two**STEP)) + epsilon)
    )
    return (first_new, second_new, ratio)

half = jnp.bfloat16
single = jnp.float32
swap = [(0, 1), (1, 0)]
main, rest = 256, 128
whole = pl.BlockSpec(memory_space=pltpu.VMEM)
remote = pl.BlockSpec(memory_space=pl.ANY)
scalars = pl.BlockSpec(memory_space=pltpu.SMEM)
params = pltpu.CompilerParams(vmem_limit_bytes=40 * 2**20)
params_most = pltpu.CompilerParams(vmem_limit_bytes=56 * 2**20)
params_all = pltpu.CompilerParams(vmem_limit_bytes=63 * 2**20)


def cost(micros):
    return pl.CostEstimate(flops=int(micros * 1.1e9), bytes_accessed=1024, transcendentals=0)


def shape(dims, dtype):
    return jax.ShapeDtypeStruct(dims, dtype)


def contract(left, right, over_left, over_right):
    return lax.dot_general(left, right, (((over_left,), (over_right,)), ((), ())), preferred_element_type=single)


def nn(left, right):
    return contract(left, right, 1, 0)


def nt(left, right):
    return contract(left, right, 1, 1)


def tn(left, right):
    return contract(left, right, 0, 0)


def flip(array, mask):
    return lax.ppermute(array, "dp", [(i, i ^ mask) for i in range(lax.axis_size("dp"))])


def trade(array):
    return lax.ppermute(array, "seq", swap)


def special(groups, shard):
    return groups == 16 and shard % 32 == 0


def tie_kernel(*refs):
    pass


def tie(arrays, *after):
    return pl.pallas_call(
        tie_kernel,
        out_shape=[shape(a.shape, a.dtype) for a in arrays],
        in_specs=[remote] * (len(arrays) + len(after)),
        out_specs=[remote] * len(arrays),
        input_output_aliases={i: i for i in range(len(arrays))},
        cost_estimate=cost(0.1),
        name="tie",
    )(*arrays, *after)


def stack_kernel(plan, *refs):
    outs = refs[len(refs) - len(plan) :]
    for out, parts in zip(outs, plan):
        rows = out.shape[0] // len(parts)
        for i, (source, part) in enumerate(parts):
            out[pl.ds(i * rows, rows), :] = refs[source][pl.ds(part * rows, rows), :]


def stack(arrays, rows, plan, *after):
    lanes, dtype = arrays[0].shape[1], arrays[0].dtype
    return pl.pallas_call(
        functools.partial(stack_kernel, plan),
        out_shape=[shape((rows * len(parts), lanes), dtype) for parts in plan],
        in_specs=[whole] * len(arrays) + [remote] * len(after),
        out_specs=[whole] * len(plan),
        compiler_params=params,
        cost_estimate=cost(1.5),
        name="stack",
    )(*arrays, *after)


def gather_blocks(block, early, late):
    rows = block.shape[0]
    one, two, four, three, eight = [flip(block, o) for o in (1, 2, 4, 3, 8)]
    across, both = stack([three, four, eight], rows, (((0, 0), (2, 0)), ((1, 0), (2, 0))), early)
    (gathered,) = stack([block, eight, four, three, two, one], rows, (tuple((i, 0) for i in range(6)),))
    second = [flip(across, 4), flip(both, 2), flip(both, 1)]
    seven, twelve, twelve_ten = stack(second[:2], rows, (((0, 0),), ((0, 1),), ((0, 1), (1, 1))), second[2], late)
    third = [flip(seven, 8), flip(twelve, 2), flip(twelve_ten, 1)]
    return [
        ((0, 8, 4, 3, 2, 1), gathered),
        ((7, 12), second[0]),
        ((6, 10), second[1]),
        ((5, 9), second[2]),
        ((15,), third[0]),
        ((14,), third[1]),
        ((13, 11), third[2]),
    ]


def pack_kernel(feats, spot, squares, pixels, block):
    side = spot[1]
    part = squares.shape[2] // 2
    lanes = pl.ds(pl.multiple_of(side * part, part), part)
    over = feats - main

    def pixel(m):
        last = pixels[m, :, pl.ds(main, over)]
        last = jnp.concatenate([last, jnp.zeros((last.shape[0], main - over), single)], axis=1)
        return jnp.where(side == 0, pixels[m, :, pl.ds(0, main)], last).astype(half)

    block[:, pl.ds(0, part)] = squares[0, :, lanes].astype(half)
    block[:, pl.ds(part, main)] = pixel(0)
    block[:, pl.ds(part + main, main)] = pixel(1)
    for m in range(1, 4):
        block[:, pl.ds(m * part + 2 * main, part)] = squares[m, :, lanes].astype(half)


def pack(spot, squares, pixels):
    _, shard, width = squares.shape
    return pl.pallas_call(
        functools.partial(pack_kernel, pixels.shape[2]),
        out_shape=shape((shard, 4 * (width // 2) + 2 * main), half),
        in_specs=[scalars, whole, whole],
        out_specs=whole,
        compiler_params=params,
        cost_estimate=cost(2),
        name="pack",
    )(spot, squares, pixels)


def gather_matrices(block, early, late):
    groups = lax.axis_size("dp")
    shard = block.shape[0]
    if special(groups, shard):
        arrays, layout = [], []
        for positions, array in gather_blocks(block, early, late):
            arrays += [array, trade(array)]
            layout += [(positions, 0), (positions, 1)]
        return arrays, tuple(layout)
    every = lax.all_gather(block, ("dp", "seq"), axis=0).reshape(groups, 2, shard, -1)
    return [every.transpose(1, 0, 2, 3).reshape(2, groups * shard, -1)], ()


def place_blocks(spot, blocks, layout, target, first):
    lanes = pl.ds(first, target.shape[2])
    if not layout:
        target[...] = blocks[0][:, :, lanes]
    for block, (positions, turn) in zip(blocks, layout):
        rows = block.shape[0] // len(positions)
        side = lax.bitwise_xor(spot[1], turn)
        for i, o in enumerate(positions):
            chip = lax.bitwise_xor(spot[0], o)
            place = pl.ds(pl.multiple_of(chip * rows, rows), rows)
            target[side, place, :] = block[pl.ds(i * rows, rows), lanes]


def copy_all(pairs, sems, first=0):
    copies = [pltpu.make_async_copy(source, target, sems.at[first + i]) for i, (source, target) in enumerate(pairs)]
    for copy in copies:
        copy.start()
    return copies


def wait_all(copies):
    for copy in copies:
        copy.wait()


def load_blocks(spot, blocks, layout, target, first, sems, base=0):
    pairs = []
    lanes = pl.ds(first, target.shape[2])
    if not layout:
        pairs.append((blocks[0].at[:, :, lanes], target))
    for block, (positions, turn) in zip(blocks, layout):
        rows = block.shape[0] // len(positions)
        side = lax.bitwise_xor(spot[1], turn)
        for i, o in enumerate(positions):
            chip = lax.bitwise_xor(spot[0], o)
            place = target.at[side, pl.ds(pl.multiple_of(chip * rows, rows), rows)]
            pairs.append((block.at[pl.ds(i * rows, rows), lanes], place))
    return copy_all(pairs, sems, base)


written = ((13, 11), (14,), (15,), (5, 9), (6, 10), (7, 12), (1,), (2,), (3,), (4,), (8,), (0,))


def store_terms(spot, terms, outs, start, count, sems, base):
    lanes = pl.ds(start, count)
    if len(outs) == 1:
        return copy_all([(terms.at[:, lanes], outs[0].at[:, lanes])], sems, base)
    pairs = []
    rows = terms.shape[0] // 16
    for positions, out in zip(written, outs):
        for i, o in enumerate(positions):
            chip = lax.bitwise_xor(spot[0], o)
            source = terms.at[pl.ds(pl.multiple_of(chip * rows, rows), rows), lanes]
            pairs.append((source, out.at[pl.ds(i * rows, rows), lanes]))
    return copy_all(pairs, sems, base)


def term_shapes(groups, shard, lanes):
    if special(groups, shard):
        return [shape((len(positions) * shard, lanes), half) for positions in written]
    return [shape((groups * shard, lanes), half)]


def send_first(terms, *after):
    if len(terms) == 1:
        return None
    got = [flip(terms[0], 1), flip(terms[1], 2), flip(terms[2], 8)]
    return tie(got, *after) if after else got


def send_second(terms, got, *after):
    if len(terms) == 1:
        return None
    rows = terms[-1].shape[0]

    def added(array, low, *high):
        total = array.astype(single)
        if low is not None:
            total = total + jnp.pad(low.astype(single), ((0, rows), (0, 0)))
        for other in high:
            total = total + jnp.pad(other.astype(single), ((rows, 0), (0, 0)))
        return total.astype(half)

    twelve, ten = got[0][:rows], got[0][rows:]
    got = [
        flip(terms[3], 1),
        flip(added(terms[4], None, ten), 2),
        flip(added(terms[5], got[2], twelve, got[1]), 4),
    ]
    return tie(got, *after) if after else got


def send_third(terms, got):
    if len(terms) == 1:
        return [lax.psum_scatter(terms[0], "dp", scatter_dimension=0, tiled=True)]
    rows = terms[-1].shape[0]
    one, two = terms[6:8]
    three, four, eight = [term.astype(single) for term in terms[8:11]]
    upper = [array[:rows].astype(single) for array in got]
    lower = [array[rows:].astype(single) for array in got]
    sent = [
        (one, 1),
        (two, 2),
        (four + upper[0] + upper[1], 4),
        (three + upper[2], 3),
        (eight + lower[0] + lower[1] + lower[2], 8),
    ]
    return [flip(array.astype(half), mask) for array, mask in sent]


def sum_own(terms, got):
    if len(terms) > 1:
        got = [terms[-1], *got]
    total = got[0].astype(single)
    for array in got[1:]:
        total = total + array.astype(single)
    return total


def sum_all(array):
    mask = 1
    size = lax.axis_size("dp")
    while mask < size:
        if mask * 2 < size:
            one, two, three = flip(array, mask), flip(array, 2 * mask), flip(array, 3 * mask)
            array = (array + one) + (two + three)
            mask *= 4
        else:
            array = array + flip(array, mask)
            mask *= 2
    return array


def standard(values):
    center = values - jnp.mean(values, axis=-1, keepdims=True)
    inverse = lax.rsqrt(jnp.mean(center * center, axis=-1, keepdims=True) + norm_epsilon)
    return center * inverse, inverse


def standard_back(grad, gain, unit, inverse):
    scaled = grad * gain
    return inverse * (
        scaled - jnp.mean(scaled, axis=-1, keepdims=True) - unit * jnp.mean(scaled * unit, axis=-1, keepdims=True)
    )


def pixel_kernel(pixels, gain, shift, normed, stats, held, tail, sem):
    copy = pltpu.make_async_copy(pixels.at[:, 0, :], held, sem)
    copy.start()
    feats = held.shape[0]
    step = 256
    over = feats - main
    tail[...] = jnp.zeros_like(tail)
    copy.wait()

    @pl.loop(0, held.shape[1] // step)
    def _(i):
        lanes = pl.ds(pl.multiple_of(i * step, step), step)
        first, last = held[pl.ds(0, main), lanes], held[pl.ds(main, over), lanes]
        mean = (jnp.sum(first, axis=0, keepdims=True) + jnp.sum(last, axis=0, keepdims=True)) / feats
        first, last = first - mean, last - mean
        spread = (
            jnp.sum(first * first, axis=0, keepdims=True) + jnp.sum(last * last, axis=0, keepdims=True)
        ) / feats
        inverse = lax.rsqrt(spread + norm_epsilon)
        normed[pl.ds(0, main), lanes] = (first * inverse * gain[pl.ds(0, main)] + shift[pl.ds(0, main)]).astype(half)
        tail[pl.ds(0, over), :] = last * inverse * gain[pl.ds(main, over)] + shift[pl.ds(main, over)]
        normed[pl.ds(main, rest), lanes] = tail[...].astype(half)
        stats[0:1, lanes] = mean
        stats[1:2, lanes] = inverse


def norm_pixels(pixels, gain, shift):
    feats, _, count = pixels.shape
    return pl.pallas_call(
        pixel_kernel,
        out_shape=[shape((main + rest, count), half), shape((2, count), single)],
        in_specs=[remote, whole, whole],
        out_specs=[whole] * 2,
        scratch_shapes=[pltpu.VMEM((feats, count), single), pltpu.VMEM((rest, 256), single), pltpu.SemaphoreType.DMA],
        compiler_params=params,
        cost_estimate=cost(7),
        name="norm_pixels",
    )(pixels, gain, shift)


def latent_kernel(latents, vectors, normed):
    unit, _ = standard(latents[...])
    normed[...] = (unit * vectors[0:1, :] + vectors[1:2, :]).astype(half)


def norm_latents(latents, vectors):
    return pl.pallas_call(
        latent_kernel,
        out_shape=shape(latents.shape, half),
        in_specs=[whole] * 2,
        out_specs=whole,
        compiler_params=params,
        cost_estimate=cost(2),
        name="norm_latents",
    )(latents, vectors)


def attend_kernel(count, layout, scale, feats, spot, *refs):
    blocks = refs[:count]
    mine, theirs, pixels_in, keep, query_out, query_pix, sent, *refs = refs[count:]
    weights, normed, pixels, query, scores, peak, more = refs
    copies = copy_all([(mine, normed.at[0]), (theirs, normed.at[1])], more)
    late = copy_all([(pixels_in, pixels)], more, 2)
    place_blocks(spot, blocks, layout, weights, 0)
    wait_all(copies)
    step, part = mine.shape[0], mine.shape[1] // 2
    for t in range(2):
        rows = pl.ds(t * step, step)
        value = nt(normed[t, :, pl.ds(0, part)], weights[0, :, pl.ds(0, part)])
        value = value + nt(normed[t, :, pl.ds(part, part)], weights[1, :, pl.ds(0, part)])
        value = value.astype(half)
        query[rows, :] = value
        query_pix[rows, pl.ds(0, main)] = (nn(value, weights[0, :, pl.ds(part, main)]) * scale).astype(half)
        query_pix[rows, pl.ds(main, rest)] = (nn(value, weights[1, :, pl.ds(part, rest)]) * scale).astype(half)
    wait_all(late)
    late = copy_all([(query, query_out)], more, 2)
    step = 1024
    peak[...] = jnp.full(peak.shape, -jnp.inf, single)

    @pl.loop(0, pixels.shape[1] // step)
    def _(j):
        lanes = pl.ds(pl.multiple_of(j * step, step), step)
        value = nn(query_pix[...], pixels[:, lanes])
        value = jnp.where(keep[:, lanes] > 0, value, masked_score)
        scores[:, lanes] = value
        some = [value[:, 128 * k : 128 * k + 128] for k in range(step // 128)]
        peak[...] = functools.reduce(jnp.maximum, some, peak[...])

    top = jnp.max(peak[...], axis=-1, keepdims=True)
    peak[...] = jnp.zeros_like(peak)
    sent[...] = jnp.zeros_like(sent)

    @pl.loop(0, pixels.shape[1] // step)
    def _(j):
        lanes = pl.ds(pl.multiple_of(j * step, step), step)
        value = jnp.exp(scores[:, lanes] - top)
        peak[...] += sum(value[:, 128 * k : 128 * k + 128] for k in range(step // 128))
        sent[...] += nt(value.astype(half), pixels[:, lanes])

    total, mix = peak[...], sent[...]
    total = jnp.sum(total, axis=-1, keepdims=True)
    lane = lax.broadcasted_iota(jnp.int32, mix.shape, 1)
    sent[...] = jnp.where(lane == feats, top, jnp.where(lane == feats + 1, total, mix))
    wait_all(late)


def attend(spot, gathered, normed, pixels, keep, scale, feats):
    blocks, layout = gathered
    rows, width = 2 * normed[0].shape[0], normed[0].shape[1]
    lanes = width // 2 + main
    return pl.pallas_call(
        functools.partial(attend_kernel, len(blocks), layout, scale, feats),
        out_shape=[shape((rows, width), half), shape((rows, main + rest), half), shape((rows, main + rest), single)],
        in_specs=[scalars] + [whole] * len(blocks) + [remote] * 3 + [whole],
        out_specs=[remote, whole, whole],
        scratch_shapes=[
            pltpu.VMEM((2, width, lanes), half),
            pltpu.VMEM((2, rows // 2, width), half),
            pltpu.VMEM(pixels.shape, half),
            pltpu.VMEM((rows, width), half),
            pltpu.VMEM((rows, pixels.shape[1]), single),
            pltpu.VMEM((rows, 128), single),
            pltpu.SemaphoreType.DMA((3,)),
        ],
        compiler_params=params,
        cost_estimate=cost(11),
        name="attend",
    )(spot, *blocks, *normed, pixels, keep)


def chain_kernel(count, layout, terms_count, feats, spot, *refs):
    blocks, refs = refs[:count], refs[count:]
    mine, theirs, latent_mine, latent_theirs, cot_mine, cot_theirs, vectors, *refs = refs
    latents_out, middle_grad, grad_pix, stats, sums, *refs = refs
    term_outs, refs = refs[:terms_count], refs[terms_count:]
    near, far, latents_in, cot_in, mixes, *refs = refs
    attended, middle_half, mixed, hidden_grad, active, out_half, attended_grad, value_mix, *refs = refs
    wide, out_wide, grad_wide, scratch, terms, sems, store_sems, more = refs
    rows_all, width = attended.shape
    step = rows_all // 2
    part = width // 2
    ready = copy_all([(mine, mixes.at[0]), (theirs, mixes.at[1])], more)
    ready += load_blocks(spot, blocks, layout, near, part + main, sems)
    ready_latents = copy_all([(latent_mine, latents_in.at[0]), (latent_theirs, latents_in.at[1])], more, 2)
    matrices = ((near, main), (far, 0), (far, part))
    leaving = []
    pair = range(2)
    rows = [pl.ds(t * step, step) for t in pair]

    def into(value, m):
        source, start = matrices[m]
        lanes = pl.ds(start, part)
        return nt(value[:, :part], source[0, :, lanes]) + nt(value[:, part:], source[1, :, lanes])

    def back(value, m, target):
        source, start = matrices[m]
        lanes = pl.ds(start, part)
        target[:, pl.ds(0, part)] = nn(value, source[0, :, lanes])
        target[:, pl.ds(part, part)] = nn(value, source[1, :, lanes])

    side = pl.ds(pl.multiple_of(spot[1] * part, part), part)

    def term(m, grad, value):
        terms[:, pl.ds(m * part, part)] = tn(grad[...], value[:, side]).astype(half)
        return store_terms(spot, terms, term_outs, m * part, part, store_sems, 16 * m)

    sums[...] = jnp.zeros_like(sums)
    value_mix[...] = jnp.zeros_like(value_mix)
    wait_all(ready)
    ready_far = load_blocks(spot, blocks, layout, far, 2 * part + 2 * main, sems, 32)
    ready_far += copy_all([(cot_mine, cot_in.at[0]), (cot_theirs, cot_in.at[1])], more, 4)
    tops, totals, attended_f, middles, units, inverses, hiddens, curves = [[None, None] for _ in range(8)]
    for t in pair:
        here, there = mixes[0, rows[t], :], mixes[1, rows[1 - t], :]
        top_here, top_there = here[:, feats : feats + 1], there[:, feats : feats + 1]
        top = jnp.maximum(top_here, top_there)
        scale_here, scale_there = jnp.exp(top_here - top), jnp.exp(top_there - top)
        total = here[:, feats + 1 : feats + 2] * scale_here + there[:, feats + 1 : feats + 2] * scale_there
        mix = (here * scale_here + there * scale_there) / total
        lane = lax.broadcasted_iota(jnp.int32, mix.shape, 1)
        value_mix[rows[t], pl.ds(0, main + rest)] = jnp.where(lane < feats, mix, 0.0).astype(half)
        tops[t], totals[t] = top, total
    for t in pair:
        value = nt(value_mix[rows[t], pl.ds(0, main)], near[0, :, pl.ds(0, main)])
        value = value + nt(value_mix[rows[t], pl.ds(main, rest)], near[1, :, pl.ds(0, rest)])
        wide[t] = value
        attended[rows[t], :] = value.astype(half)
    wait_all(ready_latents)
    for t in pair:
        middles[t] = latents_in[t] + into(attended[rows[t], :], 0)
    for t in pair:
        units[t], inverses[t] = standard(middles[t])
        mixed[rows[t], :] = (units[t] * vectors[2:3, :] + vectors[3:4, :]).astype(half)
    wait_all(ready_far)
    for t in pair:
        value = cot_in[t].astype(half)
        out_half[rows[t], :] = value
        if t == 0:
            sums[5:6, :] = jnp.sum(value.astype(single), axis=0, keepdims=True)
    for t in pair:
        hiddens[t] = into(mixed[rows[t], :], 1) + vectors[4:5, :]
    for t in pair:
        back(out_half[rows[t], :], 2, scratch.at[t])
        hidden = hiddens[t]
        curve = jnp.tanh(gelu_coeff * (hidden + 0.044715 * hidden * hidden * hidden))
        active[rows[t], :] = (0.5 * hidden * (1.0 + curve)).astype(half)
        curves[t] = curve
    leaving += term(2, out_half, active)
    out_wide[...] = middles[0] + into(active[rows[0], :], 2) + vectors[5:6, :]
    leaving += copy_all([(out_wide, latents_out)], more)
    for t in pair:
        hidden, curve = hiddens[t], curves[t]
        slope = 0.5 * (1.0 + curve) + 0.5 * hidden * (1.0 - curve * curve) * gelu_coeff * (
            1.0 + 3.0 * 0.044715 * hidden * hidden
        )
        value = (scratch[t] * slope).astype(half)
        hidden_grad[rows[t], :] = value
        if t == 0:
            sums[4:5, :] = jnp.sum(value.astype(single), axis=0, keepdims=True)
    for t in pair:
        back(hidden_grad[rows[t], :], 1, scratch.at[t])
    leaving += term(1, hidden_grad, mixed)
    for t in pair:
        mixed_grad = scratch[t]
        if t == 0:
            sums[2:3, :] = jnp.sum(mixed_grad * units[t], axis=0, keepdims=True)
            sums[3:4, :] = jnp.sum(mixed_grad, axis=0, keepdims=True)
        grad = cot_in[t] + standard_back(mixed_grad, vectors[2:3, :], units[t], inverses[t])
        if t == 0:
            grad_wide[...] = grad
            leaving += copy_all([(grad_wide, middle_grad)], more, 1)
        middle_half[rows[t], :] = grad.astype(half)
    for t in pair:
        back(middle_half[rows[t], :], 0, scratch.at[t])
    leaving += term(0, middle_half, attended)
    for t in pair:
        value = scratch[t].astype(half)
        attended_grad[rows[t], :] = value
        inner = jnp.sum(wide[t] * value.astype(single), axis=-1, keepdims=True)
        lane = lax.broadcasted_iota(jnp.int32, (step, 128), 1)
        stats[rows[t], :] = jnp.where(lane == 0, tops[t] + jnp.log(totals[t]), inner)
    for t in pair:
        value = attended_grad[rows[t], :]
        grad_pix[rows[t], pl.ds(0, main)] = nn(value, near[0, :, pl.ds(0, main)]).astype(half)
        grad_pix[rows[t], pl.ds(main, rest)] = nn(value, near[1, :, pl.ds(0, rest)]).astype(half)
    side = pl.ds(pl.multiple_of(spot[1] * main, main), main)
    terms[:, pl.ds(3 * part, main)] = tn(attended_grad[...], value_mix[:, side]).astype(half)
    leaving += store_terms(spot, terms, term_outs, 3 * part, main, store_sems, 48)
    wait_all(leaving)


def chain(spot, gathered, mine, theirs, latents, cotangents, vectors, feats, groups):
    blocks, layout = gathered
    rows, width = mine.shape[0], vectors.shape[1]
    part = width // 2
    lanes = 3 * part + main
    outs = term_shapes(groups, width // groups, lanes)
    bits = pltpu.VMEM((rows, width), half)
    result = pl.pallas_call(
        functools.partial(chain_kernel, len(blocks), layout, len(outs), feats),
        out_shape=[
            shape((rows // 2, width), single),
            shape((rows // 2, width), single),
            shape((rows, main + rest), half),
            shape((rows, 128), single),
            shape((8, width), single),
        ]
        + outs,
        in_specs=[scalars] + [remote] * (len(blocks) + 6) + [whole],
        out_specs=[remote] * 2 + [whole] * 3 + [remote] * len(outs),
        scratch_shapes=[
            pltpu.VMEM((2, width, part + main), half),
            pltpu.VMEM((2, width, 2 * part), half),
            pltpu.VMEM((2, rows // 2, width), single),
            pltpu.VMEM((2, rows // 2, width), single),
            pltpu.VMEM((2, rows, main + rest), single),
        ]
        + [bits] * 7
        + [pltpu.VMEM((rows, 2 * main), half)]
        + [pltpu.VMEM((2, rows // 2, width), single)]
        + [pltpu.VMEM((rows // 2, width), single)] * 2
        + [pltpu.VMEM((2, rows // 2, width), single)]
        + [pltpu.VMEM((width, lanes), half)]
        + [pltpu.SemaphoreType.DMA((64,)), pltpu.SemaphoreType.DMA((64,)), pltpu.SemaphoreType.DMA((6,))],
        compiler_params=params,
        cost_estimate=cost(17),
        name="chain",
    )(spot, *blocks, mine, theirs, *latents, *cotangents, vectors)
    return result[:5], result[5:]


def pixel_back_kernel(scale, turn, turns, *refs):
    (query_pix, grad_pix, stats, values_in, keep, pixels, gain, pixel_stats), refs = refs[:8], refs[8:]
    if turn > 0:
        (score_before, sums_before, _), refs = refs[:3], refs[3:]
    score_pix, sums, pixels_grad, values, held, made, score_grads, query_t, grad_t, slope, shift, sems = refs
    feats, count = held.shape
    over = feats - main
    some = main + 16
    step = 512
    origin = turn * count
    here = pl.ds(origin, count)
    early = copy_all([(values_in.at[:, here], values)], sems)
    late = copy_all([(pixels.at[:, 0, here], held)], sems, 1)
    query_t[...] = jnp.transpose(query_pix[...].astype(single))[:some].astype(half)
    grad_t[...] = jnp.transpose(grad_pix[...].astype(single))[:some].astype(half)
    slope[...] = jnp.zeros_like(slope)
    shift[...] = jnp.zeros_like(shift)
    log_total, inner = stats[:, 0:1], stats[:, 1:2]
    wait_all(early)

    def products(start):
        some_values = values[:, pl.ds(pl.multiple_of(start, step), step)]
        return nn(query_pix[...], some_values), nn(grad_pix[...], some_values)

    def norm_back(start, grad):
        lanes = pl.ds(pl.multiple_of(start, step), step)
        there = pl.ds(pl.multiple_of(origin + start, step), step)
        mean, inverse = pixel_stats[0:1, there], pixel_stats[1:2, there]
        unit_a = (held[pl.ds(0, main), lanes] - mean) * inverse
        unit_b = (held[pl.ds(main, over), lanes] - mean) * inverse
        grad_a, grad_b = grad[:main], grad[main : main + over]
        for rows, g, u in ((pl.ds(0, main), grad_a, unit_a), (pl.ds(main, over), grad_b, unit_b)):
            product = g * u
            slope[rows, :] += sum(product[:, 128 * j : 128 * j + 128] for j in range(step // 128))
            shift[rows, :] += sum(g[:, 128 * j : 128 * j + 128] for j in range(step // 128))
        scaled_a, scaled_b = grad_a * gain[pl.ds(0, main)], grad_b * gain[pl.ds(main, over)]
        flat = (jnp.sum(scaled_a, axis=0, keepdims=True) + jnp.sum(scaled_b, axis=0, keepdims=True)) / feats
        along = (
            jnp.sum(scaled_a * unit_a, axis=0, keepdims=True) + jnp.sum(scaled_b * unit_b, axis=0, keepdims=True)
        ) / feats
        made[pl.ds(0, main), lanes] = inverse * (scaled_a - flat - unit_a * along)
        made[pl.ds(main, over), lanes] = inverse * (scaled_b - flat - unit_b * along)

    def leaving(i):
        lanes = pl.ds(pl.multiple_of(2 * i * step, step), 2 * step)
        there = pl.ds(pl.multiple_of(origin + 2 * i * step, step), 2 * step)
        return pltpu.make_async_copy(made.at[:, lanes], pixels_grad.at[:, 0, there], sems.at[2 + i])

    wait_all(late)

    @pl.loop(0, count // (2 * step))
    def _(i):
        starts = [(2 * i + k) * step for k in range(2)]
        now, grads = products(starts[0]), []
        for k, start in enumerate(starts):
            scores, weight_grad = now
            if k == 0:
                now = products(starts[1])
            lanes = pl.ds(pl.multiple_of(start, step), step)
            kept = keep[:, pl.ds(pl.multiple_of(origin + start, step), step)] > 0
            attn = jnp.exp(jnp.where(kept, scores, masked_score) - log_total)
            score_grad = (attn * (weight_grad - inner)).astype(half)
            score_grads[:, lanes] = score_grad
            grads.append(nn(query_t[...], score_grad) + nn(grad_t[...], attn.astype(half)))
        for start, grad in zip(starts, grads):
            norm_back(start, grad)
        leaving(i).start()

    value = nt(score_grads[...], values[...])
    if turn > 0:
        value = value + score_before[...]
    score_pix[...] = value * scale if turn == turns - 1 else value
    lane = lax.broadcasted_iota(jnp.int32, (feats, 128), 1)
    both = jnp.where(
        lane == 0,
        jnp.sum(slope[...], axis=-1, keepdims=True),
        jnp.sum(shift[...], axis=-1, keepdims=True),
    )
    sums[...] = both + sums_before[...] if turn > 0 else both

    @pl.loop(0, count // (2 * step))
    def _(i):
        leaving(i).wait()


def pixel_back(query_pix, grad_pix, stats, normed, keep, pixels, gain, pixel_stats, scale, turn, turns, before):
    feats, _, count = pixels.shape
    rows = query_pix.shape[0]
    held = pltpu.VMEM((feats, count // turns), single)
    return pl.pallas_call(
        functools.partial(pixel_back_kernel, scale, turn, turns),
        out_shape=[shape((rows, main + rest), single), shape((feats, 128), single), shape(pixels.shape, single)],
        in_specs=[whole] * 3 + [remote, whole, remote, whole, whole] + [whole, whole, remote][: len(before)],
        out_specs=[whole, whole, remote],
        scratch_shapes=[
            pltpu.VMEM((main + rest, count // turns), half),
            held,
            held,
            pltpu.VMEM((rows, count // turns), half),
            pltpu.VMEM((main + 16, rows), half),
            pltpu.VMEM((main + 16, rows), half),
            pltpu.VMEM((feats, 128), single),
            pltpu.VMEM((feats, 128), single),
            pltpu.SemaphoreType.DMA((2 + count // turns // 512,)),
        ],
        input_output_aliases={10: 2} if before else {},
        compiler_params=params_most,
        cost_estimate=cost(18 / turns),
        name="pixel_back",
    )(query_pix, grad_pix, stats, normed, keep, pixels, gain, pixel_stats, *before)


def query_back_kernel(count, layout, terms_count, spot, *refs):
    blocks, refs = refs[:count], refs[count:]
    mine, theirs, query_in, normed_mine, normed_theirs, latents_in, grad_in, vectors, *refs = refs
    latents_grad, sums, *refs = refs
    term_outs, refs = refs[:terms_count], refs[terms_count:]
    weights, score_pix, query, normed, latents, middle_grad, query_grad, wide, terms, sems, store_sems, more = refs
    ready = load_blocks(spot, blocks, layout, weights, 0, sems)
    rows_all, width = query.shape
    step = rows_all // 2
    part = width // 2
    score_pix[:, pl.ds(main + rest, rest)] = jnp.zeros((rows_all, rest), half)
    for t in range(2):
        rows, other = pl.ds(t * step, step), pl.ds((1 - t) * step, step)
        score_pix[rows, pl.ds(0, main + rest)] = (mine[rows, :] + theirs[other, :]).astype(half)
    wait_all(ready)
    later = copy_all([(normed_mine, normed.at[0]), (normed_theirs, normed.at[1]), (query_in, query)], more)
    last = copy_all([(latents_in, latents), (grad_in, middle_grad)], more, 3)
    value = nt(score_pix[:, pl.ds(0, main)], weights[0, :, pl.ds(part, main)])
    value = value + nt(score_pix[:, pl.ds(main, rest)], weights[1, :, pl.ds(part, rest)])
    query_grad[...] = value.astype(half)
    wait_all(later)
    side = pl.ds(pl.multiple_of(spot[1] * part, part), part)
    value = tn(query_grad[pl.ds(0, step), :], normed[0, :, side])
    terms[:, pl.ds(0, part)] = (value + tn(query_grad[pl.ds(step, step), :], normed[1, :, side])).astype(half)
    leaving = store_terms(spot, terms, term_outs, 0, part, store_sems, 0)
    side = pl.ds(pl.multiple_of(spot[1] * main, main), main)
    terms[:, pl.ds(part, main)] = tn(query[...], score_pix[:, side]).astype(half)
    leaving += store_terms(spot, terms, term_outs, part, main, store_sems, 16)
    value = query_grad[pl.ds(0, step), :]
    wide[:, pl.ds(0, part)] = nn(value, weights[0, :, pl.ds(0, part)])
    wide[:, pl.ds(part, part)] = nn(value, weights[1, :, pl.ds(0, part)])
    wait_all(last)
    unit, inverse = standard(latents[...])
    grad = wide[...]
    latents_grad[...] = middle_grad[...] + standard_back(grad, vectors[0:1, :], unit, inverse)
    sums[...] = jnp.zeros_like(sums)
    sums[0:1, :] = jnp.sum(grad * unit, axis=0, keepdims=True)
    sums[1:2, :] = jnp.sum(grad, axis=0, keepdims=True)
    wait_all(leaving)


def query_back(spot, gathered, mine, theirs, query, normed, latents, middle_grad, vectors, groups):
    blocks, layout = gathered
    rows, width = query.shape
    lanes = width // 2 + main
    outs = term_shapes(groups, width // groups, lanes)
    one = pltpu.VMEM((rows // 2, width), single)
    result = pl.pallas_call(
        functools.partial(query_back_kernel, len(blocks), layout, len(outs)),
        out_shape=[shape((rows // 2, width), single), shape((8, width), single)] + outs,
        in_specs=[scalars] + [remote] * len(blocks) + [whole] * 2 + [remote] * 5 + [whole],
        out_specs=[whole] * 2 + [remote] * len(outs),
        scratch_shapes=[
            pltpu.VMEM((2, width, lanes), half),
            pltpu.VMEM((rows, 2 * main), half),
            pltpu.VMEM((rows, width), half),
            pltpu.VMEM((2, rows // 2, width), half),
            one,
            one,
            pltpu.VMEM((rows, width), half),
            one,
            pltpu.VMEM((width, lanes), half),
            pltpu.SemaphoreType.DMA((32,)),
            pltpu.SemaphoreType.DMA((32,)),
            pltpu.SemaphoreType.DMA((5,)),
        ],
        compiler_params=params_all,
        cost_estimate=cost(7),
        name="query_back",
    )(spot, *blocks, mine, theirs, query, *normed, latents, middle_grad, vectors)
    return result[:2], result[2:]


def moments_kernel(feats, *refs):
    spot, late_mine, late_theirs, early_mine, early_theirs, vectors, *refs = refs
    square_p, square_m, square_v, pixel_p, pixel_m, pixel_v, *refs = refs
    square_outs, pixel_outs, sums = refs[:4], refs[4:8], refs[8]
    width = square_p.shape[2]
    part = width // 2
    first = spot[1] == 0
    lane = lax.broadcasted_iota(jnp.int32, (1, width), 1)
    row = jnp.zeros((1, width), single)
    for m in range(6):
        mine, theirs = (late_mine, late_theirs) if m in (0, 4) else (early_mine, early_theirs)
        if m < 4:
            lanes = pl.ds(max(m - 1, 0) * part, part)
            sides, outs, k = (pl.ds(0, part), pl.ds(part, part)), square_outs, m
            params_now, first_now, second_now = square_p, square_m, square_v
        else:
            lanes = pl.ds(part if m == 4 else 3 * part, main)
            sides, outs, k = (pl.ds(0, main), pl.ds(main, feats - main)), pixel_outs, m - 4
            params_now, first_now, second_now = pixel_p, pixel_m, pixel_v
        own, other = mine[:, lanes], theirs[:, lanes]
        weight_total, update_total = jnp.zeros((1, 1), single), jnp.zeros((1, 1), single)
        for side, grad in zip(sides, (jnp.where(first, own, other), jnp.where(first, other, own))):
            grad = grad[:, : side.size]
            weight = params_now[k, :, side]
            first_new, second_new, ratio = adam_moments(grad, first_now[k, :, side], second_now[k, :, side])
            update = ratio + decay_rate * weight
            for out, value in zip(outs, (grad, first_new, second_new, update)):
                out[k, :, side] = value
            weight_total = weight_total + jnp.sum(weight * weight, keepdims=True)
            update_total = update_total + jnp.sum(update * update, keepdims=True)
        row = row + jnp.where(lane == part + m, weight_total, jnp.where(lane == part + 6 + m, update_total, 0.0))
    sums[...] = vectors[...]
    sums[7:8, pl.ds(part, part)] = row[:, part:]


def moments(spot, late, early, vectors, square, pixel):
    big, small = shape(square[0].shape, single), shape(pixel[0].shape, single)
    return pl.pallas_call(
        functools.partial(moments_kernel, pixel[0].shape[2]),
        out_shape=[big] * 4 + [small] * 4 + [shape((8, big.shape[2]), single)],
        in_specs=[scalars] + [whole] * 11,
        out_specs=[whole] * 9,
        compiler_params=params,
        cost_estimate=cost(5),
        name="moments",
    )(spot, *late, *early, vectors, *square, *pixel)


def apply_kernel(sums, square_p, square_u, pixel_p, pixel_u, *refs):
    states, outs = refs[:6], refs[6:]
    square_new, square_copy, pixel_new, pixel_copy, norms, *news = outs
    part = sums.shape[1] // 2
    squares = sums[7:8, pl.ds(part, 128)]
    weight_norm, update_norm = jnp.sqrt(squares[:, 0:6]), jnp.sqrt(squares[:, 6:12])
    trust = weight_norm / (update_norm + epsilon)
    for row, value in enumerate((weight_norm, update_norm, trust)):
        norms[row : row + 1, :] = value
    for m in range(6):
        k, weight, update, new, copy = (
            (m, square_p, square_u, square_new, square_copy)
            if m < 4
            else (m - 4, pixel_p, pixel_u, pixel_new, pixel_copy)
        )
        value = weight[k] - learn_rate * trust[:, m : m + 1] * update[k]
        new[k] = value
        copy[k] = value.astype(half)
    feats = states[3].shape[1]
    for grad, (value, first, second), out in (
        (sums[0:6, :], states[:3], news[:3]),
        (sums[6:8, 0:feats], states[3:], news[3:]),
    ):
        first_new, second_new, ratio = adam_moments(grad, first[...], second[...])
        out[0][...] = value[...] - vector_rate * ratio
        out[1][...] = first_new
        out[2][...] = second_new


def apply(sums, square_p, square_u, pixel_p, pixel_u, vectors, norms):
    outs = [(square_p, single), (square_p, half), (pixel_p, single), (pixel_p, half)]
    states = [*vectors, *norms]
    return pl.pallas_call(
        apply_kernel,
        out_shape=[shape(a.shape, dtype) for a, dtype in outs]
        + [shape((3, 6), single)]
        + [shape(a.shape, single) for a in states],
        in_specs=[whole] * 11,
        out_specs=[whole] * 11,
        compiler_params=params,
        cost_estimate=cost(4),
        name="apply",
    )(sums, square_p, square_u, pixel_p, pixel_u, *states)


def local(
    latents,
    pixels,
    keep_mask,
    cotangent,
    square_weights,
    square_first,
    square_second,
    pixel_weights,
    pixel_first,
    pixel_second,
    latent_vectors,
    latent_first,
    latent_second,
    pixel_norm,
    pixel_norm_first,
    pixel_norm_second,
):
    width = latents.shape[2]
    feats = pixels.shape[2]
    scale = width ** (-0.5)
    rank = lax.axis_index("seq")
    groups = lax.axis_size("dp")
    spot = jnp.stack([lax.axis_index("dp"), rank]).astype(jnp.int32)

    def turned(array):
        return jnp.transpose(array, (0, 2, 1))

    square = [turned(array) for array in (square_weights, square_first, square_second)]
    pixel = [turned(array) for array in (pixel_weights, pixel_first, pixel_second)]

    latents_two = (latents[0], trade(latents[0]))
    cotangent_two = (cotangent[0], trade(cotangent[0]))
    pixels_t = jnp.transpose(pixels, (2, 0, 1))
    gain, shift = pixel_norm[0][:, None], pixel_norm[1][:, None]
    pixel_normed, pixel_stats = norm_pixels(pixels_t, gain, shift)
    normed = norm_latents(latents[0], latent_vectors)
    normed = (normed, trade(normed))
    blocks = gather_matrices(pack(spot, square[0], pixel[0]), pixel_normed, normed[0])
    query, query_pix, sent = attend(spot, blocks, normed, pixel_normed, keep_mask, scale, feats)
    (latents_out, middle_grad, grad_pix, stats, chain_sums), early_terms = chain(
        spot, blocks, sent, trade(sent), latents_two, cotangent_two, latent_vectors, feats, groups
    )
    pixel_args = (query_pix, grad_pix, stats, pixel_normed, keep_mask, pixels_t, gain, pixel_stats, scale)
    turn_one = pixel_back(*pixel_args, 0, 2, ())
    if len(early_terms) > 1:
        *early_got, score_pix = tie([*send_first(early_terms), turn_one[0]], turn_one[1])
        turn_two = pixel_back(*pixel_args, 1, 2, [score_pix, *turn_one[1:]])
        early_got = send_second(early_terms, early_got, turn_two[0])
    else:
        turn_two, early_got = pixel_back(*pixel_args, 1, 2, turn_one), None
    score_pix, pixel_sums, pixels_grad = turn_two
    (latents_grad, query_sums), late_terms = query_back(
        spot, blocks, score_pix, trade(score_pix), query, normed, latents[0], middle_grad, latent_vectors, groups
    )
    early_got = send_third(early_terms, early_got)
    if len(late_terms) > 1:
        tied = tie([*late_terms[:3], *early_got], late_terms[3])
        late_terms, early_got = [*tied[:3], *late_terms[3:]], tied[3:]
    early = sum_own(early_terms, early_got)
    late = sum_own(late_terms, send_third(late_terms, send_second(late_terms, send_first(late_terms))))

    norm_terms = jnp.pad(jnp.transpose(pixel_sums[:, :2]), ((6, 0), (0, width - feats)))
    vector_terms = chain_sums + query_sums + norm_terms
    vector_terms = vector_terms + trade(vector_terms)
    square_grad, square_first_new, square_second_new, square_u, *rest_outs = moments(
        spot, (late, trade(late)), (early, trade(early)), vector_terms, square, pixel
    )
    pixel_weight_grad, pixel_first_new, pixel_second_new, pixel_u, sums = rest_outs
    square_new, square_copy, pixel_new, pixel_copy, matrix_norms, *news = apply(
        sum_all(sums),
        square[0],
        square_u,
        pixel[0],
        pixel_u,
        (latent_vectors, latent_first, latent_second),
        (pixel_norm, pixel_norm_first, pixel_norm_second),
    )
    latent_vectors_new, latent_first_new, latent_second_new = news[:3]
    pixel_norm_new, pixel_norm_first_new, pixel_norm_second_new = news[3:]
    return (
        latents_out[None],
        latents_grad[None],
        jnp.transpose(pixels_grad, (1, 2, 0)),
        turned(square_grad),
        turned(square_first_new),
        turned(square_second_new),
        turned(square_new),
        turned(square_copy),
        turned(pixel_weight_grad),
        turned(pixel_first_new),
        turned(pixel_second_new),
        turned(pixel_new),
        turned(pixel_copy),
        latent_first_new,
        latent_second_new,
        latent_vectors_new,
        pixel_norm_first_new,
        pixel_norm_second_new,
        pixel_norm_new,
        matrix_norms,
    )


def solution(mesh):
    return jax.shard_map(
        local,
        mesh=mesh,
        in_specs=(
            P("dp", "seq", None),
            P("dp", "seq", None),
            P("dp", "seq"),
            P("dp", "seq", None),
            P(None, None, "dp"),
            P(None, None, "dp"),
            P(None, None, "dp"),
            P(None, None, "dp"),
            P(None, None, "dp"),
            P(None, None, "dp"),
            P(),
            P(),
            P(),
            P(),
            P(),
            P(),
        ),
        out_specs=(
            P("dp", "seq", None),
            P("dp", "seq", None),
            P("dp", "seq", None),
            P(None, None, "dp"),
            P(None, None, "dp"),
            P(None, None, "dp"),
            P(None, None, "dp"),
            P(None, None, "dp"),
            P(None, None, "dp"),
            P(None, None, "dp"),
            P(None, None, "dp"),
            P(None, None, "dp"),
            P(None, None, "dp"),
            P(),
            P(),
            P(),
            P(),
            P(),
            P(),
            P(),
        ),
        check_vma=False,
    )
```

```python
import functools

import jax
import jax.numpy as jnp
from jax import lax
from jax.experimental import pallas as pl
from jax.experimental.pallas import tpu as pltpu
from jax.sharding import PartitionSpec as P

STEP = 10


norm_epsilon = 1e-05
beta_one = 0.9
beta_two = 0.999
decay_rate = 0.01
epsilon = 1e-06
learn_rate = 0.25
vector_rate = 1.0
masked_score = -1e30
gelu_coeff = 0.7978845608028654


def adam_moments(grad, first, second):
    first_new = beta_one * first + (1.0 - beta_one) * grad
    second_new = beta_two * second + (1.0 - beta_two) * grad * grad
    ratio = (
        first_new
        / (1.0 - beta_one**STEP)
        / (jnp.sqrt(second_new / (1.0 - beta_two**STEP)) + epsilon)
    )
    return (first_new, second_new, ratio)

half = jnp.bfloat16
single = jnp.float32
swap = [(0, 1), (1, 0)]
main, rest = 256, 128
whole = pl.BlockSpec(memory_space=pltpu.VMEM)
remote = pl.BlockSpec(memory_space=pl.ANY)
scalars = pl.BlockSpec(memory_space=pltpu.SMEM)
params = pltpu.CompilerParams(vmem_limit_bytes=40 * 2**20)
params_most = pltpu.CompilerParams(vmem_limit_bytes=52 * 2**20)
params_all = pltpu.CompilerParams(vmem_limit_bytes=63 * 2**20)


def cost(micros):
    return pl.CostEstimate(flops=int(micros * 1.1e9), bytes_accessed=1024, transcendentals=0)


def shape(dims, dtype):
    return jax.ShapeDtypeStruct(dims, dtype)


def contract(left, right, over_left, over_right):
    return lax.dot_general(left, right, (((over_left,), (over_right,)), ((), ())), preferred_element_type=single)


def nn(left, right):
    return contract(left, right, 1, 0)


def nt(left, right):
    return contract(left, right, 1, 1)


def tn(left, right):
    return contract(left, right, 0, 0)


def flip(array, mask):
    return lax.ppermute(array, "dp", [(i, i ^ mask) for i in range(lax.axis_size("dp"))])


def trade(array):
    return lax.ppermute(array, "seq", swap)


def special(groups, shard):
    return groups == 16 and shard % 32 == 0


def tie_kernel(*refs):
    pass


def tie(arrays, *after):
    return pl.pallas_call(
        tie_kernel,
        out_shape=[shape(a.shape, a.dtype) for a in arrays],
        in_specs=[remote] * (len(arrays) + len(after)),
        out_specs=[remote] * len(arrays),
        input_output_aliases={i: i for i in range(len(arrays))},
        cost_estimate=cost(0.1),
        name="tie",
    )(*arrays, *after)


def stack_kernel(plan, *refs):
    outs = refs[len(refs) - len(plan) :]
    for out, parts in zip(outs, plan):
        rows = out.shape[0] // len(parts)
        for i, (source, part) in enumerate(parts):
            out[pl.ds(i * rows, rows), :] = refs[source][pl.ds(part * rows, rows), :]


def stack(arrays, rows, plan, *after):
    lanes, dtype = arrays[0].shape[1], arrays[0].dtype
    return pl.pallas_call(
        functools.partial(stack_kernel, plan),
        out_shape=[shape((rows * len(parts), lanes), dtype) for parts in plan],
        in_specs=[whole] * len(arrays) + [remote] * len(after),
        out_specs=[whole] * len(plan),
        compiler_params=params,
        cost_estimate=cost(1.5),
        name="stack",
    )(*arrays, *after)


def gather_blocks(block, early, late):
    rows = block.shape[0]
    one, two, four, three, eight = [flip(block, o) for o in (1, 2, 4, 3, 8)]
    across, both = stack([three, four, eight], rows, (((0, 0), (2, 0)), ((1, 0), (2, 0))), early)
    (gathered,) = stack([block, eight, four, three, two, one], rows, (tuple((i, 0) for i in range(6)),))
    second = [flip(across, 4), flip(both, 2), flip(both, 1)]
    seven, twelve, twelve_ten = stack(second[:2], rows, (((0, 0),), ((0, 1),), ((0, 1), (1, 1))), second[2], late)
    third = [flip(seven, 8), flip(twelve, 2), flip(twelve_ten, 1)]
    return [
        ((0, 8, 4, 3, 2, 1), gathered),
        ((7, 12), second[0]),
        ((6, 10), second[1]),
        ((5, 9), second[2]),
        ((15,), third[0]),
        ((14,), third[1]),
        ((13, 11), third[2]),
    ]


def pack_kernel(feats, spot, squares, pixels, block):
    side = spot[1]
    part = squares.shape[2] // 2
    lanes = pl.ds(pl.multiple_of(side * part, part), part)
    over = feats - main

    def pixel(m):
        last = pixels[m, :, pl.ds(main, over)]
        last = jnp.concatenate([last, jnp.zeros((last.shape[0], main - over), single)], axis=1)
        return jnp.where(side == 0, pixels[m, :, pl.ds(0, main)], last).astype(half)

    block[:, pl.ds(0, part)] = squares[0, :, lanes].astype(half)
    block[:, pl.ds(part, main)] = pixel(0)
    block[:, pl.ds(part + main, main)] = pixel(1)
    for m in range(1, 4):
        block[:, pl.ds(m * part + 2 * main, part)] = squares[m, :, lanes].astype(half)


def pack(spot, squares, pixels):
    _, shard, width = squares.shape
    return pl.pallas_call(
        functools.partial(pack_kernel, pixels.shape[2]),
        out_shape=shape((shard, 4 * (width // 2) + 2 * main), half),
        in_specs=[scalars, whole, whole],
        out_specs=whole,
        compiler_params=params,
        cost_estimate=cost(2),
        name="pack",
    )(spot, squares, pixels)


def gather_matrices(block, early, late):
    groups = lax.axis_size("dp")
    shard = block.shape[0]
    if special(groups, shard):
        arrays, layout = [], []
        for positions, array in gather_blocks(block, early, late):
            arrays += [array, trade(array)]
            layout += [(positions, 0), (positions, 1)]
        return arrays, tuple(layout)
    every = lax.all_gather(block, ("dp", "seq"), axis=0).reshape(groups, 2, shard, -1)
    return [every.transpose(1, 0, 2, 3).reshape(2, groups * shard, -1)], ()


def place_blocks(spot, blocks, layout, target, first):
    lanes = pl.ds(first, target.shape[2])
    if not layout:
        target[...] = blocks[0][:, :, lanes]
    for block, (positions, turn) in zip(blocks, layout):
        rows = block.shape[0] // len(positions)
        side = lax.bitwise_xor(spot[1], turn)
        for i, o in enumerate(positions):
            chip = lax.bitwise_xor(spot[0], o)
            place = pl.ds(pl.multiple_of(chip * rows, rows), rows)
            target[side, place, :] = block[pl.ds(i * rows, rows), lanes]


def copy_all(pairs, sems, first=0):
    copies = [pltpu.make_async_copy(source, target, sems.at[first + i]) for i, (source, target) in enumerate(pairs)]
    for copy in copies:
        copy.start()
    return copies


def wait_all(copies):
    for copy in copies:
        copy.wait()


def load_blocks(spot, blocks, layout, target, first, sems, base=0):
    pairs = []
    lanes = pl.ds(first, target.shape[2])
    if not layout:
        pairs.append((blocks[0].at[:, :, lanes], target))
    for block, (positions, turn) in zip(blocks, layout):
        rows = block.shape[0] // len(positions)
        side = lax.bitwise_xor(spot[1], turn)
        for i, o in enumerate(positions):
            chip = lax.bitwise_xor(spot[0], o)
            place = target.at[side, pl.ds(pl.multiple_of(chip * rows, rows), rows)]
            pairs.append((block.at[pl.ds(i * rows, rows), lanes], place))
    return copy_all(pairs, sems, base)


written = ((13, 11), (14,), (15,), (5, 9), (6, 10), (7, 12), (1,), (2,), (3,), (4,), (8,), (0,))


def store_terms(spot, terms, outs, start, count, sems, base):
    lanes = pl.ds(start, count)
    if len(outs) == 1:
        return copy_all([(terms.at[:, lanes], outs[0].at[:, lanes])], sems, base)
    pairs = []
    rows = terms.shape[0] // 16
    for positions, out in zip(written, outs):
        for i, o in enumerate(positions):
            chip = lax.bitwise_xor(spot[0], o)
            source = terms.at[pl.ds(pl.multiple_of(chip * rows, rows), rows), lanes]
            pairs.append((source, out.at[pl.ds(i * rows, rows), lanes]))
    return copy_all(pairs, sems, base)


def term_shapes(groups, shard, lanes):
    if special(groups, shard):
        return [shape((len(positions) * shard, lanes), half) for positions in written]
    return [shape((groups * shard, lanes), half)]


def send_first(terms, *after):
    if len(terms) == 1:
        return None
    got = [flip(terms[0], 1), flip(terms[1], 2), flip(terms[2], 8)]
    return tie(got, *after) if after else got


def send_second(terms, got, *after):
    if len(terms) == 1:
        return None
    rows = terms[-1].shape[0]

    def added(array, low, *high):
        total = array.astype(single)
        if low is not None:
            total = total + jnp.pad(low.astype(single), ((0, rows), (0, 0)))
        for other in high:
            total = total + jnp.pad(other.astype(single), ((rows, 0), (0, 0)))
        return total.astype(half)

    twelve, ten = got[0][:rows], got[0][rows:]
    got = [
        flip(terms[3], 1),
        flip(added(terms[4], None, ten), 2),
        flip(added(terms[5], got[2], twelve, got[1]), 4),
    ]
    return tie(got, *after) if after else got


def send_third(terms, got):
    if len(terms) == 1:
        return [lax.psum_scatter(terms[0], "dp", scatter_dimension=0, tiled=True)]
    rows = terms[-1].shape[0]
    one, two = terms[6:8]
    three, four, eight = [term.astype(single) for term in terms[8:11]]
    upper = [array[:rows].astype(single) for array in got]
    lower = [array[rows:].astype(single) for array in got]
    sent = [
        (one, 1),
        (two, 2),
        (four + upper[0] + upper[1], 4),
        (three + upper[2], 3),
        (eight + lower[0] + lower[1] + lower[2], 8),
    ]
    return [flip(array.astype(half), mask) for array, mask in sent]


def sum_own(terms, got):
    if len(terms) > 1:
        got = [terms[-1], *got]
    total = got[0].astype(single)
    for array in got[1:]:
        total = total + array.astype(single)
    return total


def sum_all(array):
    mask = 1
    size = lax.axis_size("dp")
    while mask < size:
        if mask * 2 < size:
            one, two, three = flip(array, mask), flip(array, 2 * mask), flip(array, 3 * mask)
            array = (array + one) + (two + three)
            mask *= 4
        else:
            array = array + flip(array, mask)
            mask *= 2
    return array


def standard(values):
    center = values - jnp.mean(values, axis=-1, keepdims=True)
    inverse = lax.rsqrt(jnp.mean(center * center, axis=-1, keepdims=True) + norm_epsilon)
    return center * inverse, inverse


def standard_back(grad, gain, unit, inverse):
    scaled = grad * gain
    return inverse * (
        scaled - jnp.mean(scaled, axis=-1, keepdims=True) - unit * jnp.mean(scaled * unit, axis=-1, keepdims=True)
    )


def pixel_kernel(pixels, gain, shift, normed, stats, held, tail, sem):
    copy = pltpu.make_async_copy(pixels.at[:, 0, :], held, sem)
    copy.start()
    feats = held.shape[0]
    step = 256
    over = feats - main
    tail[...] = jnp.zeros_like(tail)
    copy.wait()

    @pl.loop(0, held.shape[1] // step)
    def _(i):
        lanes = pl.ds(pl.multiple_of(i * step, step), step)
        first, last = held[pl.ds(0, main), lanes], held[pl.ds(main, over), lanes]
        mean = (jnp.sum(first, axis=0, keepdims=True) + jnp.sum(last, axis=0, keepdims=True)) / feats
        first, last = first - mean, last - mean
        spread = (
            jnp.sum(first * first, axis=0, keepdims=True) + jnp.sum(last * last, axis=0, keepdims=True)
        ) / feats
        inverse = lax.rsqrt(spread + norm_epsilon)
        normed[pl.ds(0, main), lanes] = (first * inverse * gain[pl.ds(0, main)] + shift[pl.ds(0, main)]).astype(half)
        tail[pl.ds(0, over), :] = last * inverse * gain[pl.ds(main, over)] + shift[pl.ds(main, over)]
        normed[pl.ds(main, rest), lanes] = tail[...].astype(half)
        stats[0:1, lanes] = mean
        stats[1:2, lanes] = inverse


def norm_pixels(pixels, gain, shift):
    feats, _, count = pixels.shape
    return pl.pallas_call(
        pixel_kernel,
        out_shape=[shape((main + rest, count), half), shape((2, count), single)],
        in_specs=[remote, whole, whole],
        out_specs=[whole] * 2,
        scratch_shapes=[pltpu.VMEM((feats, count), single), pltpu.VMEM((rest, 256), single), pltpu.SemaphoreType.DMA],
        compiler_params=params,
        cost_estimate=cost(7),
        name="norm_pixels",
    )(pixels, gain, shift)


def latent_kernel(latents, vectors, normed):
    unit, _ = standard(latents[...])
    normed[...] = (unit * vectors[0:1, :] + vectors[1:2, :]).astype(half)


def norm_latents(latents, vectors):
    return pl.pallas_call(
        latent_kernel,
        out_shape=shape(latents.shape, half),
        in_specs=[whole] * 2,
        out_specs=whole,
        compiler_params=params,
        cost_estimate=cost(2),
        name="norm_latents",
    )(latents, vectors)


def attend_kernel(count, layout, scale, feats, spot, *refs):
    blocks = refs[:count]
    mine, theirs, pixels_in, keep, query_out, query_pix, sent, *refs = refs[count:]
    weights, normed, pixels, query, scores, peak, more = refs
    copies = copy_all([(mine, normed.at[0]), (theirs, normed.at[1])], more)
    late = copy_all([(pixels_in, pixels)], more, 2)
    place_blocks(spot, blocks, layout, weights, 0)
    wait_all(copies)
    step, part = mine.shape[0], mine.shape[1] // 2
    for t in range(2):
        rows = pl.ds(t * step, step)
        value = nt(normed[t, :, pl.ds(0, part)], weights[0, :, pl.ds(0, part)])
        value = value + nt(normed[t, :, pl.ds(part, part)], weights[1, :, pl.ds(0, part)])
        value = value.astype(half)
        query[rows, :] = value
        query_pix[rows, pl.ds(0, main)] = (nn(value, weights[0, :, pl.ds(part, main)]) * scale).astype(half)
        query_pix[rows, pl.ds(main, rest)] = (nn(value, weights[1, :, pl.ds(part, rest)]) * scale).astype(half)
    wait_all(late)
    late = copy_all([(query, query_out)], more, 2)
    step = 1024
    peak[...] = jnp.full(peak.shape, -jnp.inf, single)

    @pl.loop(0, pixels.shape[1] // step)
    def _(j):
        lanes = pl.ds(pl.multiple_of(j * step, step), step)
        value = nn(query_pix[...], pixels[:, lanes])
        value = jnp.where(keep[:, lanes] > 0, value, masked_score)
        scores[:, lanes] = value
        some = [value[:, 128 * k : 128 * k + 128] for k in range(step // 128)]
        peak[...] = functools.reduce(jnp.maximum, some, peak[...])

    top = jnp.max(peak[...], axis=-1, keepdims=True)
    peak[...] = jnp.zeros_like(peak)
    sent[...] = jnp.zeros_like(sent)

    @pl.loop(0, pixels.shape[1] // step)
    def _(j):
        lanes = pl.ds(pl.multiple_of(j * step, step), step)
        value = jnp.exp(scores[:, lanes] - top)
        peak[...] += sum(value[:, 128 * k : 128 * k + 128] for k in range(step // 128))
        sent[...] += nt(value.astype(half), pixels[:, lanes])

    total, mix = peak[...], sent[...]
    total = jnp.sum(total, axis=-1, keepdims=True)
    lane = lax.broadcasted_iota(jnp.int32, mix.shape, 1)
    sent[...] = jnp.where(lane == feats, top, jnp.where(lane == feats + 1, total, mix))
    wait_all(late)


def attend(spot, gathered, normed, pixels, keep, scale, feats):
    blocks, layout = gathered
    rows, width = 2 * normed[0].shape[0], normed[0].shape[1]
    lanes = width // 2 + main
    return pl.pallas_call(
        functools.partial(attend_kernel, len(blocks), layout, scale, feats),
        out_shape=[shape((rows, width), half), shape((rows, main + rest), half), shape((rows, main + rest), single)],
        in_specs=[scalars] + [whole] * len(blocks) + [remote] * 3 + [whole],
        out_specs=[remote, whole, whole],
        scratch_shapes=[
            pltpu.VMEM((2, width, lanes), half),
            pltpu.VMEM((2, rows // 2, width), half),
            pltpu.VMEM(pixels.shape, half),
            pltpu.VMEM((rows, width), half),
            pltpu.VMEM((rows, pixels.shape[1]), single),
            pltpu.VMEM((rows, 128), single),
            pltpu.SemaphoreType.DMA((3,)),
        ],
        compiler_params=params,
        cost_estimate=cost(11),
        name="attend",
    )(spot, *blocks, *normed, pixels, keep)


def chain_kernel(count, layout, terms_count, feats, spot, *refs):
    blocks, refs = refs[:count], refs[count:]
    mine, theirs, latent_mine, latent_theirs, cot_mine, cot_theirs, vectors, *refs = refs
    latents_out, middle_grad, grad_pix, stats, sums, *refs = refs
    term_outs, refs = refs[:terms_count], refs[terms_count:]
    near, far, latents_in, cot_in, mixes, *refs = refs
    attended, middle_half, mixed, hidden_grad, active, out_half, attended_grad, value_mix, *refs = refs
    wide, out_wide, grad_wide, scratch, terms, sems, store_sems, more = refs
    rows_all, width = attended.shape
    step = rows_all // 2
    part = width // 2
    ready = copy_all([(mine, mixes.at[0]), (theirs, mixes.at[1])], more)
    ready += load_blocks(spot, blocks, layout, near, part + main, sems)
    ready_latents = copy_all([(latent_mine, latents_in.at[0]), (latent_theirs, latents_in.at[1])], more, 2)
    matrices = ((near, main), (far, 0), (far, part))
    leaving = []
    pair = range(2)
    rows = [pl.ds(t * step, step) for t in pair]

    def into(value, m):
        source, start = matrices[m]
        lanes = pl.ds(start, part)
        return nt(value[:, :part], source[0, :, lanes]) + nt(value[:, part:], source[1, :, lanes])

    def back(value, m, target):
        source, start = matrices[m]
        lanes = pl.ds(start, part)
        target[:, pl.ds(0, part)] = nn(value, source[0, :, lanes])
        target[:, pl.ds(part, part)] = nn(value, source[1, :, lanes])

    side = pl.ds(pl.multiple_of(spot[1] * part, part), part)

    def term(m, grad, value):
        terms[:, pl.ds(m * part, part)] = tn(grad[...], value[:, side]).astype(half)
        return store_terms(spot, terms, term_outs, m * part, part, store_sems, 16 * m)

    sums[...] = jnp.zeros_like(sums)
    value_mix[...] = jnp.zeros_like(value_mix)
    wait_all(ready)
    ready_far = load_blocks(spot, blocks, layout, far, 2 * part + 2 * main, sems, 32)
    ready_far += copy_all([(cot_mine, cot_in.at[0]), (cot_theirs, cot_in.at[1])], more, 4)
    tops, totals, attended_f, middles, units, inverses, hiddens, curves = [[None, None] for _ in range(8)]
    for t in pair:
        here, there = mixes[0, rows[t], :], mixes[1, rows[1 - t], :]
        top_here, top_there = here[:, feats : feats + 1], there[:, feats : feats + 1]
        top = jnp.maximum(top_here, top_there)
        scale_here, scale_there = jnp.exp(top_here - top), jnp.exp(top_there - top)
        total = here[:, feats + 1 : feats + 2] * scale_here + there[:, feats + 1 : feats + 2] * scale_there
        mix = (here * scale_here + there * scale_there) / total
        lane = lax.broadcasted_iota(jnp.int32, mix.shape, 1)
        value_mix[rows[t], pl.ds(0, main + rest)] = jnp.where(lane < feats, mix, 0.0).astype(half)
        tops[t], totals[t] = top, total
    for t in pair:
        value = nt(value_mix[rows[t], pl.ds(0, main)], near[0, :, pl.ds(0, main)])
        value = value + nt(value_mix[rows[t], pl.ds(main, rest)], near[1, :, pl.ds(0, rest)])
        wide[t] = value
        attended[rows[t], :] = value.astype(half)
    wait_all(ready_latents)
    for t in pair:
        middles[t] = latents_in[t] + into(attended[rows[t], :], 0)
    for t in pair:
        units[t], inverses[t] = standard(middles[t])
        mixed[rows[t], :] = (units[t] * vectors[2:3, :] + vectors[3:4, :]).astype(half)
    wait_all(ready_far)
    for t in pair:
        value = cot_in[t].astype(half)
        out_half[rows[t], :] = value
        if t == 0:
            sums[5:6, :] = jnp.sum(value.astype(single), axis=0, keepdims=True)
    for t in pair:
        hiddens[t] = into(mixed[rows[t], :], 1) + vectors[4:5, :]
    for t in pair:
        back(out_half[rows[t], :], 2, scratch.at[t])
        hidden = hiddens[t]
        curve = jnp.tanh(gelu_coeff * (hidden + 0.044715 * hidden * hidden * hidden))
        active[rows[t], :] = (0.5 * hidden * (1.0 + curve)).astype(half)
        curves[t] = curve
    leaving += term(2, out_half, active)
    out_wide[...] = middles[0] + into(active[rows[0], :], 2) + vectors[5:6, :]
    leaving += copy_all([(out_wide, latents_out)], more)
    for t in pair:
        hidden, curve = hiddens[t], curves[t]
        slope = 0.5 * (1.0 + curve) + 0.5 * hidden * (1.0 - curve * curve) * gelu_coeff * (
            1.0 + 3.0 * 0.044715 * hidden * hidden
        )
        value = (scratch[t] * slope).astype(half)
        hidden_grad[rows[t], :] = value
        if t == 0:
            sums[4:5, :] = jnp.sum(value.astype(single), axis=0, keepdims=True)
    for t in pair:
        back(hidden_grad[rows[t], :], 1, scratch.at[t])
    leaving += term(1, hidden_grad, mixed)
    for t in pair:
        mixed_grad = scratch[t]
        if t == 0:
            sums[2:3, :] = jnp.sum(mixed_grad * units[t], axis=0, keepdims=True)
            sums[3:4, :] = jnp.sum(mixed_grad, axis=0, keepdims=True)
        grad = cot_in[t] + standard_back(mixed_grad, vectors[2:3, :], units[t], inverses[t])
        if t == 0:
            grad_wide[...] = grad
            leaving += copy_all([(grad_wide, middle_grad)], more, 1)
        middle_half[rows[t], :] = grad.astype(half)
    for t in pair:
        back(middle_half[rows[t], :], 0, scratch.at[t])
    leaving += term(0, middle_half, attended)
    for t in pair:
        value = scratch[t].astype(half)
        attended_grad[rows[t], :] = value
        inner = jnp.sum(wide[t] * value.astype(single), axis=-1, keepdims=True)
        lane = lax.broadcasted_iota(jnp.int32, (step, 128), 1)
        stats[rows[t], :] = jnp.where(lane == 0, tops[t] + jnp.log(totals[t]), inner)
    for t in pair:
        value = attended_grad[rows[t], :]
        grad_pix[rows[t], pl.ds(0, main)] = nn(value, near[0, :, pl.ds(0, main)]).astype(half)
        grad_pix[rows[t], pl.ds(main, rest)] = nn(value, near[1, :, pl.ds(0, rest)]).astype(half)
    side = pl.ds(pl.multiple_of(spot[1] * main, main), main)
    terms[:, pl.ds(3 * part, main)] = tn(attended_grad[...], value_mix[:, side]).astype(half)
    leaving += store_terms(spot, terms, term_outs, 3 * part, main, store_sems, 48)
    wait_all(leaving)


def chain(spot, gathered, mine, theirs, latents, cotangents, vectors, feats, groups):
    blocks, layout = gathered
    rows, width = mine.shape[0], vectors.shape[1]
    part = width // 2
    lanes = 3 * part + main
    outs = term_shapes(groups, width // groups, lanes)
    bits = pltpu.VMEM((rows, width), half)
    result = pl.pallas_call(
        functools.partial(chain_kernel, len(blocks), layout, len(outs), feats),
        out_shape=[
            shape((rows // 2, width), single),
            shape((rows // 2, width), single),
            shape((rows, main + rest), half),
            shape((rows, 128), single),
            shape((8, width), single),
        ]
        + outs,
        in_specs=[scalars] + [remote] * (len(blocks) + 6) + [whole],
        out_specs=[remote] * 2 + [whole] * 3 + [remote] * len(outs),
        scratch_shapes=[
            pltpu.VMEM((2, width, part + main), half),
            pltpu.VMEM((2, width, 2 * part), half),
            pltpu.VMEM((2, rows // 2, width), single),
            pltpu.VMEM((2, rows // 2, width), single),
            pltpu.VMEM((2, rows, main + rest), single),
        ]
        + [bits] * 7
        + [pltpu.VMEM((rows, 2 * main), half)]
        + [pltpu.VMEM((2, rows // 2, width), single)]
        + [pltpu.VMEM((rows // 2, width), single)] * 2
        + [pltpu.VMEM((2, rows // 2, width), single)]
        + [pltpu.VMEM((width, lanes), half)]
        + [pltpu.SemaphoreType.DMA((64,)), pltpu.SemaphoreType.DMA((64,)), pltpu.SemaphoreType.DMA((6,))],
        compiler_params=params,
        cost_estimate=cost(17),
        name="chain",
    )(spot, *blocks, mine, theirs, *latents, *cotangents, vectors)
    return result[:5], result[5:]


def pixel_back_kernel(scale, turn, turns, *refs):
    (query_pix, grad_pix, stats, values_in, keep, pixels, gain, pixel_stats), refs = refs[:8], refs[8:]
    if turn > 0:
        (score_before, sums_before, _), refs = refs[:3], refs[3:]
    score_pix, sums, pixels_grad, values, held, made, score_grads, query_t, grad_t, slope, shift, sems = refs
    feats, count = held.shape
    over = feats - main
    some = main + 16
    step = 512
    origin = turn * count
    here = pl.ds(origin, count)
    early = copy_all([(values_in.at[:, here], values)], sems)
    late = copy_all([(pixels.at[:, 0, here], held)], sems, 1)
    query_t[...] = jnp.transpose(query_pix[...].astype(single))[:some].astype(half)
    grad_t[...] = jnp.transpose(grad_pix[...].astype(single))[:some].astype(half)
    slope[...] = jnp.zeros_like(slope)
    shift[...] = jnp.zeros_like(shift)
    log_total, inner = stats[:, 0:1], stats[:, 1:2]
    wait_all(early)

    def products(start):
        some_values = values[:, pl.ds(pl.multiple_of(start, step), step)]
        return nn(query_pix[...], some_values), nn(grad_pix[...], some_values)

    def norm_back(start, grad):
        lanes = pl.ds(pl.multiple_of(start, step), step)
        there = pl.ds(pl.multiple_of(origin + start, step), step)
        mean, inverse = pixel_stats[0:1, there], pixel_stats[1:2, there]
        unit_a = (held[pl.ds(0, main), lanes] - mean) * inverse
        unit_b = (held[pl.ds(main, over), lanes] - mean) * inverse
        grad_a, grad_b = grad[:main], grad[main : main + over]
        for rows, g, u in ((pl.ds(0, main), grad_a, unit_a), (pl.ds(main, over), grad_b, unit_b)):
            product = g * u
            slope[rows, :] += sum(product[:, 128 * j : 128 * j + 128] for j in range(step // 128))
            shift[rows, :] += sum(g[:, 128 * j : 128 * j + 128] for j in range(step // 128))
        scaled_a, scaled_b = grad_a * gain[pl.ds(0, main)], grad_b * gain[pl.ds(main, over)]
        flat = (jnp.sum(scaled_a, axis=0, keepdims=True) + jnp.sum(scaled_b, axis=0, keepdims=True)) / feats
        along = (
            jnp.sum(scaled_a * unit_a, axis=0, keepdims=True) + jnp.sum(scaled_b * unit_b, axis=0, keepdims=True)
        ) / feats
        made[pl.ds(0, main), lanes] = inverse * (scaled_a - flat - unit_a * along)
        made[pl.ds(main, over), lanes] = inverse * (scaled_b - flat - unit_b * along)

    def leaving(i):
        lanes = pl.ds(pl.multiple_of(2 * i * step, step), 2 * step)
        there = pl.ds(pl.multiple_of(origin + 2 * i * step, step), 2 * step)
        return pltpu.make_async_copy(made.at[:, lanes], pixels_grad.at[:, 0, there], sems.at[2 + i])

    wait_all(late)

    @pl.loop(0, count // (2 * step))
    def _(i):
        starts = [(2 * i + k) * step for k in range(2)]
        now, grads = products(starts[0]), []
        for k, start in enumerate(starts):
            scores, weight_grad = now
            if k == 0:
                now = products(starts[1])
            lanes = pl.ds(pl.multiple_of(start, step), step)
            kept = keep[:, pl.ds(pl.multiple_of(origin + start, step), step)] > 0
            attn = jnp.exp(jnp.where(kept, scores, masked_score) - log_total)
            score_grad = (attn * (weight_grad - inner)).astype(half)
            score_grads[:, lanes] = score_grad
            grads.append(nn(query_t[...], score_grad) + nn(grad_t[...], attn.astype(half)))
        for start, grad in zip(starts, grads):
            norm_back(start, grad)
        leaving(i).start()

    value = nt(score_grads[...], values[...])
    if turn > 0:
        value = value + score_before[...]
    score_pix[...] = value * scale if turn == turns - 1 else value
    sums[...] = sums_before[...] if turn > 0 else jnp.zeros_like(sums)
    for row, array in ((6, slope), (7, shift)):
        sums[row : row + 1, pl.ds(0, main + rest)] += jnp.sum(jnp.transpose(array[...]), axis=0, keepdims=True)

    @pl.loop(0, count // (2 * step))
    def _(i):
        leaving(i).wait()


def pixel_back(query_pix, grad_pix, stats, normed, keep, pixels, gain, pixel_stats, scale, turn, turns, before):
    feats, _, count = pixels.shape
    rows = query_pix.shape[0]
    held = pltpu.VMEM((feats, count // turns), single)
    return pl.pallas_call(
        functools.partial(pixel_back_kernel, scale, turn, turns),
        out_shape=[shape((rows, main + rest), single), shape((8, 2 * rows), single), shape(pixels.shape, single)],
        in_specs=[whole] * 3 + [remote, whole, remote, whole, whole] + [whole, whole, remote][: len(before)],
        out_specs=[whole, whole, remote],
        scratch_shapes=[
            pltpu.VMEM((main + rest, count // turns), half),
            held,
            held,
            pltpu.VMEM((rows, count // turns), half),
            pltpu.VMEM((main + 16, rows), half),
            pltpu.VMEM((main + 16, rows), half),
            pltpu.VMEM((main + rest, 128), single),
            pltpu.VMEM((main + rest, 128), single),
            pltpu.SemaphoreType.DMA((2 + count // turns // 512,)),
        ],
        input_output_aliases={10: 2} if before else {},
        compiler_params=params_most,
        cost_estimate=cost(18 / turns),
        name="pixel_back",
    )(query_pix, grad_pix, stats, normed, keep, pixels, gain, pixel_stats, *before)


def query_back_kernel(count, layout, terms_count, spot, *refs):
    blocks, refs = refs[:count], refs[count:]
    mine, theirs, query_in, normed_mine, normed_theirs, latents_in, grad_in, vectors, *refs = refs
    latents_grad, sums, *refs = refs
    term_outs, refs = refs[:terms_count], refs[terms_count:]
    weights, score_pix, query, normed, latents, middle_grad, query_grad, wide, terms, sems, store_sems, more = refs
    ready = load_blocks(spot, blocks, layout, weights, 0, sems)
    rows_all, width = query.shape
    step = rows_all // 2
    part = width // 2
    score_pix[:, pl.ds(main + rest, rest)] = jnp.zeros((rows_all, rest), half)
    for t in range(2):
        rows, other = pl.ds(t * step, step), pl.ds((1 - t) * step, step)
        score_pix[rows, pl.ds(0, main + rest)] = (mine[rows, :] + theirs[other, :]).astype(half)
    wait_all(ready)
    later = copy_all([(normed_mine, normed.at[0]), (normed_theirs, normed.at[1]), (query_in, query)], more)
    last = copy_all([(latents_in, latents), (grad_in, middle_grad)], more, 3)
    value = nt(score_pix[:, pl.ds(0, main)], weights[0, :, pl.ds(part, main)])
    value = value + nt(score_pix[:, pl.ds(main, rest)], weights[1, :, pl.ds(part, rest)])
    query_grad[...] = value.astype(half)
    wait_all(later)
    side = pl.ds(pl.multiple_of(spot[1] * part, part), part)
    value = tn(query_grad[pl.ds(0, step), :], normed[0, :, side])
    terms[:, pl.ds(0, part)] = (value + tn(query_grad[pl.ds(step, step), :], normed[1, :, side])).astype(half)
    leaving = store_terms(spot, terms, term_outs, 0, part, store_sems, 0)
    side = pl.ds(pl.multiple_of(spot[1] * main, main), main)
    terms[:, pl.ds(part, main)] = tn(query[...], score_pix[:, side]).astype(half)
    leaving += store_terms(spot, terms, term_outs, part, main, store_sems, 16)
    value = query_grad[pl.ds(0, step), :]
    wide[:, pl.ds(0, part)] = nn(value, weights[0, :, pl.ds(0, part)])
    wide[:, pl.ds(part, part)] = nn(value, weights[1, :, pl.ds(0, part)])
    wait_all(last)
    unit, inverse = standard(latents[...])
    grad = wide[...]
    latents_grad[...] = middle_grad[...] + standard_back(grad, vectors[0:1, :], unit, inverse)
    sums[...] = jnp.zeros_like(sums)
    sums[0:1, :] = jnp.sum(grad * unit, axis=0, keepdims=True)
    sums[1:2, :] = jnp.sum(grad, axis=0, keepdims=True)
    wait_all(leaving)


def query_back(spot, gathered, mine, theirs, query, normed, latents, middle_grad, vectors, groups):
    blocks, layout = gathered
    rows, width = query.shape
    lanes = width // 2 + main
    outs = term_shapes(groups, width // groups, lanes)
    one = pltpu.VMEM((rows // 2, width), single)
    result = pl.pallas_call(
        functools.partial(query_back_kernel, len(blocks), layout, len(outs)),
        out_shape=[shape((rows // 2, width), single), shape((8, width), single)] + outs,
        in_specs=[scalars] + [remote] * len(blocks) + [whole] * 2 + [remote] * 5 + [whole],
        out_specs=[whole] * 2 + [remote] * len(outs),
        scratch_shapes=[
            pltpu.VMEM((2, width, lanes), half),
            pltpu.VMEM((rows, 2 * main), half),
            pltpu.VMEM((rows, width), half),
            pltpu.VMEM((2, rows // 2, width), half),
            one,
            one,
            pltpu.VMEM((rows, width), half),
            one,
            pltpu.VMEM((width, lanes), half),
            pltpu.SemaphoreType.DMA((32,)),
            pltpu.SemaphoreType.DMA((32,)),
            pltpu.SemaphoreType.DMA((5,)),
        ],
        compiler_params=params_all,
        cost_estimate=cost(7),
        name="query_back",
    )(spot, *blocks, mine, theirs, query, *normed, latents, middle_grad, vectors)
    return result[:2], result[2:]


def moments_kernel(feats, *refs):
    spot, late_mine, late_theirs, early_mine, early_theirs, vectors, *refs = refs
    square_p, square_m, square_v, pixel_p, pixel_m, pixel_v, *refs = refs
    square_outs, pixel_outs, sums = refs[:4], refs[4:8], refs[8]
    width = square_p.shape[2]
    part = width // 2
    first = spot[1] == 0
    lane = lax.broadcasted_iota(jnp.int32, (1, width), 1)
    row = jnp.zeros((1, width), single)
    for m in range(6):
        mine, theirs = (late_mine, late_theirs) if m in (0, 4) else (early_mine, early_theirs)
        if m < 4:
            lanes = pl.ds(max(m - 1, 0) * part, part)
            sides, outs, k = (pl.ds(0, part), pl.ds(part, part)), square_outs, m
            params_now, first_now, second_now = square_p, square_m, square_v
        else:
            lanes = pl.ds(part if m == 4 else 3 * part, main)
            sides, outs, k = (pl.ds(0, main), pl.ds(main, feats - main)), pixel_outs, m - 4
            params_now, first_now, second_now = pixel_p, pixel_m, pixel_v
        own, other = mine[:, lanes], theirs[:, lanes]
        weight_total, update_total = jnp.zeros((1, 1), single), jnp.zeros((1, 1), single)
        for side, grad in zip(sides, (jnp.where(first, own, other), jnp.where(first, other, own))):
            grad = grad[:, : side.size]
            weight = params_now[k, :, side]
            first_new, second_new, ratio = adam_moments(grad, first_now[k, :, side], second_now[k, :, side])
            update = ratio + decay_rate * weight
            for out, value in zip(outs, (grad, first_new, second_new, update)):
                out[k, :, side] = value
            weight_total = weight_total + jnp.sum(weight * weight, keepdims=True)
            update_total = update_total + jnp.sum(update * update, keepdims=True)
        row = row + jnp.where(lane == part + m, weight_total, jnp.where(lane == part + 6 + m, update_total, 0.0))
    sums[...] = vectors[...]
    sums[7:8, pl.ds(part, part)] = row[:, part:]


def moments(spot, late, early, vectors, square, pixel):
    big, small = shape(square[0].shape, single), shape(pixel[0].shape, single)
    return pl.pallas_call(
        functools.partial(moments_kernel, pixel[0].shape[2]),
        out_shape=[big] * 4 + [small] * 4 + [shape((8, big.shape[2]), single)],
        in_specs=[scalars] + [whole] * 11,
        out_specs=[whole] * 9,
        compiler_params=params,
        cost_estimate=cost(5),
        name="moments",
    )(spot, *late, *early, vectors, *square, *pixel)


def apply_kernel(sums, square_p, square_u, pixel_p, pixel_u, *refs):
    states, outs = refs[:6], refs[6:]
    square_new, square_copy, pixel_new, pixel_copy, norms, *news = outs
    part = sums.shape[1] // 2
    squares = sums[7:8, pl.ds(part, 128)]
    weight_norm, update_norm = jnp.sqrt(squares[:, 0:6]), jnp.sqrt(squares[:, 6:12])
    trust = weight_norm / (update_norm + epsilon)
    for row, value in enumerate((weight_norm, update_norm, trust)):
        norms[row : row + 1, :] = value
    for m in range(6):
        k, weight, update, new, copy = (
            (m, square_p, square_u, square_new, square_copy)
            if m < 4
            else (m - 4, pixel_p, pixel_u, pixel_new, pixel_copy)
        )
        value = weight[k] - learn_rate * trust[:, m : m + 1] * update[k]
        new[k] = value
        copy[k] = value.astype(half)
    feats = states[3].shape[1]
    for grad, (value, first, second), out in (
        (sums[0:6, :], states[:3], news[:3]),
        (sums[6:8, 0:feats], states[3:], news[3:]),
    ):
        first_new, second_new, ratio = adam_moments(grad, first[...], second[...])
        out[0][...] = value[...] - vector_rate * ratio
        out[1][...] = first_new
        out[2][...] = second_new


def apply(sums, square_p, square_u, pixel_p, pixel_u, vectors, norms):
    outs = [(square_p, single), (square_p, half), (pixel_p, single), (pixel_p, half)]
    states = [*vectors, *norms]
    return pl.pallas_call(
        apply_kernel,
        out_shape=[shape(a.shape, dtype) for a, dtype in outs]
        + [shape((3, 6), single)]
        + [shape(a.shape, single) for a in states],
        in_specs=[whole] * 11,
        out_specs=[whole] * 11,
        compiler_params=params,
        cost_estimate=cost(4),
        name="apply",
    )(sums, square_p, square_u, pixel_p, pixel_u, *states)


def local(
    latents,
    pixels,
    keep_mask,
    cotangent,
    square_weights,
    square_first,
    square_second,
    pixel_weights,
    pixel_first,
    pixel_second,
    latent_vectors,
    latent_first,
    latent_second,
    pixel_norm,
    pixel_norm_first,
    pixel_norm_second,
):
    width = latents.shape[2]
    feats = pixels.shape[2]
    scale = width ** (-0.5)
    rank = lax.axis_index("seq")
    groups = lax.axis_size("dp")
    spot = jnp.stack([lax.axis_index("dp"), rank]).astype(jnp.int32)

    def turned(array):
        return jnp.transpose(array, (0, 2, 1))

    square = [turned(array) for array in (square_weights, square_first, square_second)]
    pixel = [turned(array) for array in (pixel_weights, pixel_first, pixel_second)]

    latents_two = (latents[0], trade(latents[0]))
    cotangent_two = (cotangent[0], trade(cotangent[0]))
    pixels_t = jnp.transpose(pixels, (2, 0, 1))
    gain, shift = pixel_norm[0][:, None], pixel_norm[1][:, None]
    pixel_normed, pixel_stats = norm_pixels(pixels_t, gain, shift)
    normed = norm_latents(latents[0], latent_vectors)
    normed = (normed, trade(normed))
    blocks = gather_matrices(pack(spot, square[0], pixel[0]), pixel_normed, normed[0])
    query, query_pix, sent = attend(spot, blocks, normed, pixel_normed, keep_mask, scale, feats)
    (latents_out, middle_grad, grad_pix, stats, chain_sums), early_terms = chain(
        spot, blocks, sent, trade(sent), latents_two, cotangent_two, latent_vectors, feats, groups
    )
    pixel_args = (query_pix, grad_pix, stats, pixel_normed, keep_mask, pixels_t, gain, pixel_stats, scale)
    turn_one = pixel_back(*pixel_args, 0, 2, ())
    if len(early_terms) > 1:
        *early_got, score_pix = tie([*send_first(early_terms), turn_one[0]], turn_one[1])
        turn_two = pixel_back(*pixel_args, 1, 2, [score_pix, *turn_one[1:]])
        early_got = send_second(early_terms, early_got, turn_two[0])
    else:
        turn_two, early_got = pixel_back(*pixel_args, 1, 2, turn_one), None
    score_pix, pixel_sums, pixels_grad = turn_two
    (latents_grad, query_sums), late_terms = query_back(
        spot, blocks, score_pix, trade(score_pix), query, normed, latents[0], middle_grad, latent_vectors, groups
    )
    early_got = send_third(early_terms, early_got)
    if len(late_terms) > 1:
        tied = tie([*late_terms[:3], *early_got], late_terms[3])
        late_terms, early_got = [*tied[:3], *late_terms[3:]], tied[3:]
    early = sum_own(early_terms, early_got)
    late = sum_own(late_terms, send_third(late_terms, send_second(late_terms, send_first(late_terms))))

    vector_terms = chain_sums + query_sums + pixel_sums
    vector_terms = vector_terms + trade(vector_terms)
    square_grad, square_first_new, square_second_new, square_u, *rest_outs = moments(
        spot, (late, trade(late)), (early, trade(early)), vector_terms, square, pixel
    )
    pixel_weight_grad, pixel_first_new, pixel_second_new, pixel_u, sums = rest_outs
    square_new, square_copy, pixel_new, pixel_copy, matrix_norms, *news = apply(
        sum_all(sums),
        square[0],
        square_u,
        pixel[0],
        pixel_u,
        (latent_vectors, latent_first, latent_second),
        (pixel_norm, pixel_norm_first, pixel_norm_second),
    )
    latent_vectors_new, latent_first_new, latent_second_new = news[:3]
    pixel_norm_new, pixel_norm_first_new, pixel_norm_second_new = news[3:]
    return (
        latents_out[None],
        latents_grad[None],
        jnp.transpose(pixels_grad, (1, 2, 0)),
        turned(square_grad),
        turned(square_first_new),
        turned(square_second_new),
        turned(square_new),
        turned(square_copy),
        turned(pixel_weight_grad),
        turned(pixel_first_new),
        turned(pixel_second_new),
        turned(pixel_new),
        turned(pixel_copy),
        latent_first_new,
        latent_second_new,
        latent_vectors_new,
        pixel_norm_first_new,
        pixel_norm_second_new,
        pixel_norm_new,
        matrix_norms,
    )


def solution(mesh):
    return jax.shard_map(
        local,
        mesh=mesh,
        in_specs=(
            P("dp", "seq", None),
            P("dp", "seq", None),
            P("dp", "seq"),
            P("dp", "seq", None),
            P(None, None, "dp"),
            P(None, None, "dp"),
            P(None, None, "dp"),
            P(None, None, "dp"),
            P(None, None, "dp"),
            P(None, None, "dp"),
            P(),
            P(),
            P(),
            P(),
            P(),
            P(),
        ),
        out_specs=(
            P("dp", "seq", None),
            P("dp", "seq", None),
            P("dp", "seq", None),
            P(None, None, "dp"),
            P(None, None, "dp"),
            P(None, None, "dp"),
            P(None, None, "dp"),
            P(None, None, "dp"),
            P(None, None, "dp"),
            P(None, None, "dp"),
            P(None, None, "dp"),
            P(None, None, "dp"),
            P(None, None, "dp"),
            P(),
            P(),
            P(),
            P(),
            P(),
            P(),
            P(),
        ),
        check_vma=False,
    )
```
